32 devices in a mesh: dp: 8 (over z, y), mp: 4 (over x, core).
Axes of the slice: x: 2, y: 2, z: 4, core: 2. Of those that a mesh axis runs over, the one named last changes fastest.
Arguments:
- images: bfloat16 [64, 196, 256], P('dp'), may hold values from -6 to 6
- labels: int32 [64, 196, 256], P('dp'), may hold values from 0 to 8
- background: int32 [64], P('dp'), may hold values 0 or 1
- patients: int32 [64], P('dp'), may hold values from 0 to 15
- stem_w: float32 [256, 1024], P('dp'), may hold values from -0.375 to 0.375
- embed_w: float32 [1024, 768], P('dp'), may hold values from -0.1875 to 0.1875
- token_params: float32 [202, 768], P(None, 'dp')
- qkv_w: float32 [768, 2304], P('dp', 'mp'), may hold values from -0.21875 to 0.21875
- out_w: float32 [768, 768], P('mp', 'dp'), may hold values from -0.625 to 0.625
- mlp_in_w: float32 [768, 3072], P('dp', 'mp'), may hold values from -0.21875 to 0.21875
- mlp_out_w: float32 [3072, 768], P('mp', 'dp'), may hold values from -0.109375 to 0.109375
- skip_w: float32 [1024, 2560], P('dp'), may hold values from -0.1875 to 0.1875
- decoder_w: float32 [365120], P('dp')
- stem_m: float32 [256, 1024], P('dp'), may hold values from -4.172325e-07 to 4.172325e-07
- embed_m: float32 [1024, 768], P('dp'), may hold values from -4.172325e-07 to 4.172325e-07
- token_m: float32 [202, 768], P(None, 'dp'), may hold values from -4.172325e-07 to 4.172325e-07
- qkv_m: float32 [768, 2304], P('dp', 'mp'), may hold values from -4.172325e-07 to 4.172325e-07
- out_m: float32 [768, 768], P('mp', 'dp'), may hold values from -4.172325e-07 to 4.172325e-07
- mlp_in_m: float32 [768, 3072], P('dp', 'mp'), may hold values from -4.172325e-07 to 4.172325e-07
- mlp_out_m: float32 [3072, 768], P('mp', 'dp'), may hold values from -4.172325e-07 to 4.172325e-07
- skip_m: float32 [1024, 2560], P('dp'), may hold values from -4.172325e-07 to 4.172325e-07
- decoder_m: float32 [365120], P('dp'), may hold values from -4.172325e-07 to 4.172325e-07
- stem_v: float32 [256, 1024], P('dp'), may hold values from 3.5498253e-16 to 1.4199301e-15
- embed_v: float32 [1024, 768], P('dp'), may hold values from 3.5498253e-16 to 1.4199301e-15
- token_v: float32 [202, 768], P(None, 'dp'), may hold values from 3.5498253e-16 to 1.4199301e-15
- qkv_v: float32 [768, 2304], P('dp', 'mp'), may hold values from 3.5498253e-16 to 1.4199301e-15
- out_v: float32 [768, 768], P('mp', 'dp'), may hold values from 3.5498253e-16 to 1.4199301e-15
- mlp_in_v: float32 [768, 3072], P('dp', 'mp'), may hold values from 3.5498253e-16 to 1.4199301e-15
- mlp_out_v: float32 [3072, 768], P('mp', 'dp'), may hold values from 3.5498253e-16 to 1.4199301e-15
- skip_v: float32 [1024, 2560], P('dp'), may hold values from 3.5498253e-16 to 1.4199301e-15
- decoder_v: float32 [365120], P('dp'), may hold values from 3.5498253e-16 to 1.4199301e-15
Outputs:
- loss: float32 [], replicated
- pixel_count: float32 [], replicated
- grad_norm: float32 [], replicated
- new_stem_w: float32 [256, 1024], P('dp')
- new_embed_w: float32 [1024, 768], P('dp')
- new_token_params: float32 [202, 768], P(None, 'dp')
- new_qkv_w: float32 [768, 2304], P('dp', 'mp')
- new_out_w: float32 [768, 768], P('mp', 'dp')
- new_mlp_in_w: float32 [768, 3072], P('dp', 'mp')
- new_mlp_out_w: float32 [3072, 768], P('mp', 'dp')
- new_skip_w: float32 [1024, 2560], P('dp')
- new_decoder_w: float32 [365120], P('dp')
- new_stem_m: float32 [256, 1024], P('dp')
- new_embed_m: float32 [1024, 768], P('dp')
- new_token_m: float32 [202, 768], P(None, 'dp')
- new_qkv_m: float32 [768, 2304], P('dp', 'mp')
- new_out_m: float32 [768, 768], P('mp', 'dp')
- new_mlp_in_m: float32 [768, 3072], P('dp', 'mp')
- new_mlp_out_m: float32 [3072, 768], P('mp', 'dp')
- new_skip_m: float32 [1024, 2560], P('dp')
- new_decoder_m: float32 [365120], P('dp')
- new_stem_v: float32 [256, 1024], P('dp')
- new_embed_v: float32 [1024, 768], P('dp')
- new_token_v: float32 [202, 768], P(None, 'dp')
- new_qkv_v: float32 [768, 2304], P('dp', 'mp')
- new_out_v: float32 [768, 768], P('mp', 'dp')
- new_mlp_in_v: float32 [768, 3072], P('dp', 'mp')
- new_mlp_out_v: float32 [3072, 768], P('mp', 'dp')
- new_skip_v: float32 [1024, 2560], P('dp')
- new_decoder_v: float32 [365120], P('dp')
The draws below stay inside these ranges and needn't reach their ends.
All inputs are finite; a program needn't handle non-finite values. No bound on the sum of `background` on one device may be relied on, other than what follows from the above.
Results may differ from the reference program's by a relative error of at most 0.0075.
Values may be sent and summed in bfloat16 or wider, within the bound.
No kernel may reach another device: no remote copies, remote signals or barrier semaphores. Data moves between devices by JAX's collectives and lax.ppermute only.
A program may use at most 256 MiB of HBM per device.

```python
import math
import jax
import jax.numpy as jnp
from jax import lax

D = 768
HEADS = 12
HEAD_DIM = 64
FF = 3072
C_STEM = 1024
PATCHES = 196
PIXELS = 256
CHAN_A = 256
CHAN_B = 128
CHAN_C = 64
CHAN_D = 16
CLASSES = 9
PATIENTS = 16
STEP = 10
SLICES = 64
SKIPW = 2560
DEC_FLAT = 365120
PARAMS = 11268160


def draw_token_params(key, part):
    key = jax.random.fold_in(key, 11)
    total_rows = PATCHES + 6
    noise = jax.random.normal(key, (total_rows, D), jnp.float32)
    row_id = jnp.arange(total_rows, dtype=jnp.int32)[:, None]
    column = jnp.arange(D, dtype=jnp.int32)[None, :].astype(jnp.float32)
    rising = 0.5 + 1.5 * column / D
    is_gain = (row_id >= PATCHES) & ((row_id - PATCHES) % 2 == 0)
    gain_value = rising * (1.0 + 0.15 * noise)
    other = jnp.where(row_id >= PATCHES, 0.3, 0.5) * noise
    return jnp.where(is_gain, gain_value, other)


def draw_decoder_w(key, part):
    key = jax.random.fold_in(key, 12)
    index = jnp.arange(DEC_FLAT, dtype=jnp.int32)
    edge_one = D * CHAN_A
    edge_two = edge_one + CHAN_A * 4 * CHAN_B
    edge_three = edge_two + CHAN_B * 4 * CHAN_C
    edge_four = edge_three + CHAN_C * 4 * CHAN_D
    fan_in = jnp.where(index < edge_one, D, jnp.where(index < edge_two, CHAN_A, jnp.where(index < edge_three, CHAN_B, jnp.where(index < edge_four, CHAN_C, CHAN_D))))
    return jax.random.normal(key, (DEC_FLAT,), jnp.float32) * lax.rsqrt(fan_in.astype(jnp.float32))


def plant(drawn, stream_key, smallest, top_value):
    place = [jax.random.randint(jax.random.fold_in(stream_key, axis), (), 0, length) for axis, length in enumerate(drawn.shape)]
    longest = drawn.shape.index(max(drawn.shape))
    neighbour = place[:longest] + [(place[longest] + 1) % drawn.shape[longest]] + place[longest + 1:]
    return drawn.at[tuple(place)].set(smallest).at[tuple(neighbour)].set(top_value)


def block_scale(stream_key, extent, shards, smallest, largest):
    level, own = 1.0, jax.random.fold_in(stream_key, 6)
    for position, blocks in shards:
        heights = jnp.exp(jax.random.uniform(jax.random.fold_in(own, position), (blocks,), jnp.float32, smallest / len(shards), largest / len(shards)))
        level = level * jnp.repeat(heights, extent[position] // blocks).reshape([-1 if axis == position else 1 for axis in range(len(extent))])
    return level


def bell_draw(key, dims, deviation, bound, shards=(), held_as=jnp.bfloat16):
    level = block_scale(key, dims, shards, -0.22, 0.18) if shards else 1.0
    entries = jax.random.normal(key, dims, jnp.float32) * deviation * level
    return jnp.minimum(jnp.maximum(entries, -bound), bound).astype(held_as)


def setup_inputs(seed: int = 0) -> dict:
    splits = jax.random.split(jax.random.key(seed), 32)
    images = bell_draw(splits[0], (SLICES, PATCHES, PIXELS), 1.0, 6.0, ((0, 8),))
    labels = plant(jax.random.randint(splits[1], (SLICES, PATCHES, PIXELS), 0, CLASSES), jax.random.fold_in(splits[1], 1), 0, CLASSES - 1).astype(jnp.int32)
    background = plant((jax.random.randint(splits[2], (SLICES,), 0, 4) < 1).astype(jnp.int32), jax.random.fold_in(splits[2], 1), 0, 1)
    patients = plant(jax.random.randint(splits[3], (SLICES,), 0, PATIENTS), jax.random.fold_in(splits[3], 1), 0, PATIENTS - 1).astype(jnp.int32)
    stem_w = bell_draw(splits[4], (PIXELS, C_STEM), PIXELS ** -0.5, 0.375, ((0, 8),), jnp.float32)
    embed_w = bell_draw(splits[5], (C_STEM, D), C_STEM ** -0.5, 0.1875, ((0, 8),), jnp.float32)
    token_params = draw_token_params(jax.random.fold_in(splits[31], 71), 0)
    qkv_w = bell_draw(splits[7], (D, 3 * D), D ** -0.5, 0.21875, ((0, 8), (1, 4)), jnp.float32)
    out_w = bell_draw(splits[8], (D, D), (D // 8) ** -0.5, 0.625, ((0, 4), (1, 8)), jnp.float32)
    mlp_in_w = bell_draw(splits[9], (D, FF), D ** -0.5, 0.21875, ((0, 8), (1, 4)), jnp.float32)
    mlp_out_w = bell_draw(splits[10], (FF, D), FF ** -0.5, 0.109375, ((0, 4), (1, 8)), jnp.float32)
    skip_w = bell_draw(splits[11], (C_STEM, SKIPW), C_STEM ** -0.5, 0.1875, ((0, 8),), jnp.float32)
    decoder_w = draw_decoder_w(jax.random.fold_in(splits[31], 71), 0)
    stem_m = bell_draw(splits[13], (PIXELS, C_STEM), (0.00022 / PARAMS ** 0.5), 4.172325134277344e-07, ((0, 8),), jnp.float32)
    embed_m = bell_draw(splits[14], (C_STEM, D), (0.00022 / PARAMS ** 0.5), 4.172325134277344e-07, ((0, 8),), jnp.float32)
    token_m = bell_draw(splits[15], (PATCHES + 6, D), (0.00022 / PARAMS ** 0.5), 4.172325134277344e-07, ((1, 8),), jnp.float32)
    qkv_m = bell_draw(splits[16], (D, 3 * D), (0.00022 / PARAMS ** 0.5), 4.172325134277344e-07, ((0, 8), (1, 4)), jnp.float32)
    out_m = bell_draw(splits[17], (D, D), (0.00022 / PARAMS ** 0.5), 4.172325134277344e-07, ((0, 4), (1, 8)), jnp.float32)
    mlp_in_m = bell_draw(splits[18], (D, FF), (0.00022 / PARAMS ** 0.5), 4.172325134277344e-07, ((0, 8), (1, 4)), jnp.float32)
    mlp_out_m = bell_draw(splits[19], (FF, D), (0.00022 / PARAMS ** 0.5), 4.172325134277344e-07, ((0, 4), (1, 8)), jnp.float32)
    skip_m = bell_draw(splits[20], (C_STEM, SKIPW), (0.00022 / PARAMS ** 0.5), 4.172325134277344e-07, ((0, 8),), jnp.float32)
    decoder_m = bell_draw(splits[21], (DEC_FLAT,), (0.00022 / PARAMS ** 0.5), 4.172325134277344e-07, ((0, 8),), jnp.float32)
    stem_v = jnp.clip(jnp.exp(math.log(1.4199301397559692e-15) - 1.3862944 * jax.random.uniform(splits[22], (PIXELS, C_STEM), jnp.float32) ** block_scale(splits[22], (PIXELS, C_STEM), ((0, 8),), -0.2, 0.2)), 3.549825349389923e-16, 1.4199301397559692e-15)
    embed_v = jnp.clip(jnp.exp(math.log(1.4199301397559692e-15) - 1.3862944 * jax.random.uniform(splits[23], (C_STEM, D), jnp.float32) ** block_scale(splits[23], (C_STEM, D), ((0, 8),), -0.2, 0.2)), 3.549825349389923e-16, 1.4199301397559692e-15)
    token_v = jnp.clip(jnp.exp(math.log(1.4199301397559692e-15) - 1.3862944 * jax.random.uniform(splits[24], (PATCHES + 6, D), jnp.float32) ** block_scale(splits[24], (PATCHES + 6, D), ((1, 8),), -0.2, 0.2)), 3.549825349389923e-16, 1.4199301397559692e-15)
    qkv_v = jnp.clip(jnp.exp(math.log(1.4199301397559692e-15) - 1.3862944 * jax.random.uniform(splits[25], (D, 3 * D), jnp.float32) ** block_scale(splits[25], (D, 3 * D), ((0, 8), (1, 4)), -0.2, 0.2)), 3.549825349389923e-16, 1.4199301397559692e-15)
    out_v = jnp.clip(jnp.exp(math.log(1.4199301397559692e-15) - 1.3862944 * jax.random.uniform(splits[26], (D, D), jnp.float32) ** block_scale(splits[26], (D, D), ((0, 4), (1, 8)), -0.2, 0.2)), 3.549825349389923e-16, 1.4199301397559692e-15)
    mlp_in_v = jnp.clip(jnp.exp(math.log(1.4199301397559692e-15) - 1.3862944 * jax.random.uniform(splits[27], (D, FF), jnp.float32) ** block_scale(splits[27], (D, FF), ((0, 8), (1, 4)), -0.2, 0.2)), 3.549825349389923e-16, 1.4199301397559692e-15)
    mlp_out_v = jnp.clip(jnp.exp(math.log(1.4199301397559692e-15) - 1.3862944 * jax.random.uniform(splits[28], (FF, D), jnp.float32) ** block_scale(splits[28], (FF, D), ((0, 4), (1, 8)), -0.2, 0.2)), 3.549825349389923e-16, 1.4199301397559692e-15)
    skip_v = jnp.clip(jnp.exp(math.log(1.4199301397559692e-15) - 1.3862944 * jax.random.uniform(splits[29], (C_STEM, SKIPW), jnp.float32) ** block_scale(splits[29], (C_STEM, SKIPW), ((0, 8),), -0.2, 0.2)), 3.549825349389923e-16, 1.4199301397559692e-15)
    decoder_v = jnp.clip(jnp.exp(math.log(1.4199301397559692e-15) - 1.3862944 * jax.random.uniform(splits[30], (DEC_FLAT,), jnp.float32) ** block_scale(splits[30], (DEC_FLAT,), ((0, 8),), -0.2, 0.2)), 3.549825349389923e-16, 1.4199301397559692e-15)
    return {"images": images, "labels": labels, "background": background, "patients": patients, "stem_w": stem_w, "embed_w": embed_w, "token_params": token_params, "qkv_w": qkv_w, "out_w": out_w, "mlp_in_w": mlp_in_w, "mlp_out_w": mlp_out_w, "skip_w": skip_w, "decoder_w": decoder_w, "stem_m": stem_m, "embed_m": embed_m, "token_m": token_m, "qkv_m": qkv_m, "out_m": out_m, "mlp_in_m": mlp_in_m, "mlp_out_m": mlp_out_m, "skip_m": skip_m, "decoder_m": decoder_m, "stem_v": stem_v, "embed_v": embed_v, "token_v": token_v, "qkv_v": qkv_v, "out_v": out_v, "mlp_in_v": mlp_in_v, "mlp_out_v": mlp_out_v, "skip_v": skip_v, "decoder_v": decoder_v}


@jax.custom_vjp
def low(v):
    return lax.optimization_barrier(v.astype(jnp.bfloat16)).astype(jnp.float32)

@jax.custom_vjp
def low_back(v):
    return v

def low_keep(v):
    return (low(v), None)

def low_pass(kept, grad):
    return (grad,)

def back_keep(v):
    return (v, None)

def back_low(kept, grad):
    return (low(grad),)
low.defvjp(low_keep, low_pass)
low_back.defvjp(back_keep, back_low)
norm_eps = 1e-06
dice_eps = 1e-05
clip_limit = 0.002
learn_rate = 0.05
token_rate = 0.5
beta_one = 0.9
beta_two = 0.999
adam_eps = 1e-08
decay_rate = 0.01
highest = lax.Precision.HIGHEST

def gelu_fn(value):
    return jax.nn.gelu(value, approximate=True)

def layer_norm(inputs, gain, shift):
    center = inputs - lax.optimization_barrier(jnp.mean(inputs, axis=-1, keepdims=True))
    spread = lax.optimization_barrier(jnp.mean(center * center, axis=-1, keepdims=True))
    return center * lax.rsqrt(spread + norm_eps) * gain + shift

def product(left, right):
    return low_back(jnp.dot(left, right, precision=highest))

def split_decoder(flat):
    edge_one = D * CHAN_A
    edge_two = edge_one + CHAN_A * 4 * CHAN_B
    edge_three = edge_two + CHAN_B * 4 * CHAN_C
    edge_four = edge_three + CHAN_C * 4 * CHAN_D
    return (flat[:edge_one].reshape(D, CHAN_A), flat[edge_one:edge_two].reshape(CHAN_A, 4 * CHAN_B), flat[edge_two:edge_three].reshape(CHAN_B, 4 * CHAN_C), flat[edge_three:edge_four].reshape(CHAN_C, 4 * CHAN_D), flat[edge_four:].reshape(CHAN_D, 4 * CLASSES))

def forward(masters, pixels, labels, background, patients):
    stem_w, embed_w, tokens, qkv_w, out_w, mlp_in_w, mlp_out_w, skip_w, decoder_w = [low(weight) for weight in masters]
    dec_w, up_one, up_two, up_three, head_w = split_decoder(decoder_w)
    slices = pixels.shape[0]
    hidden = low(gelu_fn(product(pixels, stem_w)))
    embed = product(hidden, embed_w) + tokens[:PATCHES]
    normed = low(layer_norm(embed, tokens[PATCHES], tokens[PATCHES + 1]))
    triple = product(normed, qkv_w).reshape(slices, PATCHES, HEADS, 3, HEAD_DIM)
    triple = low(triple)
    queries = triple[:, :, :, 0]
    keys_low = triple[:, :, :, 1]
    values = triple[:, :, :, 2]
    scores = low_back(jnp.einsum('sqhd,skhd->shqk', queries, keys_low, precision=highest)) * HEAD_DIM ** (-0.5)
    attend = jax.nn.softmax(scores, axis=-1)
    context = low_back(jnp.einsum('shqk,skhd->sqhd', low(attend), values, precision=highest))
    context = low(context).reshape(slices, PATCHES, D)
    resid = embed + product(context, out_w)
    normed2 = low(layer_norm(resid, tokens[PATCHES + 2], tokens[PATCHES + 3]))
    inner = low(gelu_fn(product(normed2, mlp_in_w)))
    resid2 = resid + product(inner, mlp_out_w)
    final = low(layer_norm(resid2, tokens[PATCHES + 4], tokens[PATCHES + 5]))
    level0 = low(gelu_fn(product(final, dec_w)))
    skips = product(hidden, skip_w)
    split_a = 4 * CHAN_B
    split_b = split_a + 16 * CHAN_C
    level1 = low(gelu_fn(product(level0, up_one).reshape(slices, PATCHES, 4, CHAN_B) + skips[..., :split_a].reshape(slices, PATCHES, 4, CHAN_B)))
    level2 = low(gelu_fn(product(level1, up_two).reshape(slices, PATCHES, 16, CHAN_C) + skips[..., split_a:split_b].reshape(slices, PATCHES, 16, CHAN_C)))
    level3 = low(gelu_fn(product(level2, up_three).reshape(slices, PATCHES, 64, CHAN_D) + skips[..., split_b:].reshape(slices, PATCHES, 64, CHAN_D)))
    logits = product(level3, head_w).reshape(slices, PATCHES, PIXELS, CLASSES)
    log_prob = jax.nn.log_softmax(logits, axis=-1)
    onehot = (labels[..., None] == jnp.arange(CLASSES, dtype=jnp.int32)).astype(jnp.float32)
    keep = (1 - background).astype(jnp.float32)
    ce_sum = -jnp.sum(keep[:, None, None, None] * onehot * log_prob)
    pixel_count = jnp.sum(keep) * (PATCHES * PIXELS)
    class_prob = jnp.exp(log_prob)
    intersection = lax.optimization_barrier(jnp.sum(class_prob * onehot, axis=(1, 2)))
    pred_sum = lax.optimization_barrier(jnp.sum(class_prob, axis=(1, 2)))
    true_sum = lax.optimization_barrier(jnp.sum(onehot, axis=(1, 2)))
    owner = (patients[:, None] == jnp.arange(PATIENTS, dtype=jnp.int32)).astype(jnp.float32)
    pat_over = jnp.dot(owner.T, intersection, precision=highest)
    pat_pred = jnp.dot(owner.T, pred_sum, precision=highest)
    pat_true = jnp.dot(owner.T, true_sum, precision=highest)
    dice = (2.0 * pat_over + dice_eps) / (pat_pred + pat_true + dice_eps)
    loss = ce_sum / jnp.maximum(pixel_count, 1.0) + 1.0 - jnp.mean(dice)
    return (loss, pixel_count)

def adamw(weight, grad, first, second, rate):
    first_new = beta_one * first + (1.0 - beta_one) * grad
    second_new = beta_two * second + (1.0 - beta_two) * grad * grad
    first_hat = first_new / (1.0 - beta_one ** STEP)
    second_hat = second_new / (1.0 - beta_two ** STEP)
    new_weight = weight - rate * (first_hat / (jnp.sqrt(second_hat) + adam_eps) + decay_rate * weight)
    return (new_weight, first_new, second_new)

def reference(images, labels, background, patients, stem_w, embed_w, token_params, qkv_w, out_w, mlp_in_w, mlp_out_w, skip_w, decoder_w, stem_m, embed_m, token_m, qkv_m, out_m, mlp_in_m, mlp_out_m, skip_m, decoder_m, stem_v, embed_v, token_v, qkv_v, out_v, mlp_in_v, mlp_out_v, skip_v, decoder_v):
    masters = (stem_w, embed_w, token_params, qkv_w, out_w, mlp_in_w, mlp_out_w, skip_w, decoder_w)
    firsts = (stem_m, embed_m, token_m, qkv_m, out_m, mlp_in_m, mlp_out_m, skip_m, decoder_m)
    seconds = (stem_v, embed_v, token_v, qkv_v, out_v, mlp_in_v, mlp_out_v, skip_v, decoder_v)
    rates = (learn_rate, learn_rate, token_rate, learn_rate, learn_rate, learn_rate, learn_rate, learn_rate, learn_rate)
    pixels = images.astype(jnp.float32)

    def loss_of(params):
        return forward(params, pixels, labels, background, patients)
    loss, pullback, pixel_count = jax.vjp(loss_of, masters, has_aux=True)
    grads = pullback(jnp.ones_like(loss))[0]
    total = sum((jnp.sum(grad * grad) for grad in grads))
    grad_norm = jnp.sqrt(total)
    factor = jnp.minimum(1.0, clip_limit / (grad_norm + 1e-06))
    results = [adamw(weight, grad * factor, first, second, rate) for weight, grad, first, second, rate in zip(masters, grads, firsts, seconds, rates)]
    news = [item[0] for item in results]
    moms = [item[1] for item in results]
    secs = [item[2] for item in results]
    return (loss, pixel_count, grad_norm, news[0], news[1], news[2], news[3], news[4], news[5], news[6], news[7], news[8], moms[0], moms[1], moms[2], moms[3], moms[4], moms[5], moms[6], moms[7], moms[8], secs[0], secs[1], secs[2], secs[3], secs[4], secs[5], secs[6], secs[7], secs[8])
```

```python
import jax
import jax.numpy as jnp
from jax import lax
from jax.experimental import pallas as pl
from jax.experimental.pallas import tpu as pltpu
from jax.sharding import PartitionSpec as P

D = 768
HEAD_DIM = 64
PATCHES = 196
PAD = 208
PIXELS = 256
C_STEM = 1024
CHAN_A = 256
CHAN_B = 128
CHAN_C = 64
CHAN_D = 16
CLASSES = 9
PATIENTS = 16
STEP = 10
GROUP = 32
LANES = 128

norm_eps = 1e-06
dice_eps = 1e-05
clip_limit = 0.002
learn_rate = 0.05
token_rate = 0.5
beta_one = 0.9
beta_two = 0.999
adam_eps = 1e-08
decay_rate = 0.01
highest = lax.Precision.HIGHEST
bf16 = jnp.bfloat16
f32 = jnp.float32
MIB = 1024 * 1024


def gelu_fn(value):
    return jax.nn.gelu(value, approximate=True)


def layer_norm(inputs, gain, shift):
    center = inputs - jnp.mean(inputs, axis=-1, keepdims=True)
    spread = jnp.mean(center * center, axis=-1, keepdims=True)
    return center * lax.rsqrt(spread + norm_eps) * gain + shift


def matmul(left, right):
    return jnp.dot(left, right, preferred_element_type=f32)


def matmul_t(left, right):
    return lax.dot_general(left, right, (((1,), (1,)), ((), ())), preferred_element_type=f32)


def t_matmul(left, right):
    return lax.dot_general(left, right, (((0,), (0,)), ((), ())), preferred_element_type=f32)


def gelu_back(pre_value, grad):
    return jax.vjp(gelu_fn, pre_value)[1](grad)[0]


def norm_back(inputs, gain, shift, grad):
    return jax.vjp(layer_norm, inputs, gain, shift)[1](grad)


def swap(value, axis, bit):
    size = lax.axis_size(axis)
    return lax.ppermute(value, axis, [(i, i ^ (1 << bit)) for i in range(size)])


def my_bit(axis, bit):
    return (lax.axis_index(axis) >> bit) & 1


def double(value, axis, bit, dim):
    other = swap(value, axis, bit)
    mine = my_bit(axis, bit)
    low_half = jnp.where(mine == 0, value, other)
    high_half = jnp.where(mine == 0, other, value)
    return jnp.stack([low_half, high_half], axis=dim)


def halve(kept, axis, bit, dim):
    mine = my_bit(axis, bit)
    send = lax.dynamic_index_in_dim(kept, 1 - mine, dim, keepdims=False).astype(bf16)
    keep = lax.dynamic_index_in_dim(kept, mine, dim, keepdims=False).astype(f32)
    return keep + swap(send, axis, bit).astype(f32)


def log_two(size):
    return size.bit_length() - 1


def gather_rows(block):
    bits = log_two(lax.axis_size("dp"))
    value = block
    for step, bit in enumerate(reversed(range(bits))):
        value = double(value, "dp", bit, step)
    return value.reshape(-1, block.shape[-1])


def scatter_rows(kept):
    size = lax.axis_size("dp")
    bits = log_two(size)
    rows = kept.shape[0] // size
    value = kept.reshape((2,) * bits + (rows, kept.shape[1]))
    for bit in range(bits):
        value = halve(value, "dp", bit, bits - 1 - bit)
    return value


def butterfly(value):
    for axis, bits in (("mp", 2), ("dp", log_two(lax.axis_size("dp")))):
        for bit in range(bits):
            value = value + swap(value, axis, bit)
    return value


def attn_forward_kernel(tri_ref, ctx_ref):
    slices = tri_ref.shape[0] // PAD
    heads = tri_ref.shape[1] // (3 * HEAD_DIM)
    column = lax.broadcasted_iota(jnp.int32, (PAD, PAD), 1)
    for s in range(slices):
        rows = pl.ds(s * PAD, PAD)
        for h in range(heads):
            base = h * 3 * HEAD_DIM
            queries = tri_ref[rows, base : base + HEAD_DIM]
            keys_low = tri_ref[rows, base + HEAD_DIM : base + 2 * HEAD_DIM]
            values = tri_ref[rows, base + 2 * HEAD_DIM : base + 3 * HEAD_DIM]
            attend = soft_rows(matmul_t(queries, keys_low), column)
            context = matmul(attend.astype(bf16), values)
            ctx_ref[rows, h * HEAD_DIM : (h + 1) * HEAD_DIM] = context.astype(bf16)


def soft_rows(scores, column):
    scores = jnp.where(column < PATCHES, scores * HEAD_DIM ** (-0.5), -jnp.inf)
    top = jnp.max(scores, axis=-1, keepdims=True)
    weight = jnp.exp(scores - top)
    return weight / jnp.sum(weight, axis=-1, keepdims=True)


def attn_backward_kernel(tri_ref, gctx_ref, gtri_ref):
    slices = tri_ref.shape[0] // PAD
    heads = tri_ref.shape[1] // (3 * HEAD_DIM)
    column = lax.broadcasted_iota(jnp.int32, (PAD, PAD), 1)
    for s in range(slices):
        rows = pl.ds(s * PAD, PAD)
        for h in range(heads):
            base = h * 3 * HEAD_DIM
            queries = tri_ref[rows, base : base + HEAD_DIM]
            keys_low = tri_ref[rows, base + HEAD_DIM : base + 2 * HEAD_DIM]
            values = tri_ref[rows, base + 2 * HEAD_DIM : base + 3 * HEAD_DIM]
            gctx = gctx_ref[rows, h * HEAD_DIM : (h + 1) * HEAD_DIM]
            attend = soft_rows(matmul_t(queries, keys_low), column)
            g_attend = matmul_t(gctx, values)
            g_values = t_matmul(attend.astype(bf16), gctx)
            inner = jnp.sum(attend * g_attend, axis=-1, keepdims=True)
            g_scores = attend * (g_attend - inner) * HEAD_DIM ** (-0.5)
            g_low = g_scores.astype(bf16)
            g_queries = matmul(g_low, keys_low)
            g_keys = t_matmul(g_low, queries)
            gtri_ref[rows, base : base + HEAD_DIM] = g_queries.astype(bf16)
            gtri_ref[rows, base + HEAD_DIM : base + 2 * HEAD_DIM] = g_keys.astype(bf16)
            gtri_ref[rows, base + 2 * HEAD_DIM : base + 3 * HEAD_DIM] = g_values.astype(bf16)


def attn_forward(triple):
    rows, width = triple.shape
    part = 3 * 3 * HEAD_DIM
    steps = width // (2 * part)
    return pl.pallas_call(
        attn_forward_kernel,
        grid=(steps,),
        in_specs=[pl.BlockSpec((rows, 2 * part), lambda i: (0, i))],
        out_specs=pl.BlockSpec((rows, 2 * part // 3), lambda i: (0, i)),
        out_shape=jax.ShapeDtypeStruct((rows, width // 3), bf16),
        compiler_params=pltpu.CompilerParams(vmem_limit_bytes=32 * MIB),
        name="attn_forward",
    )(triple)


def attn_backward(triple, gctx):
    rows, width = triple.shape
    part = 3 * 3 * HEAD_DIM
    steps = width // (2 * part)
    return pl.pallas_call(
        attn_backward_kernel,
        grid=(steps,),
        in_specs=[
            pl.BlockSpec((rows, 2 * part), lambda i: (0, i)),
            pl.BlockSpec((rows, 2 * part // 3), lambda i: (0, i)),
        ],
        out_specs=pl.BlockSpec((rows, 2 * part), lambda i: (0, i)),
        out_shape=jax.ShapeDtypeStruct((rows, width), bf16),
        compiler_params=pltpu.CompilerParams(vmem_limit_bytes=32 * MIB),
        name="attn_backward",
    )(triple, gctx)


CHUNK = 16


def class_probs(logits_ref, rows, group):
    width = CLASSES * LANES
    values = [
        logits_ref[rows, group * width + c * LANES : group * width + (c + 1) * LANES]
        for c in range(CLASSES)
    ]
    top = values[0]
    for value in values[1:]:
        top = jnp.maximum(top, value)
    weights = [jnp.exp(value - top) for value in values]
    total = weights[0]
    for weight in weights[1:]:
        total = total + weight
    scale = 1.0 / total
    return values, [weight * scale for weight in weights], top + jnp.log(total)


def loss_forward_kernel(level_ref, head_ref, label_ref, logits_ref, stats_ref):
    inner = head_ref.shape[0]
    width = head_ref.shape[1]
    groups = level_ref.shape[1] // inner
    for g in range(groups):
        logits_ref[:, g * width : (g + 1) * width] = matmul(
            level_ref[:, g * inner : (g + 1) * inner], head_ref[...]
        )
    stats_ref[...] = jnp.zeros_like(stats_ref)

    @pl.loop(0, PAD // CHUNK)
    def _(i):
        start = pl.multiple_of(i * CHUNK, CHUNK)
        rows = pl.ds(start, CHUNK)
        row_id = lax.broadcasted_iota(jnp.int32, (CHUNK, LANES), 0) + start
        inside = (row_id < PATCHES).astype(f32)
        for g in range(groups):
            values, probs, log_total = class_probs(logits_ref, rows, g)
            label = label_ref[rows, g * LANES : (g + 1) * LANES]
            cross = jnp.zeros((CHUNK, LANES), f32)
            for c in range(CLASSES):
                hot = (label == c).astype(f32)
                cross = cross + hot * (log_total - values[c])
                for k, term in enumerate((hot * probs[c], inside * probs[c], hot)):
                    spot = 8 * (3 * c + k)
                    part = term[:8]
                    for r in range(8, CHUNK, 8):
                        part = part + term[r : r + 8]
                    stats_ref[0, spot : spot + 8, :] += part
            spot = 8 * 3 * CLASSES
            part = cross[:8]
            for r in range(8, CHUNK, 8):
                part = part + cross[r : r + 8]
            stats_ref[0, spot : spot + 8, :] += part


def loss_forward(level, head, labels):
    rows, width = level.shape
    slices = rows // PAD
    out_width = CLASSES * PIXELS
    stat_rows = 8 * (3 * CLASSES + 1)
    return pl.pallas_call(
        loss_forward_kernel,
        grid=(slices,),
        in_specs=[
            pl.BlockSpec((PAD, width), lambda i: (i, 0)),
            pl.BlockSpec(head.shape, lambda i: (0, 0)),
            pl.BlockSpec((PAD, PIXELS), lambda i: (i, 0)),
        ],
        out_specs=[
            pl.BlockSpec((PAD, out_width), lambda i: (i, 0)),
            pl.BlockSpec((1, stat_rows, LANES), lambda i: (i, 0, 0)),
        ],
        out_shape=[
            jax.ShapeDtypeStruct((rows, out_width), f32),
            jax.ShapeDtypeStruct((slices, stat_rows, LANES), f32),
        ],
        compiler_params=pltpu.CompilerParams(vmem_limit_bytes=40 * MIB),
        name="loss_forward",
    )(level, head, labels)


def loss_backward_kernel(
    coef_ref, logits_ref, label_ref, level_ref, head_ref, g_level_ref, g_head_ref, g_scr
):
    step = pl.program_id(0)
    inner = head_ref.shape[0]
    width = head_ref.shape[1]
    groups = level_ref.shape[1] // inner
    cross_scale = coef_ref[step, 2 * CLASSES]

    @pl.when(step == 0)
    def _():
        g_head_ref[...] = jnp.zeros_like(g_head_ref)

    @pl.loop(0, PAD // CHUNK)
    def _(i):
        start = pl.multiple_of(i * CHUNK, CHUNK)
        rows = pl.ds(start, CHUNK)
        row_id = lax.broadcasted_iota(jnp.int32, (CHUNK, LANES), 0) + start
        inside = (row_id < PATCHES).astype(f32)
        for g in range(groups):
            values, probs, log_total = class_probs(logits_ref, rows, g)
            label = label_ref[rows, g * LANES : (g + 1) * LANES]
            mean = jnp.zeros((CHUNK, LANES), f32)
            pulls = []
            for c in range(CLASSES):
                hot = label == c
                pull = jnp.where(hot, coef_ref[step, c], 0.0) + coef_ref[step, CLASSES + c]
                pulls.append(pull)
                mean = mean + probs[c] * pull
            mean = mean - cross_scale
            for c in range(CLASSES):
                grad = probs[c] * (pulls[c] - mean)
                grad = grad - jnp.where(label == c, cross_scale, 0.0)
                spot = g * width + c * LANES
                g_scr[rows, spot : spot + LANES] = (grad * inside).astype(bf16)

    for g in range(groups):
        part = g_scr[:, g * width : (g + 1) * width]
        g_level_ref[:, g * inner : (g + 1) * inner] = matmul_t(part, head_ref[...])
        g_head_ref[...] += t_matmul(level_ref[:, g * inner : (g + 1) * inner], part)


def loss_backward(coef, logits, labels, level, head):
    rows, width = level.shape
    slices = rows // PAD
    out_width = CLASSES * PIXELS
    return pl.pallas_call(
        loss_backward_kernel,
        grid=(slices,),
        in_specs=[
            pl.BlockSpec(memory_space=pltpu.SMEM),
            pl.BlockSpec((PAD, out_width), lambda i: (i, 0)),
            pl.BlockSpec((PAD, PIXELS), lambda i: (i, 0)),
            pl.BlockSpec((PAD, width), lambda i: (i, 0)),
            pl.BlockSpec(head.shape, lambda i: (0, 0)),
        ],
        out_specs=[
            pl.BlockSpec((PAD, width), lambda i: (i, 0)),
            pl.BlockSpec(head.shape, lambda i: (0, 0)),
        ],
        out_shape=[
            jax.ShapeDtypeStruct((rows, width), f32),
            jax.ShapeDtypeStruct(head.shape, f32),
        ],
        scratch_shapes=[pltpu.VMEM((PAD, out_width), bf16)],
        compiler_params=pltpu.CompilerParams(vmem_limit_bytes=40 * MIB),
        name="loss_backward",
    )(coef, logits, labels, level, head)


def split_decoder(flat):
    edge_one = D * CHAN_A
    edge_two = edge_one + CHAN_A * 4 * CHAN_B
    edge_three = edge_two + CHAN_B * 4 * CHAN_C
    edge_four = edge_three + CHAN_C * 4 * CHAN_D
    return (
        flat[:edge_one].reshape(D, CHAN_A),
        flat[edge_one:edge_two].reshape(CHAN_A, 4 * CHAN_B),
        flat[edge_two:edge_three].reshape(CHAN_B, 4 * CHAN_C),
        flat[edge_three:edge_four].reshape(CHAN_C, 4 * CHAN_D),
        flat[edge_four:].reshape(CHAN_D, 4 * CLASSES),
    )


def same_block(rows, columns, inner, outer):
    row = lax.broadcasted_iota(jnp.int32, (rows, columns), 0) // inner
    column = lax.broadcasted_iota(jnp.int32, (rows, columns), 1) // outer
    return row == column


def block_diag(weight, parents):
    inner, outer = weight.shape
    mask = same_block(parents * inner, parents * outer, inner, outer)
    tiled = jnp.tile(weight, (parents, parents))
    return jnp.where(mask, tiled, jnp.zeros_like(tiled))


def block_diag_grad(grad_big, parents, inner, outer):
    mask = same_block(parents * inner, parents * outer, inner, outer)
    masked = jnp.where(mask, grad_big, 0.0)
    folded = jnp.sum(masked.reshape(parents, inner, parents * outer), axis=0)
    return jnp.sum(folded.reshape(inner, parents, outer), axis=1)


def head_masks():
    wide = CLASSES * GROUP * 4
    column = lax.broadcasted_iota(jnp.int32, (4 * CLASSES, wide), 1)
    source = lax.broadcasted_iota(jnp.int32, (4 * CLASSES, wide), 0)
    pick = source == (column % 4) * CLASSES + column // (GROUP * 4)
    row = lax.broadcasted_iota(jnp.int32, (GROUP * CHAN_D, wide), 0)
    across = lax.broadcasted_iota(jnp.int32, (GROUP * CHAN_D, wide), 1)
    mask = row // CHAN_D == (across // 4) % GROUP
    return pick, mask


def big_head_of(head_b):
    pick, mask = head_masks()
    spread = matmul(head_b, pick.astype(bf16)).astype(bf16)
    tiled = jnp.tile(spread, (GROUP, 1))
    return jnp.where(mask, tiled, jnp.zeros_like(tiled))


def head_grad_of(grad_big):
    pick, mask = head_masks()
    masked = jnp.where(mask, grad_big, 0.0)
    folded = jnp.sum(masked.reshape(GROUP, CHAN_D, -1), axis=0)
    return lax.dot_general(
        folded, pick.astype(f32), (((1,), (1,)), ((), ())), precision=highest,
        preferred_element_type=f32,
    )


def stack_columns(value, width):
    count = value.shape[-1] // width
    return jnp.concatenate(
        [value[..., i * width : (i + 1) * width] for i in range(count)], axis=-2
    )


def unstack_columns(value, count):
    rows = value.shape[-2] // count
    return jnp.concatenate(
        [value[..., i * rows : (i + 1) * rows, :] for i in range(count)], axis=-1
    )


def pad_to(value, axis, size):
    widths = [(0, 0)] * value.ndim
    widths[axis] = (0, size - value.shape[axis])
    return jnp.pad(value, widths)


class Shared:
    def __init__(self, stem_w, embed_w, token_params, decoder_w):
        self.stem_rows = stem_w.shape[0]
        self.embed_rows = embed_w.shape[0]
        self.token_rows = token_params.shape[1]
        self.flat = decoder_w.shape[0]
        self.flat_rows = -(-self.flat // (2 * LANES * 16)) * 16
        self.stem_count = C_STEM // 2 // LANES
        self.embed_count = D // 2 // LANES
        self.cuts = [0]
        for rows in (
            self.stem_rows * self.stem_count,
            self.embed_rows * self.embed_count,
            self.token_rows,
            self.flat_rows,
        ):
            self.cuts.append(self.cuts[-1] + rows)

    def half_flat(self, flat):
        padded = pad_to(flat, flat.ndim - 1, 2 * self.flat_rows * LANES)
        return padded.reshape(flat.shape[:-1] + (2, self.flat_rows, LANES))

    def pieces(self, value):
        one, two, three, four = (
            value[..., a:b, :] for a, b in zip(self.cuts[:-1], self.cuts[1:], strict=True)
        )
        return (
            unstack_columns(one, self.stem_count),
            unstack_columns(two, self.embed_count),
            three,
            four,
        )


def half_columns(value, core, axis=-1):
    axis = axis % value.ndim
    size = value.shape[axis] // 2
    return lax.dynamic_slice_in_dim(value, core * size, size, axis)


def adamw(weight, grad, first, second, rate):
    first_new = beta_one * first + (1.0 - beta_one) * grad
    second_new = beta_two * second + (1.0 - beta_two) * grad * grad
    first_hat = first_new / (1.0 - beta_one**STEP)
    second_hat = second_new / (1.0 - beta_two**STEP)
    new_weight = weight - rate * (
        first_hat / (jnp.sqrt(second_hat) + adam_eps) + decay_rate * weight
    )
    return (new_weight, first_new, second_new)


def body(
    images,
    labels,
    background,
    patients,
    *state,
):
    masters, firsts, seconds = state[:9], state[9:18], state[18:]
    stem_w, embed_w, token_params, qkv_w, out_w, mlp_in_w, mlp_out_w, skip_w, decoder_w = masters
    n_dp = lax.axis_size("dp")
    n_mp = lax.axis_size("mp")
    mp_id = lax.axis_index("mp")
    core = mp_id & 1
    slices = images.shape[0] // n_mp
    rows = slices * PAD
    shared = Shared(stem_w, embed_w, token_params, decoder_w)
    attn_cut = qkv_w.shape[1]
    heads_each = attn_cut // (3 * HEAD_DIM)
    ctx_each = heads_each * HEAD_DIM
    in_each = mlp_in_w.shape[1]

    token_t = pad_to(token_params.T, 1, 2 * LANES)
    dec_half = lax.dynamic_index_in_dim(shared.half_flat(decoder_w), core, 0, keepdims=False)
    first_block = jnp.concatenate(
        [
            stack_columns(half_columns(stem_w, core), LANES),
            stack_columns(half_columns(embed_w, core), LANES),
            half_columns(token_t, core),
            dec_half,
        ],
        axis=0,
    ).astype(bf16)
    attn_block = jnp.concatenate([qkv_w, out_w.T], axis=1).astype(bf16)
    mlp_block = jnp.concatenate([mlp_in_w, mlp_out_w.T], axis=1).astype(bf16)
    skip_block = half_columns(skip_w, core).astype(bf16)

    first_all = double(gather_rows(first_block), "mp", 0, 0)
    first_all = first_all.reshape((2, n_dp) + first_block.shape)
    pieces = shared.pieces(first_all)
    stem_b = jnp.concatenate([pieces[0][0], pieces[0][1]], axis=-1).reshape(PIXELS, C_STEM)
    embed_b = jnp.concatenate([pieces[1][0], pieces[1][1]], axis=-1).reshape(C_STEM, D)
    token_all = jnp.concatenate([pieces[2][0], pieces[2][1]], axis=-1).reshape(D, 2 * LANES)
    tokens = token_all.T.astype(f32)[: PATCHES + 6]
    dec_flat = jnp.swapaxes(pieces[3], 0, 1).reshape(n_dp, -1)[:, : shared.flat].reshape(-1)
    dec_b, one_b, two_b, three_b, head_b = split_decoder(dec_flat)

    def gather_split(block):
        both = double(gather_rows(block), "mp", 1, 1)
        both = both.reshape(both.shape[0], -1)
        return double(both, "mp", 0, 0)

    attn_all = gather_split(attn_block)
    mlp_all = gather_split(mlp_block)
    skip_all = double(gather_rows(skip_block), "mp", 0, 0)

    attn_width = attn_block.shape[1]
    qkv_parts = [
        attn_all[c][:, x * attn_width : x * attn_width + attn_cut]
        for c in range(2)
        for x in range(2)
    ]
    out_parts = [
        attn_all[c][:, x * attn_width + attn_cut : (x + 1) * attn_width]
        for c in range(2)
        for x in range(2)
    ]
    in_parts = [
        mlp_all[c][:, 2 * x * in_each : (2 * x + 1) * in_each] for c in range(2) for x in range(2)
    ]
    down_parts = [
        mlp_all[c][:, (2 * x + 1) * in_each : (2 * x + 2) * in_each]
        for c in range(2)
        for x in range(2)
    ]
    qkv_b = jnp.concatenate(qkv_parts, axis=1)
    out_t = jnp.concatenate(out_parts, axis=1)
    in_b = jnp.concatenate(in_parts, axis=1)
    down_t = jnp.concatenate(down_parts, axis=1)
    skip_b = jnp.concatenate([skip_all[0], skip_all[1]], axis=1)

    take = lambda value: lax.dynamic_slice_in_dim(value, mp_id * slices, slices, 0)
    pixels = pad_to(take(images), 1, PAD).reshape(rows, PIXELS)
    label_own = jnp.pad(take(labels), ((0, 0), (0, PAD - PATCHES), (0, 0)), constant_values=-1)
    label_own = label_own.reshape(rows, PIXELS)
    keep = (1 - take(background)).astype(f32)
    owner = (take(patients)[:, None] == jnp.arange(PATIENTS, dtype=jnp.int32)).astype(f32)

    pos = jnp.tile(pad_to(tokens[:PATCHES], 0, PAD), (slices, 1))
    g1, b1, g2, b2, gf, bf = (tokens[PATCHES + i] for i in range(6))
    pre_stem = matmul(pixels, stem_b)
    hidden = gelu_fn(pre_stem).astype(bf16)
    embed = matmul(hidden, embed_b) + pos
    normed = layer_norm(embed, g1, b1).astype(bf16)
    triple = matmul(normed, qkv_b).astype(bf16)
    context = attn_forward(triple)
    resid = embed + matmul_t(context, out_t)
    normed2 = layer_norm(resid, g2, b2).astype(bf16)
    pre_inner = matmul(normed2, in_b)
    inner = gelu_fn(pre_inner).astype(bf16)
    resid2 = resid + matmul_t(inner, down_t)
    final_low = layer_norm(resid2, gf, bf).astype(bf16)
    pre_zero = matmul(final_low, dec_b)
    level0 = gelu_fn(pre_zero).astype(bf16)
    skips = matmul(hidden, skip_b)
    split_a = 4 * CHAN_B
    split_b = split_a + 16 * CHAN_C
    big_two = block_diag(two_b, 4)
    big_three = block_diag(three_b, 16)
    big_head = big_head_of(head_b)
    pre_one = matmul(level0, one_b) + skips[:, :split_a]
    level1 = gelu_fn(pre_one).astype(bf16)
    pre_two = matmul(level1, big_two) + skips[:, split_a:split_b]
    level2 = gelu_fn(pre_two).astype(bf16)
    pre_three = matmul(level2, big_three) + skips[:, split_b:]
    level3 = gelu_fn(pre_three).astype(bf16)
    logits, stats = loss_forward(level3, big_head, label_own)

    sums = jnp.sum(stats.reshape(slices, 3 * CLASSES + 1, 8 * LANES), axis=-1)
    class_sums = sums[:, : 3 * CLASSES]
    pat_sums = jnp.sum(owner[:, :, None] * class_sums[:, None, :], axis=0)
    cross_sum = jnp.sum(keep * sums[:, 3 * CLASSES])
    packed = jnp.concatenate(
        [pat_sums.reshape(-1), cross_sum[None], jnp.sum(keep)[None]]
    )
    packed = pad_to(packed, 0, 4 * LANES).reshape(4, LANES)
    packed = butterfly(packed).reshape(-1)
    pat_all = packed[: PATIENTS * 3 * CLASSES].reshape(PATIENTS, CLASSES, 3)
    ce_total = packed[PATIENTS * 3 * CLASSES]
    pixel_count = packed[PATIENTS * 3 * CLASSES + 1] * (PATCHES * PIXELS)
    pat_over, pat_pred, pat_true = pat_all[..., 0], pat_all[..., 1], pat_all[..., 2]
    denominator = pat_pred + pat_true + dice_eps
    dice = (2.0 * pat_over + dice_eps) / denominator
    count_floor = jnp.maximum(pixel_count, 1.0)
    loss = ce_total / count_floor + 1.0 - jnp.mean(dice)
    cells = PATIENTS * CLASSES
    over_coef = -2.0 / (cells * denominator)
    pred_coef = (2.0 * pat_over + dice_eps) / (cells * denominator * denominator)
    pick_own = lambda table: jnp.sum(owner[:, :, None] * table[None], axis=1)
    coef = jnp.concatenate(
        [pick_own(over_coef), pick_own(pred_coef), (keep / count_floor)[:, None]], axis=1
    )

    grad_level3, grad_big_head = loss_backward(coef, logits, label_own, level3, big_head)
    grad_head = head_grad_of(grad_big_head)
    grad_pre3 = gelu_back(pre_three, grad_level3).astype(bf16)
    grad_level2 = matmul_t(grad_pre3, big_three)
    grad_pre2 = gelu_back(pre_two, grad_level2).astype(bf16)
    grad_level1 = matmul_t(grad_pre2, big_two)
    grad_pre1 = gelu_back(pre_one, grad_level1).astype(bf16)

    def shared_pair(left, right):
        send = t_matmul(left, half_columns(right, 1 - core)).astype(bf16)
        return send, t_matmul(left, half_columns(right, core))

    def core_sum(send, own):
        return own + swap(send, "mp", 0).astype(f32)

    def shared_finish(kept):
        value = lax.reduce_precision(scatter_rows(kept), 8, 7).astype(bf16)
        return value.astype(f32) + swap(value, "mp", 1).astype(f32)

    grad_skips = jnp.concatenate([grad_pre1, grad_pre2, grad_pre3], axis=1)
    skip_half = shared_finish(core_sum(*shared_pair(hidden, grad_skips)))
    grad_hidden_skip = matmul_t(grad_skips, skip_b)
    grad_level0 = matmul_t(grad_pre1, one_b)
    grad_pre0 = gelu_back(pre_zero, grad_level0).astype(bf16)
    grad_final = matmul_t(grad_pre0, dec_b)
    grad_three = block_diag_grad(t_matmul(level2, grad_pre3), 16, CHAN_C, 4 * CHAN_D)
    grad_two = block_diag_grad(t_matmul(level1, grad_pre2), 4, CHAN_B, 4 * CHAN_C)
    grad_one = t_matmul(level0, grad_pre1)
    grad_dec = t_matmul(final_low, grad_pre0)
    grad_decoder = jnp.concatenate(
        [
            grad_dec.reshape(-1),
            grad_one.reshape(-1),
            grad_two.reshape(-1),
            grad_three.reshape(-1),
            grad_head.reshape(-1),
        ]
    )

    grad_resid2, grad_gf, grad_bf = norm_back(resid2, gf, bf, grad_final)
    grad_resid2_low = grad_resid2.astype(bf16)
    grad_inner = matmul(grad_resid2_low, down_t)
    grad_pre = gelu_back(pre_inner, grad_inner).astype(bf16)

    def mlp_half(which):
        g_in = t_matmul(normed2, half_columns(grad_pre, which))
        g_down = t_matmul(grad_resid2_low, half_columns(inner, which))
        return jnp.concatenate(
            [
                g_in[:, :in_each],
                g_down[:, :in_each],
                g_in[:, in_each:],
                g_down[:, in_each:],
            ],
            axis=1,
        )

    def split_finish(kept):
        width = kept.shape[1] // 2
        x = my_bit("mp", 1)
        send = lax.dynamic_slice_in_dim(kept, (1 - x) * width, width, 1).astype(bf16)
        own = lax.dynamic_slice_in_dim(kept, x * width, width, 1)
        return scatter_rows(own + swap(send, "mp", 1).astype(f32))

    mlp_own = split_finish(core_sum(mlp_half(1 - core).astype(bf16), mlp_half(core)))

    grad_resid_ln, grad_g2, grad_b2 = norm_back(resid, g2, b2, matmul_t(grad_pre, in_b))
    grad_resid = grad_resid2 + grad_resid_ln
    grad_resid_low = grad_resid.astype(bf16)
    grad_context = matmul(grad_resid_low, out_t).astype(bf16)
    grad_triple = attn_backward(triple, grad_context)

    def attn_half(which):
        g_qkv = t_matmul(normed, half_columns(grad_triple, which))
        g_out = t_matmul(grad_resid_low, half_columns(context, which))
        return jnp.concatenate(
            [
                g_qkv[:, :attn_cut],
                g_out[:, :ctx_each],
                g_qkv[:, attn_cut:],
                g_out[:, ctx_each:],
            ],
            axis=1,
        )

    attn_own = split_finish(core_sum(attn_half(1 - core).astype(bf16), attn_half(core)))

    grad_embed_ln, grad_g1, grad_b1 = norm_back(embed, g1, b1, matmul_t(grad_triple, qkv_b))
    grad_embed = grad_resid + grad_embed_ln
    gains = jnp.stack([grad_g1, grad_b1, grad_g2, grad_b2, grad_gf, grad_bf])
    grad_pos = jnp.sum(grad_embed.reshape(slices, PAD, D), axis=0)[:PATCHES]
    grad_token = pad_to(jnp.concatenate([grad_pos, gains], axis=0).T, 1, 2 * LANES)
    grad_embed_low = grad_embed.astype(bf16)
    grad_hidden = matmul_t(grad_embed_low, embed_b) + grad_hidden_skip
    grad_pre_stem = gelu_back(pre_stem, grad_hidden).astype(bf16)
    stem_pair = shared_pair(pixels, grad_pre_stem)
    embed_pair = shared_pair(hidden, grad_embed_low)
    decoder_halves = shared.half_flat(grad_decoder.reshape(n_dp, -1))

    def first_half(which, stem_part, embed_part):
        blocks = lambda value: value.reshape(n_dp, -1, value.shape[-1])
        packed_half = jnp.concatenate(
            [
                stack_columns(blocks(stem_part), LANES),
                stack_columns(blocks(embed_part), LANES),
                blocks(half_columns(grad_token, which)).astype(stem_part.dtype),
                lax.dynamic_index_in_dim(decoder_halves, which, 1, keepdims=False).astype(
                    stem_part.dtype
                ),
            ],
            axis=1,
        )
        return packed_half.reshape(-1, LANES)

    first_half_sum = shared_finish(
        core_sum(
            first_half(1 - core, stem_pair[0], embed_pair[0]),
            first_half(core, stem_pair[1], embed_pair[1]),
        )
    )

    square = lambda value: jnp.sum(value * value)
    n_copies = n_mp // 2
    local = (
        square(mlp_own)
        + square(attn_own)
        + (square(skip_half) + square(first_half_sum)) / n_copies
    )
    total = butterfly(jnp.broadcast_to(local, (8, LANES)))[0, 0]
    grad_norm = jnp.sqrt(total)
    factor = jnp.minimum(1.0, clip_limit / (grad_norm + 1e-06))

    skip_both = double(skip_half, "mp", 0, 0)
    red_skip = jnp.concatenate([skip_both[0], skip_both[1]], axis=1)
    own = shared.pieces(double(first_half_sum, "mp", 0, 0))
    red_stem = jnp.concatenate([own[0][0], own[0][1]], axis=-1)
    red_embed = jnp.concatenate([own[1][0], own[1][1]], axis=-1)
    token_both = jnp.concatenate([own[2][0], own[2][1]], axis=-1)
    red_token = token_both[:, : PATCHES + 6].T
    red_decoder = own[3].reshape(-1)[: shared.flat]
    red_qkv = attn_own[:, :attn_cut]
    red_out = attn_own[:, attn_cut:].T
    red_in = mlp_own[:, :in_each]
    red_down = mlp_own[:, in_each:].T
    reduced = (
        red_stem, red_embed, red_token, red_qkv, red_out, red_in, red_down, red_skip, red_decoder,
    )
    rates = [learn_rate] * 9
    rates[2] = token_rate
    results = [
        adamw(weight, grad * factor, first, second, rate)
        for weight, grad, first, second, rate in zip(
            masters, reduced, firsts, seconds, rates, strict=True
        )
    ]
    news = [item[0] for item in results]
    moms = [item[1] for item in results]
    secs = [item[2] for item in results]
    return (loss, pixel_count, grad_norm, *news, *moms, *secs)


def solution(mesh):
    weights = (
        P("dp", None),
        P("dp", None),
        P(None, "dp"),
        P("dp", "mp"),
        P("mp", "dp"),
        P("dp", "mp"),
        P("mp", "dp"),
        P("dp", None),
        P("dp"),
    )
    placed = (P("dp", None, None), P("dp", None, None), P("dp"), P("dp")) + weights * 3
    outs = (P(), P(), P()) + weights * 3
    return jax.shard_map(body, mesh=mesh, in_specs=placed, out_specs=outs, check_vma=False)
```

```python
import jax
import jax.numpy as jnp
from jax import lax
from jax.experimental import pallas as pl
from jax.experimental.pallas import tpu as pltpu
from jax.sharding import PartitionSpec as P

D = 768
HEAD_DIM = 64
PATCHES = 196
PAD = 208
PIXELS = 256
C_STEM = 1024
CHAN_A = 256
CHAN_B = 128
CHAN_C = 64
CHAN_D = 16
CLASSES = 9
PATIENTS = 16
STEP = 10
GROUP = 32
LANES = 128

norm_eps = 1e-06
dice_eps = 1e-05
clip_limit = 0.002
learn_rate = 0.05
token_rate = 0.5
beta_one = 0.9
beta_two = 0.999
adam_eps = 1e-08
decay_rate = 0.01
highest = lax.Precision.HIGHEST
bf16 = jnp.bfloat16
f32 = jnp.float32
MIB = 1024 * 1024


def layer_norm(inputs, gain, shift):
    center = inputs - jnp.mean(inputs, axis=-1, keepdims=True)
    spread = jnp.mean(center * center, axis=-1, keepdims=True)
    return center * lax.rsqrt(spread + norm_eps) * gain + shift


def matmul(left, right):
    return jnp.dot(left, right, preferred_element_type=f32)


def matmul_t(left, right):
    return lax.dot_general(left, right, (((1,), (1,)), ((), ())), preferred_element_type=f32)


def t_matmul(left, right):
    return lax.dot_general(left, right, (((0,), (0,)), ((), ())), preferred_element_type=f32)


FULL = pl.BlockSpec(memory_space=pltpu.VMEM)
SCALAR = pl.BlockSpec(memory_space=pltpu.SMEM)
BLOCK = 256
CHUNK = 16
GELU_SCALE = 0.7978845608028654
GELU_CUBE = 0.044715


def cost(micros):
    return pl.CostEstimate(
        flops=int(micros * 3e9), bytes_accessed=int(micros * 9e6), transcendentals=0
    )


def params():
    return pltpu.CompilerParams(vmem_limit_bytes=58 * MIB)


def run_after(kernel, count, after):
    extra = len(after)

    def ordered(*refs):
        kernel(*refs[:count], *refs[count + extra :])

    return ordered, [pl.BlockSpec(memory_space=pl.ANY)] * extra


def swap(value, axis, bit):
    size = lax.axis_size(axis)
    return lax.ppermute(value, axis, [(i, i ^ (1 << bit)) for i in range(size)])


def my_bit(axis, bit):
    return (lax.axis_index(axis) >> bit) & 1


def log_two(size):
    return size.bit_length() - 1


def gather_kernel(lanes, mine_ref, own_ref, other_ref, out_ref):
    mine = mine_ref[0]
    for which, source_ref in ((mine, own_ref), (1 - mine, other_ref)):
        if lanes:
            width = own_ref.shape[1]
            out_ref[:, pl.ds(pl.multiple_of(which * width, LANES), width)] = source_ref[...]
        else:
            for a in range(out_ref.shape[0]):
                out_ref[a, which] = source_ref[a]


def gate_kernel(value_ref, *refs):
    pass


def run_gate(value, *tokens):
    anywhere = pl.BlockSpec(memory_space=pl.ANY)
    return pl.pallas_call(
        gate_kernel,
        in_specs=[anywhere] * (1 + len(tokens)),
        out_specs=anywhere,
        out_shape=jax.ShapeDtypeStruct(value.shape, value.dtype),
        input_output_aliases={0: 0},
        name="gate",
    )(value, *tokens)


class Gather:
    def __init__(self, block):
        self.value = block
        self.bits = []
        self.pending = None

    def start(self, axis, bit):
        self.pending = (axis, bit, swap(self.value, axis, bit))
        return self.value

    def finish(self, after=()):
        axis, bit, other = self.pending
        rows, columns = self.value.shape
        lanes = axis == "mp"
        if lanes:
            shape, out = (rows, columns), (rows, 2 * columns)
        else:
            ahead = 2 ** sum(b > bit for b in self.bits)
            self.bits.append(bit)
            shape = (ahead, rows // ahead, columns)
            out = (ahead, 2, rows // ahead, columns)
        kernel, waits = run_after(lambda *refs: gather_kernel(lanes, *refs), 3, after)
        value = pl.pallas_call(
            kernel,
            in_specs=[SCALAR] + [FULL] * 2 + waits,
            out_specs=FULL,
            out_shape=jax.ShapeDtypeStruct(out, self.value.dtype),
            compiler_params=params(),
            cost_estimate=cost(0.1),
            name="gather_step",
        )(my_bit(axis, bit).reshape(1), self.value.reshape(shape), other.reshape(shape), *after)
        self.value = value.reshape(-1, value.shape[-1])
        return self.value

    def step(self, axis, bit, after=()):
        self.start(axis, bit)
        return self.finish(after)


def scatter_kernel(lanes, mine_ref, *refs):
    terms, (send_ref, keep_ref) = refs[:-2], refs[-2:]
    mine = mine_ref[0]
    for which, out_ref in ((1 - mine, send_ref), (mine, keep_ref)):
        if lanes:
            width = out_ref.shape[1]
            cols = pl.ds(pl.multiple_of(which * width, LANES), width)
            total = sum(term[:, cols].astype(f32) for term in terms)
            out_ref[...] = total.astype(out_ref.dtype)
        else:
            total = sum(term[0, which].astype(f32) for term in terms)
            out_ref[0] = total.astype(out_ref.dtype)


class Scatter:
    def __init__(self, *terms):
        self.bits = list(reversed(range(log_two(lax.axis_size("dp")))))
        self.terms = list(terms)
        self.send = None

    def step(self, axis, bit, kept_type=f32, after=()):
        rows, columns = self.terms[0].shape
        lanes = axis == "mp"
        if lanes:
            shape, half = (rows, columns), (rows, columns // 2)
            steps = max(rows // (LANES + CHUNK), 1)
            steps = next(k for k in range(steps, 0, -1) if rows % (k * CHUNK) == 0 or k == 1)
            block = lambda size: pl.BlockSpec((rows // steps, size[1]), lambda i: (i, 0))
        else:
            steps = 2 ** self.bits.index(bit)
            self.bits.remove(bit)
            shape = (steps, 2, rows // (2 * steps), columns)
            half = (steps, rows // (2 * steps), columns)
            block = lambda size: pl.BlockSpec(
                (1,) + size[1:], lambda i: (i,) + (0,) * (len(size) - 1)
            )
        count = len(self.terms)
        body_kernel = lambda *refs: scatter_kernel(lanes, *refs)
        kernel, waits = run_after(body_kernel, 1 + count, after)
        send, kept = pl.pallas_call(
            kernel,
            grid=(steps,),
            in_specs=[SCALAR] + [block(shape)] * count + waits,
            out_specs=[block(half)] * 2,
            out_shape=[jax.ShapeDtypeStruct(half, bf16), jax.ShapeDtypeStruct(half, kept_type)],
            compiler_params=params(),
            cost_estimate=cost(0.1),
            name="scatter_step",
        )(my_bit(axis, bit).reshape(1), *[term.reshape(shape) for term in self.terms], *after)
        flat = lambda value: value.reshape(-1, value.shape[-1])
        self.send = flat(send)
        self.terms = [flat(kept), swap(self.send, axis, bit)]
        return self.send

    def total(self):
        return sum(term.astype(f32) for term in self.terms)


def butterfly(value):
    for axis, bits in (("mp", 2), ("dp", log_two(lax.axis_size("dp")))):
        for bit in range(bits):
            value = value + swap(value, axis, bit)
    return value


def gelu_pair(value):
    square = value * value
    wave = jnp.tanh(value * (GELU_SCALE + (GELU_SCALE * GELU_CUBE) * square))
    half = 0.5 + 0.5 * wave
    inner = GELU_SCALE + (3.0 * GELU_SCALE * GELU_CUBE) * square
    return value * half, half + 0.5 * value * (1.0 - wave * wave) * inner


def norm_rows(x_ref, gain, shift, out_ref):
    @pl.loop(0, x_ref.shape[0] // CHUNK, unroll=13)
    def _(i):
        rows = pl.ds(pl.multiple_of(i * CHUNK, CHUNK), CHUNK)
        out_ref[rows, :] = layer_norm(x_ref[rows, :], gain, shift).astype(out_ref.dtype)


def norm_back_rows(x_ref, gain, grad_ref, extra_ref, out_ref, low_ref, sum_ref):
    sum_ref[...] = jnp.zeros_like(sum_ref)

    @pl.loop(0, x_ref.shape[0] // CHUNK, unroll=13)
    def _(i):
        rows = pl.ds(pl.multiple_of(i * CHUNK, CHUNK), CHUNK)
        value = x_ref[rows, :]
        grad = grad_ref[rows, :]
        center = value - jnp.mean(value, axis=-1, keepdims=True)
        scale = lax.rsqrt(jnp.mean(center * center, axis=-1, keepdims=True) + norm_eps)
        hat = center * scale
        for k, term in enumerate((grad * hat, grad)):
            sum_ref[8 * k : 8 * k + 8, :] += term[:8] + term[8:]
        pull = grad * gain
        mean_one = jnp.mean(pull, axis=-1, keepdims=True)
        mean_two = jnp.mean(pull * hat, axis=-1, keepdims=True)
        result = scale * (pull - mean_one - hat * mean_two)
        if extra_ref is not None:
            result = result + extra_ref[rows, :]
        out_ref[rows, :] = result
        low_ref[rows, :] = result.astype(bf16)


def gelu_blocks(width):
    return [slice(j, j + BLOCK) for j in range(0, width, BLOCK)]


def soft_rows(scores, column):
    scores = jnp.where(column < PATCHES, scores * HEAD_DIM ** (-0.5), -jnp.inf)
    top = jnp.max(scores, axis=-1, keepdims=True)
    weight = jnp.exp(scores - top)
    return weight * (1.0 / jnp.sum(weight, axis=-1, keepdims=True))


def enter_kernel(
    pixels_ref, stem_ref, embed_w_ref, token_ref, own_ref, other_ref,
    hidden_ref, slope_ref, embed_ref, normed_ref, tri_ref, ctx_ref,
):
    for cols in gelu_blocks(C_STEM):
        value, slope = gelu_pair(matmul(pixels_ref[...], stem_ref[:, cols]))
        hidden_ref[:, cols] = value.astype(bf16)
        slope_ref[:, cols] = slope.astype(bf16)
    slices = pixels_ref.shape[0] // PAD
    for cols in gelu_blocks(D):
        value = matmul(hidden_ref[...], embed_w_ref[:, cols])
        for s in range(slices):
            rows = slice(s * PAD, (s + 1) * PAD)
            embed_ref[rows, cols] = value[rows] + token_ref[:PAD, cols]
    gain, shift = token_ref[PATCHES : PATCHES + 1, :], token_ref[PATCHES + 1 : PATCHES + 2, :]
    norm_rows(embed_ref, gain, shift, normed_ref)
    width = tri_ref.shape[2]
    heads = width // (3 * HEAD_DIM)
    stride = width + width // 3
    column = lax.broadcasted_iota(jnp.int32, (PAD, PAD), 1)
    for p in range(tri_ref.shape[0]):
        start = (p % 2) * stride
        weight_ref = (own_ref, other_ref)[p // 2]
        tri_ref[p] = matmul(normed_ref[...], weight_ref[:, start : start + width]).astype(bf16)

    @pl.loop(0, tri_ref.shape[0])
    def _(p):
        for s in range(slices):
            rows = slice(s * PAD, (s + 1) * PAD)
            for h in range(heads):
                base = h * 3 * HEAD_DIM
                queries = tri_ref[p, rows, base : base + HEAD_DIM]
                keys_low = tri_ref[p, rows, base + HEAD_DIM : base + 2 * HEAD_DIM]
                values = tri_ref[p, rows, base + 2 * HEAD_DIM : base + 3 * HEAD_DIM]
                attend = soft_rows(matmul_t(queries, keys_low), column)
                context = matmul(attend.astype(bf16), values)
                ctx_ref[p, rows, h * HEAD_DIM : (h + 1) * HEAD_DIM] = context.astype(bf16)


def enter(pixels, stem_b, embed_b, tokens, attn_all, width):
    rows = pixels.shape[0]
    parts = 4
    return pl.pallas_call(
        enter_kernel,
        in_specs=[FULL] * 6,
        out_specs=[FULL] * 6,
        out_shape=[
            jax.ShapeDtypeStruct((rows, C_STEM), bf16),
            jax.ShapeDtypeStruct((rows, C_STEM), bf16),
            jax.ShapeDtypeStruct((rows, D), f32),
            jax.ShapeDtypeStruct((rows, D), bf16),
            jax.ShapeDtypeStruct((parts, rows, width), bf16),
            jax.ShapeDtypeStruct((parts, rows, width // 3), bf16),
        ],
        compiler_params=params(),
        cost_estimate=cost(20),
        name="enter",
    )(pixels, stem_b, embed_b, tokens, *attn_all)


def middle_kernel(
    ctx_ref, embed_ref, token_ref, own_ref, other_ref, mlp_ref,
    resid_ref, normed2_ref, slope_ref, inner_ref, resid2_ref, final_ref,
):
    p = pl.program_id(0)

    @pl.when(p == 0)
    def _():
        part = ctx_ref.shape[2]
        stride = 4 * part
        for q in range(ctx_ref.shape[0]):
            start = (q % 2) * stride + 3 * part
            weight_ref = (own_ref, other_ref)[q // 2]
            term = matmul_t(ctx_ref[q], weight_ref[:, start : start + part])
            if q == 0:
                resid_ref[...] = embed_ref[...] + term
            else:
                resid_ref[...] += term
        gain, shift = token_ref[PATCHES + 2 : PATCHES + 3, :], token_ref[PATCHES + 3 : PATCHES + 4, :]
        norm_rows(resid_ref, gain, shift, normed2_ref)
        resid2_ref[...] = resid_ref[...]

    each = mlp_ref.shape[2] // 2
    for cols in gelu_blocks(each):
        value, slope = gelu_pair(matmul(normed2_ref[...], mlp_ref[0, :, cols]))
        inner_ref[0, :, cols] = value.astype(bf16)
        slope_ref[0, :, cols] = slope.astype(bf16)
    resid2_ref[...] += matmul_t(inner_ref[0], mlp_ref[0, :, each:])

    @pl.when(p == pl.num_programs(0) - 1)
    def _():
        gain, shift = token_ref[PATCHES + 4 : PATCHES + 5, :], token_ref[PATCHES + 5 : PATCHES + 6, :]
        norm_rows(resid2_ref, gain, shift, final_ref)


def whole_of(value):
    return pl.BlockSpec(value.shape, lambda *_: (0,) * len(value.shape))


def part_of(value):
    rest = len(value.shape) - 1
    return pl.BlockSpec((1,) + tuple(value.shape[1:]), lambda i, *_: (i,) + (0,) * rest)


def middle(context, embed, tokens, attn_all, mlp_all):
    rows = embed.shape[0]
    parts, _, width = mlp_all.shape
    each = width // 2
    outs = [
        jax.ShapeDtypeStruct((rows, D), f32),
        jax.ShapeDtypeStruct((rows, D), bf16),
        jax.ShapeDtypeStruct((parts, rows, each), bf16),
        jax.ShapeDtypeStruct((parts, rows, each), bf16),
        jax.ShapeDtypeStruct((rows, D), f32),
        jax.ShapeDtypeStruct((rows, D), bf16),
    ]
    values = (context, embed, tokens, *attn_all)
    return pl.pallas_call(
        middle_kernel,
        grid=(parts,),
        in_specs=[whole_of(value) for value in values] + [part_of(mlp_all)],
        out_specs=[(part_of if len(out.shape) == 3 else whole_of)(out) for out in outs],
        out_shape=outs,
        compiler_params=params(),
        cost_estimate=cost(26),
        name="middle",
    )(*values, mlp_all)


def class_probs(logits_ref, rows, group):
    width = CLASSES * LANES
    values = [
        logits_ref[rows, group * width + c * LANES : group * width + (c + 1) * LANES]
        for c in range(CLASSES)
    ]
    top = values[0]
    for value in values[1:]:
        top = jnp.maximum(top, value)
    weights = [jnp.exp(value - top) for value in values]
    total = weights[0]
    for weight in weights[1:]:
        total = total + weight
    scale = 1.0 / total
    return values, [weight * scale for weight in weights], top + jnp.log(total)


SPLIT_A = 4 * CHAN_B
SPLIT_B = SPLIT_A + 16 * CHAN_C
SKIPW = SPLIT_B + 64 * CHAN_D


def leave_kernel(
    core_ref, hidden_ref, final_ref, skip_own_ref, skip_other_ref, dec_ref, one_ref, two_ref, three_ref, head_ref, label_ref,
    slope0_ref, level0_ref, slope_ref, level1_ref, level2_ref, level3_ref, logits_ref, stats_ref,
    skips,
):
    value, slope = gelu_pair(matmul(final_ref[...], dec_ref[...]))
    level0_ref[...] = value.astype(bf16)
    slope0_ref[...] = slope

    half = skip_own_ref.shape[1]
    core = core_ref[0]
    for which, weight_ref in ((core, skip_own_ref), (1 - core, skip_other_ref)):
        for j in range(0, half, BLOCK):
            cols = pl.ds(pl.multiple_of(which * half + j, LANES), BLOCK)
            skips[:, cols] = matmul(hidden_ref[...], weight_ref[:, j : j + BLOCK])

    def stage(source, weight, out_ref, cols, skip_cols):
        pre = matmul(source, weight) + skips[:, skip_cols : skip_cols + BLOCK]
        value, slope = gelu_pair(pre)
        out_ref[:, cols : cols + BLOCK] = value.astype(bf16)
        slope_ref[:, skip_cols : skip_cols + BLOCK] = slope.astype(bf16)

    for i in range(2):
        stage(level0_ref[...], one_ref[:, i * BLOCK : (i + 1) * BLOCK], level1_ref, i * BLOCK, i * BLOCK)
    for i in range(4):
        stage(
            level1_ref[:, i * CHAN_B : (i + 1) * CHAN_B], two_ref[...], level2_ref, i * BLOCK,
            SPLIT_A + i * BLOCK,
        )
    for i in range(4):
        stage(
            level2_ref[:, i * BLOCK : (i + 1) * BLOCK], three_ref[...], level3_ref, i * BLOCK,
            SPLIT_B + i * BLOCK,
        )
    inner = head_ref.shape[0]
    width = head_ref.shape[1]
    groups = level3_ref.shape[1] // inner
    for g in range(groups):
        logits_ref[:, g * width : (g + 1) * width] = matmul(
            level3_ref[:, g * inner : (g + 1) * inner], head_ref[...]
        )
    stats_ref[...] = jnp.zeros_like(stats_ref)
    slices = stats_ref.shape[0]
    per_slice = PAD // CHUNK

    @pl.loop(0, slices)
    def _(s):
        @pl.loop(0, per_slice)
        def _(i):
            start = pl.multiple_of(s * PAD + i * CHUNK, CHUNK)
            rows = pl.ds(start, CHUNK)
            row_id = lax.broadcasted_iota(jnp.int32, (CHUNK, LANES), 0) + i * CHUNK
            inside = (row_id < PATCHES).astype(f32)
            for g in range(groups):
                values, probs, log_total = class_probs(logits_ref, rows, g)
                label = label_ref[rows, g * LANES : (g + 1) * LANES]
                cross = jnp.zeros((CHUNK, LANES), f32)
                for c in range(CLASSES):
                    hot = (label == c).astype(f32)
                    cross = cross + hot * (log_total - values[c])
                    for k, term in enumerate((hot * probs[c], inside * probs[c], hot)):
                        spot = 8 * (3 * c + k)
                        stats_ref[s, spot : spot + 8, :] += term[:8] + term[8:]
                spot = 8 * 3 * CLASSES
                stats_ref[s, spot : spot + 8, :] += cross[:8] + cross[8:]


def leave(core, hidden, final_low, skip_all, dec_b, one_b, two_b, three_four, big_head, labels):
    rows = hidden.shape[0]
    slices = rows // PAD
    stat_rows = 8 * (3 * CLASSES + 1)
    return pl.pallas_call(
        leave_kernel,
        in_specs=[SCALAR] + [FULL] * 10,
        out_specs=[FULL] * 8,
        out_shape=[
            jax.ShapeDtypeStruct((rows, CHAN_A), f32),
            jax.ShapeDtypeStruct((rows, CHAN_A), bf16),
            jax.ShapeDtypeStruct((rows, SKIPW), bf16),
            jax.ShapeDtypeStruct((rows, 4 * CHAN_B), bf16),
            jax.ShapeDtypeStruct((rows, 16 * CHAN_C), bf16),
            jax.ShapeDtypeStruct((rows, 64 * CHAN_D), bf16),
            jax.ShapeDtypeStruct((rows, CLASSES * PIXELS), f32),
            jax.ShapeDtypeStruct((slices, stat_rows, LANES), f32),
        ],
        scratch_shapes=[pltpu.VMEM((rows, SKIPW), f32)],
        compiler_params=params(),
        cost_estimate=cost(16),
        name="leave",
    )(core, hidden, final_low, *skip_all, dec_b, one_b, two_b, three_four, big_head, labels)


def leave_back_kernel(
    coef_ref, logits_ref, label_ref, slope_ref, head_ref, three_ref, two_ref,
    g_logits_ref, g_skips_ref,
):
    inner = head_ref.shape[0]
    width = head_ref.shape[1]
    groups = 64 * CHAN_D // inner
    slices = logits_ref.shape[0] // PAD

    @pl.loop(0, slices)
    def _(s):
        cross_scale = coef_ref[s, 2 * CLASSES]

        @pl.loop(0, PAD // CHUNK)
        def _(i):
            start = pl.multiple_of(s * PAD + i * CHUNK, CHUNK)
            rows = pl.ds(start, CHUNK)
            row_id = lax.broadcasted_iota(jnp.int32, (CHUNK, LANES), 0) + i * CHUNK
            inside = (row_id < PATCHES).astype(f32)
            for g in range(groups):
                _, probs, _ = class_probs(logits_ref, rows, g)
                label = label_ref[rows, g * LANES : (g + 1) * LANES]
                mean = jnp.zeros((CHUNK, LANES), f32)
                pulls = []
                for c in range(CLASSES):
                    pull = jnp.where(label == c, coef_ref[s, c], 0.0) + coef_ref[s, CLASSES + c]
                    pulls.append(pull)
                    mean = mean + probs[c] * pull
                mean = mean - cross_scale
                for c in range(CLASSES):
                    grad = probs[c] * (pulls[c] - mean)
                    grad = grad - jnp.where(label == c, cross_scale, 0.0)
                    spot = g * width + c * LANES
                    g_logits_ref[rows, spot : spot + LANES] = (grad * inside).astype(bf16)

    for i in range(4):
        g, part = (i * BLOCK) // inner, (i * BLOCK) % inner
        grad = matmul_t(g_logits_ref[:, g * width : (g + 1) * width], head_ref[part : part + BLOCK, :])
        cols = slice(SPLIT_B + i * BLOCK, SPLIT_B + (i + 1) * BLOCK)
        g_skips_ref[:, cols] = (grad * slope_ref[:, cols].astype(f32)).astype(bf16)
    for i in range(4):
        source = g_skips_ref[:, SPLIT_B + i * BLOCK : SPLIT_B + (i + 1) * BLOCK]
        cols = slice(SPLIT_A + i * BLOCK, SPLIT_A + (i + 1) * BLOCK)
        g_skips_ref[:, cols] = (matmul_t(source, three_ref[...]) * slope_ref[:, cols].astype(f32)).astype(bf16)
    for i in range(4):
        source = g_skips_ref[:, SPLIT_A + i * BLOCK : SPLIT_A + (i + 1) * BLOCK]
        cols = slice(i * CHAN_B, (i + 1) * CHAN_B)
        g_skips_ref[:, cols] = (matmul_t(source, two_ref[...]) * slope_ref[:, cols].astype(f32)).astype(bf16)


def leave_back(coef, logits, labels, slope, big_head, three_four, two_b):
    rows = logits.shape[0]
    return pl.pallas_call(
        leave_back_kernel,
        in_specs=[SCALAR] + [FULL] * 6,
        out_specs=[FULL] * 2,
        out_shape=[
            jax.ShapeDtypeStruct((rows, CLASSES * PIXELS), bf16),
            jax.ShapeDtypeStruct((rows, SKIPW), bf16),
        ],
        compiler_params=params(),
        cost_estimate=cost(10),
        name="leave_back",
    )(coef, logits, labels, slope, big_head, three_four, two_b)


def skip_grad_kernel(core_ref, hidden_ref, g_skips_ref, send_ref, keep_ref):
    half = send_ref.shape[1]
    core = core_ref[0]
    for which, out_ref in ((1 - core, send_ref), (core, keep_ref)):
        for j in range(0, half, half // 2):
            cols = pl.ds(pl.multiple_of(which * half + j, LANES), half // 2)
            out_ref[:, j : j + half // 2] = t_matmul(hidden_ref[...], g_skips_ref[:, cols]).astype(
                bf16
            )


def skip_grad(core, hidden, g_skips):
    shape = (hidden.shape[1], g_skips.shape[1] // 2)
    return pl.pallas_call(
        skip_grad_kernel,
        in_specs=[SCALAR] + [FULL] * 2,
        out_specs=[FULL] * 2,
        out_shape=[jax.ShapeDtypeStruct(shape, bf16)] * 2,
        compiler_params=params(),
        cost_estimate=cost(6),
        name="skip_grad",
    )(core, hidden, g_skips)


def turn_kernel(
    g_skips_ref, one_ref, slope0_ref, dec_ref, resid2_ref, token_ref,
    g_pre0_ref, g_resid2_ref, low_ref, sums_ref, g_final,
):
    grad = matmul_t(g_skips_ref[:, :SPLIT_A], one_ref[...])
    g_pre0_ref[...] = (grad * slope0_ref[...]).astype(bf16)
    g_final[...] = matmul_t(g_pre0_ref[...], dec_ref[...])
    norm_back_rows(
        resid2_ref, token_ref[PATCHES + 4 : PATCHES + 5, :], g_final, None, g_resid2_ref, low_ref, sums_ref
    )


def turn(g_skips, one_b, slope0, dec_b, resid2, tokens, after=()):
    rows = resid2.shape[0]
    kernel, waits = run_after(turn_kernel, 6, after)
    return pl.pallas_call(
        kernel,
        in_specs=[FULL] * 6 + waits,
        out_specs=[FULL] * 4,
        out_shape=[
            jax.ShapeDtypeStruct((rows, CHAN_A), bf16),
            jax.ShapeDtypeStruct((rows, D), f32),
            jax.ShapeDtypeStruct((rows, D), bf16),
            jax.ShapeDtypeStruct((16, D), f32),
        ],
        scratch_shapes=[pltpu.VMEM((rows, D), f32)],
        compiler_params=params(),
        cost_estimate=cost(11),
        name="turn",
    )(g_skips, one_b, slope0, dec_b, resid2, tokens, *after)


FLAT_DEC = D * CHAN_A // LANES
FLAT_ONE = FLAT_DEC + CHAN_A * 4 * CHAN_B // LANES
FLAT_TWO = FLAT_ONE + CHAN_B * 4 * CHAN_C // LANES
FLAT_THREE = FLAT_TWO + CHAN_C * 4 * CHAN_D // LANES


def decoder_grad_kernel(
    level3_ref, g_logits_ref, level2_ref, level1_ref, g_skips_ref, level0_ref, final_ref, g_pre0_ref,
    out_ref, flat_ref, square_ref,
):
    size = out_ref.shape[1]
    flat = (FLAT_THREE * LANES + 4 * CLASSES * CHAN_D) // size
    inner, width = GROUP * CHAN_D, CLASSES * LANES
    tail = flat_ref.shape[0] - FLAT_THREE
    flat_ref[FLAT_THREE:, :] = jnp.zeros((tail, LANES), f32)

    def spread(value, base, count):
        for j in range(count):
            flat_ref[pl.ds(base + j, value.shape[0], stride=count), :] = value[
                :, j * LANES : (j + 1) * LANES
            ]

    spread(t_matmul(final_ref[...], g_pre0_ref[...]), 0, CHAN_A // LANES)
    spread(t_matmul(level0_ref[...], g_skips_ref[:, :SPLIT_A]), FLAT_DEC, SPLIT_A // LANES)
    three = jnp.zeros((CHAN_C, 4 * CHAN_D), f32)
    two = jnp.zeros((CHAN_B, 4 * CHAN_C), f32)
    for i in range(4):
        big = t_matmul(
            level2_ref[:, i * BLOCK : (i + 1) * BLOCK],
            g_skips_ref[:, SPLIT_B + i * BLOCK : SPLIT_B + (i + 1) * BLOCK],
        )
        for k in range(4):
            at = slice(k * CHAN_C, (k + 1) * CHAN_C)
            three += big[at, at]
        two += t_matmul(
            level1_ref[:, i * CHAN_B : (i + 1) * CHAN_B],
            g_skips_ref[:, SPLIT_A + i * BLOCK : SPLIT_A + (i + 1) * BLOCK],
        )
    spread(two, FLAT_ONE, 4 * CHAN_C // LANES)
    square_ref[...] = three
    flat_ref[FLAT_TWO:FLAT_THREE, :] = jnp.concatenate(
        [square_ref[pl.ds(j, CHAN_C // 2, stride=2), :] for j in range(2)], axis=1
    )
    head = jnp.zeros((CHAN_D, width), f32)
    row = lax.broadcasted_iota(jnp.int32, (CHAN_D, width), 0)
    across = lax.broadcasted_iota(jnp.int32, (CHAN_D, width), 1)
    parent = (across // 4) % GROUP
    for g in range(level3_ref.shape[1] // inner):
        big = t_matmul(
            level3_ref[:, g * inner : (g + 1) * inner], g_logits_ref[:, g * width : (g + 1) * width]
        )
        for k in range(GROUP):
            head += jnp.where(parent == k, big[k * CHAN_D : (k + 1) * CHAN_D, :], 0.0)
    column = lax.broadcasted_iota(jnp.int32, (width, LANES), 0)
    target = lax.broadcasted_iota(jnp.int32, (width, LANES), 1)
    pick = target == (column % 4) * CLASSES + column // (GROUP * 4)
    small = jnp.dot(head, pick.astype(f32), precision=highest, preferred_element_type=f32)
    lane = lax.broadcasted_iota(jnp.int32, (1, LANES), 1)
    lines = [jnp.zeros((1, LANES), f32) for _ in range(8)]
    for k in range(CHAN_D):
        line, start = divmod(k * 4 * CLASSES, LANES)
        value = small[k : k + 1, :]
        if start:
            value = pltpu.roll(value, start, 1)
        lines[line] = lines[line] + jnp.where(lane >= start, value, 0.0)
        if start + 4 * CLASSES > LANES:
            lines[line + 1] = lines[line + 1] + jnp.where(
                lane < start + 4 * CLASSES - LANES, value, 0.0
            )
    flat_ref[FLAT_THREE : FLAT_THREE + 8, :] = jnp.concatenate(lines, axis=0)

    rows = out_ref.shape[2]
    line_id = lax.broadcasted_iota(jnp.int32, (rows, LANES), 0)
    lane_id = lax.broadcasted_iota(jnp.int32, (rows, LANES), 1)
    for d in range(size):
        for c in range(2):
            first, start = divmod(d * flat + c * rows * LANES, LANES)
            value = flat_ref[first : first + rows, :]
            if start:
                after = flat_ref[first + 1 : first + 1 + rows, :]
                value = jnp.where(
                    lane_id < LANES - start,
                    pltpu.roll(value, LANES - start, 1),
                    pltpu.roll(after, LANES - start, 1),
                )
            inside = (line_id + c * rows) * LANES + lane_id < flat
            out_ref[c, d] = jnp.where(inside, value, 0.0).astype(bf16)


def decoder_grad(
    level3, g_logits, level2, level1, g_skips, level0, final_low, g_pre0, size, rows, after=()
):
    kernel, waits = run_after(decoder_grad_kernel, 8, after)
    flat = (FLAT_THREE * LANES + 4 * CLASSES * CHAN_D) // size
    lines = (size - 1) * flat // LANES + 2 * rows + 8
    lines = -(-max(lines, FLAT_THREE + 8) // 8) * 8
    return pl.pallas_call(
        kernel,
        in_specs=[FULL] * 8 + waits,
        out_specs=FULL,
        out_shape=jax.ShapeDtypeStruct((2, size, rows, LANES), bf16),
        scratch_shapes=[pltpu.VMEM((lines, LANES), f32), pltpu.VMEM((CHAN_C, 4 * CHAN_D), f32)],
        compiler_params=params(),
        cost_estimate=cost(7),
        name="decoder_grad",
    )(level3, g_logits, level2, level1, g_skips, level0, final_low, g_pre0, *after)


def first_grad_kernel(
    core_ref, pixels_ref, g_stem_ref, hidden_ref, low_ref, pos_ref, sums1_ref, sums2_ref, sumsf_ref,
    dec_ref, send_ref, keep_ref, token_ref,
):
    core = core_ref[0]
    size = send_ref.shape[0]
    stem_rows, embed_rows, token_rows = PIXELS // size, C_STEM // size, D // size
    token_ref[...] = jnp.zeros_like(token_ref)
    token_ref[:PATCHES, :] = pos_ref[:PATCHES, :]
    for i, sums_ref in enumerate((sums1_ref, sums2_ref, sumsf_ref)):
        for k in range(2):
            at = PATCHES + 2 * i + k
            token_ref[at : at + 1, :] = jnp.sum(
                sums_ref[8 * k : 8 * k + 8, :], axis=0, keepdims=True
            )
    for which, out_ref in ((1 - core, send_ref), (core, keep_ref)):
        spot = 0
        half = C_STEM // 2
        for j in range(0, half, BLOCK):
            cols = pl.ds(pl.multiple_of(which * half + j, LANES), BLOCK)
            part = t_matmul(pixels_ref[...], g_stem_ref[:, cols]).astype(bf16)
            for k in range(0, BLOCK, LANES):
                for d in range(size):
                    out_ref[d, spot : spot + stem_rows, :] = part[
                        d * stem_rows : (d + 1) * stem_rows, k : k + LANES
                    ]
                spot += stem_rows
        half = D // 2
        cols = pl.ds(pl.multiple_of(which * half, LANES), half)
        part = t_matmul(hidden_ref[...], low_ref[:, cols]).astype(bf16)
        for k in range(0, half, LANES):
            for d in range(size):
                out_ref[d, spot : spot + embed_rows, :] = part[
                    d * embed_rows : (d + 1) * embed_rows, k : k + LANES
                ]
            spot += embed_rows
        turned = token_ref[pl.ds(pl.multiple_of(which * LANES, LANES), LANES), :].T.astype(bf16)
        for d in range(size):
            out_ref[d, spot : spot + token_rows, :] = turned[d * token_rows : (d + 1) * token_rows]
            out_ref[d, spot + token_rows :, :] = dec_ref[which, d]


def first_grad(core, pixels, g_stem, hidden, low, pos, sums1, sums2, sumsf, dec, rows, after=()):
    kernel, waits = run_after(first_grad_kernel, 10, after)
    shape = (dec.shape[1], rows, LANES)
    return pl.pallas_call(
        kernel,
        in_specs=[SCALAR] + [FULL] * 9 + waits,
        out_specs=[FULL] * 2,
        out_shape=[jax.ShapeDtypeStruct(shape, bf16)] * 2,
        scratch_shapes=[pltpu.VMEM((2 * LANES, D), f32)],
        compiler_params=params(),
        cost_estimate=cost(6),
        name="first_grad",
    )(core, pixels, g_stem, hidden, low, pos, sums1, sums2, sumsf, dec, *after)


def unpack_kernel(core_ref, own_ref, other_ref, stem_ref, embed_ref, token_ref, turned_ref):
    core = core_ref[0]
    size = own_ref.shape[0]
    stem_rows, embed_rows, token_rows = PIXELS // size, C_STEM // size, D // size
    for which, block_ref in ((core, own_ref), (1 - core, other_ref)):
        spot = 0
        for target_ref, rows, half in (
            (stem_ref, stem_rows, C_STEM // 2),
            (embed_ref, embed_rows, D // 2),
            (turned_ref, token_rows, LANES),
        ):
            for k in range(0, half, LANES):
                cols = pl.ds(pl.multiple_of(which * half + k, LANES), LANES)
                for d in range(size):
                    target_ref[d * rows : (d + 1) * rows, cols] = block_ref[
                        d, spot : spot + rows, :
                    ].astype(target_ref.dtype)
                spot += rows
    token_ref[...] = turned_ref[...].T


def unpack(core, own, other):
    return pl.pallas_call(
        unpack_kernel,
        in_specs=[SCALAR] + [FULL] * 2,
        out_specs=[FULL] * 3,
        out_shape=[
            jax.ShapeDtypeStruct((PIXELS, C_STEM), bf16),
            jax.ShapeDtypeStruct((C_STEM, D), bf16),
            jax.ShapeDtypeStruct((2 * LANES, D), f32),
        ],
        scratch_shapes=[pltpu.VMEM((D, 2 * LANES), f32)],
        compiler_params=params(),
        cost_estimate=cost(4),
        name="unpack",
    )(core, own, other)


def pack_kernel(core_ref, stem_ref, embed_ref, token_ref, dec_ref, out_ref):
    core = core_ref[0]
    spot = 0
    for source_ref in (stem_ref, embed_ref, token_ref):
        rows, half = source_ref.shape[0], source_ref.shape[1] // 2
        for k in range(0, half, LANES):
            cols = pl.ds(pl.multiple_of(core * half + k, LANES), LANES)
            out_ref[spot : spot + rows, :] = source_ref[:, cols].astype(bf16)
            spot += rows
    out_ref[spot:, :] = dec_ref[core].astype(bf16)


def pack(core, stem_w, embed_w, token_t, dec, rows):
    return pl.pallas_call(
        pack_kernel,
        in_specs=[SCALAR] + [FULL] * 4,
        out_specs=FULL,
        out_shape=jax.ShapeDtypeStruct((rows, LANES), bf16),
        compiler_params=params(),
        cost_estimate=cost(2),
        name="pack",
    )(core, stem_w, embed_w, token_t, dec)


def middle_back_kernel(
    low2_ref, mlp_ref, slope_ref, resid_ref, token_ref, g_resid2_ref, own_ref, other_ref,
    g_pre_ref, g_resid_ref, low_ref, g_ctx_ref, sums_ref, g_normed,
):
    p = pl.program_id(0)
    each = mlp_ref.shape[2] // 2
    for cols in gelu_blocks(each):
        down = mlp_ref[0, :, each + cols.start : each + cols.stop]
        grad = matmul(low2_ref[...], down) * slope_ref[0, :, cols].astype(f32)
        g_pre_ref[0, :, cols] = grad.astype(bf16)
    term = matmul_t(g_pre_ref[0], mlp_ref[0, :, :each])

    @pl.when(p == 0)
    def _():
        g_normed[...] = term

    @pl.when(p > 0)
    def _():
        g_normed[...] += term

    @pl.when(p == pl.num_programs(0) - 1)
    def _():
        norm_back_rows(
            resid_ref, token_ref[PATCHES + 2 : PATCHES + 3, :], g_normed, g_resid2_ref,
            g_resid_ref, low_ref, sums_ref,
        )
        part = g_ctx_ref.shape[2]
        for q in range(g_ctx_ref.shape[0]):
            start = (q % 2) * 4 * part + 3 * part
            weight_ref = (own_ref, other_ref)[q // 2]
            g_ctx_ref[q] = matmul(low_ref[...], weight_ref[:, start : start + part]).astype(bf16)


def middle_back(low2, mlp_all, slope, resid, tokens, g_resid2, attn_all, after=()):
    kernel, waits = run_after(middle_back_kernel, 8, after)
    rows = resid.shape[0]
    parts, _, each = slope.shape
    part = attn_all[0].shape[1] // 8
    outs = [
        jax.ShapeDtypeStruct((parts, rows, each), bf16),
        jax.ShapeDtypeStruct((rows, D), f32),
        jax.ShapeDtypeStruct((rows, D), bf16),
        jax.ShapeDtypeStruct((parts, rows, part), bf16),
        jax.ShapeDtypeStruct((16, D), f32),
    ]
    values = (resid, tokens, g_resid2, *attn_all)
    return pl.pallas_call(
        kernel,
        grid=(parts,),
        in_specs=[whole_of(low2), part_of(mlp_all), part_of(slope)]
        + [whole_of(value) for value in values]
        + waits,
        out_specs=[part_of(outs[0])] + [whole_of(out) for out in outs[1:]],
        out_shape=outs,
        scratch_shapes=[pltpu.VMEM((rows, D), f32)],
        compiler_params=params(),
        cost_estimate=cost(21),
        name="middle_back",
    )(low2, mlp_all, slope, *values, *after)


def half_grad_kernel(core_ref, left_ref, right_ref, send_ref, keep_ref):
    core = core_ref[0]
    each = right_ref.shape[2]
    for which, out_ref in ((1 - core, send_ref), (core, keep_ref)):
        for x in range(2):
            out_ref[:, x * each : (x + 1) * each] = t_matmul(
                left_ref[...], right_ref[2 * x + which]
            ).astype(bf16)


def half_grad(core, left, right, after=()):
    kernel, waits = run_after(half_grad_kernel, 3, after)
    shape = (left.shape[1], 2 * right.shape[2])
    return pl.pallas_call(
        kernel,
        in_specs=[SCALAR] + [FULL] * 2 + waits,
        out_specs=[FULL] * 2,
        out_shape=[jax.ShapeDtypeStruct(shape, bf16)] * 2,
        compiler_params=params(),
        cost_estimate=cost(6),
        name="half_grad",
    )(core, left, right, *after)


def attn_back_kernel(tri_ref, g_ctx_ref, g_tri_ref):
    slices = tri_ref.shape[1] // PAD
    heads = tri_ref.shape[2] // (3 * HEAD_DIM)
    column = lax.broadcasted_iota(jnp.int32, (PAD, PAD), 1)
    for s in range(slices):
        rows = slice(s * PAD, (s + 1) * PAD)
        for h in range(heads):
            base = h * 3 * HEAD_DIM
            queries = tri_ref[0, rows, base : base + HEAD_DIM]
            keys_low = tri_ref[0, rows, base + HEAD_DIM : base + 2 * HEAD_DIM]
            values = tri_ref[0, rows, base + 2 * HEAD_DIM : base + 3 * HEAD_DIM]
            gctx = g_ctx_ref[0, rows, h * HEAD_DIM : (h + 1) * HEAD_DIM]
            attend = soft_rows(matmul_t(queries, keys_low), column)
            g_attend = matmul_t(gctx, values)
            g_values = t_matmul(attend.astype(bf16), gctx)
            inner = jnp.sum(attend * g_attend, axis=-1, keepdims=True)
            g_scores = attend * (g_attend - inner) * HEAD_DIM ** (-0.5)
            g_low = g_scores.astype(bf16)
            g_tri_ref[0, rows, base : base + HEAD_DIM] = matmul(g_low, keys_low).astype(bf16)
            g_tri_ref[0, rows, base + HEAD_DIM : base + 2 * HEAD_DIM] = t_matmul(
                g_low, queries
            ).astype(bf16)
            g_tri_ref[0, rows, base + 2 * HEAD_DIM : base + 3 * HEAD_DIM] = g_values.astype(bf16)


def attn_back(triple, g_ctx, after=()):
    parts, rows, width = triple.shape
    whole = lambda size: pl.BlockSpec((1, rows, size), lambda i: (i, 0, 0))
    kernel, waits = run_after(attn_back_kernel, 2, after)
    return pl.pallas_call(
        kernel,
        grid=(parts,),
        in_specs=[whole(width), whole(width // 3)] + waits,
        out_specs=whole(width),
        out_shape=jax.ShapeDtypeStruct(triple.shape, bf16),
        compiler_params=params(),
        cost_estimate=cost(15),
        name="attn_back",
    )(triple, g_ctx, *after)


def attn_grad_kernel(normed_ref, g_tri_ref, low_ref, ctx_ref, send_ref, keep_ref):
    width = g_tri_ref.shape[2]
    stride = width + width // 3
    for which, out_ref in ((1, send_ref), (0, keep_ref)):
        for x in range(2):
            part = 2 * which + x
            at = x * stride
            out_ref[:, at : at + width] = t_matmul(normed_ref[...], g_tri_ref[part]).astype(
                out_ref.dtype
            )
            out_ref[:, at + width : at + stride] = t_matmul(low_ref[...], ctx_ref[part]).astype(
                out_ref.dtype
            )


def attn_grad(normed, g_tri, low, context, after=()):
    shape = (D, 2 * (g_tri.shape[2] + context.shape[2]))
    kernel, waits = run_after(attn_grad_kernel, 4, after)
    return pl.pallas_call(
        kernel,
        in_specs=[FULL] * 4 + waits,
        out_specs=[FULL] * 2,
        out_shape=[jax.ShapeDtypeStruct(shape, bf16)] * 2,
        compiler_params=params(),
        cost_estimate=cost(7),
        name="attn_grad",
    )(normed, g_tri, low, context, *after)


def enter_back_kernel(
    core_ref, g_tri_ref, own_ref, other_ref, embed_ref, token_ref, g_resid_ref, embed_w_ref,
    g_skips_ref, skip_own_ref, skip_other_ref, slope_ref, low_ref, g_stem_ref, g_pos_ref, sums_ref, g_normed, g_embed,
):
    width = g_tri_ref.shape[2]
    stride = width + width // 3
    for p in range(g_tri_ref.shape[0]):
        start = (p % 2) * stride
        weight_ref = (own_ref, other_ref)[p // 2]
        term = matmul_t(g_tri_ref[p], weight_ref[:, start : start + width])
        if p == 0:
            g_normed[...] = term
        else:
            g_normed[...] += term
    norm_back_rows(
        embed_ref, token_ref[PATCHES : PATCHES + 1, :], g_normed, g_resid_ref, g_embed, low_ref, sums_ref
    )
    pos = g_embed[:PAD, :]
    for s in range(1, embed_ref.shape[0] // PAD):
        pos = pos + g_embed[s * PAD : (s + 1) * PAD, :]
    g_pos_ref[...] = pos
    half = skip_own_ref.shape[1]
    core = core_ref[0]
    for cols in gelu_blocks(C_STEM):
        grad = matmul_t(low_ref[...], embed_w_ref[cols, :])
        for which, weight_ref in ((core, skip_own_ref), (1 - core, skip_other_ref)):
            part = pl.ds(pl.multiple_of(which * half, LANES), half)
            grad += matmul_t(g_skips_ref[:, part], weight_ref[cols, :])
        g_stem_ref[:, cols] = (grad * slope_ref[:, cols].astype(f32)).astype(bf16)


def enter_back(core, g_tri, attn_all, embed, tokens, g_resid, embed_b, g_skips, skip_all, slope, after=()):
    rows = embed.shape[0]
    kernel, waits = run_after(enter_back_kernel, 12, after)
    return pl.pallas_call(
        kernel,
        in_specs=[SCALAR] + [FULL] * 11 + waits,
        out_specs=[FULL] * 4,
        out_shape=[
            jax.ShapeDtypeStruct((rows, D), bf16),
            jax.ShapeDtypeStruct((rows, C_STEM), bf16),
            jax.ShapeDtypeStruct((PAD, D), f32),
            jax.ShapeDtypeStruct((16, D), f32),
        ],
        scratch_shapes=[pltpu.VMEM((rows, D), f32), pltpu.VMEM((rows, D), f32)],
        compiler_params=params(),
        cost_estimate=cost(21),
        name="enter_back",
    )(core, g_tri, *attn_all, embed, tokens, g_resid, embed_b, g_skips, *skip_all, slope, *after)


def split_decoder(flat):
    edge_one = D * CHAN_A
    edge_two = edge_one + CHAN_A * 4 * CHAN_B
    edge_three = edge_two + CHAN_B * 4 * CHAN_C
    edge_four = edge_three + CHAN_C * 4 * CHAN_D
    return (
        flat[:edge_one].reshape(D, CHAN_A),
        flat[edge_one:edge_two].reshape(CHAN_A, 4 * CHAN_B),
        flat[edge_two:edge_three].reshape(CHAN_B, 4 * CHAN_C),
        flat[edge_three:edge_four].reshape(CHAN_C, 4 * CHAN_D),
        flat[edge_four:].reshape(CHAN_D, 4 * CLASSES),
    )


def same_block(rows, columns, inner, outer):
    row = lax.broadcasted_iota(jnp.int32, (rows, columns), 0) // inner
    column = lax.broadcasted_iota(jnp.int32, (rows, columns), 1) // outer
    return row == column


def block_diag(weight, parents):
    inner, outer = weight.shape
    mask = same_block(parents * inner, parents * outer, inner, outer)
    tiled = jnp.tile(weight, (parents, parents))
    return jnp.where(mask, tiled, jnp.zeros_like(tiled))


def head_masks():
    wide = CLASSES * GROUP * 4
    column = lax.broadcasted_iota(jnp.int32, (4 * CLASSES, wide), 1)
    source = lax.broadcasted_iota(jnp.int32, (4 * CLASSES, wide), 0)
    pick = source == (column % 4) * CLASSES + column // (GROUP * 4)
    row = lax.broadcasted_iota(jnp.int32, (GROUP * CHAN_D, wide), 0)
    across = lax.broadcasted_iota(jnp.int32, (GROUP * CHAN_D, wide), 1)
    mask = row // CHAN_D == (across // 4) % GROUP
    return pick, mask


def big_head_of(head_b):
    pick, mask = head_masks()
    spread = matmul(head_b, pick.astype(bf16)).astype(bf16)
    tiled = jnp.tile(spread, (GROUP, 1))
    return jnp.where(mask, tiled, jnp.zeros_like(tiled))


def stack_columns(value, width):
    count = value.shape[-1] // width
    return jnp.concatenate(
        [value[..., i * width : (i + 1) * width] for i in range(count)], axis=-2
    )


def unstack_columns(value, count):
    rows = value.shape[-2] // count
    return jnp.concatenate(
        [value[..., i * rows : (i + 1) * rows, :] for i in range(count)], axis=-1
    )


def pad_to(value, axis, size):
    widths = [(0, 0)] * value.ndim
    widths[axis] = (0, size - value.shape[axis])
    return jnp.pad(value, widths)


class Shared:
    def __init__(self, stem_w, embed_w, token_params, decoder_w):
        self.stem_rows = stem_w.shape[0]
        self.embed_rows = embed_w.shape[0]
        self.token_rows = token_params.shape[1]
        self.flat = decoder_w.shape[0]
        self.flat_rows = -(-self.flat // (2 * LANES * 16)) * 16
        self.stem_count = C_STEM // 2 // LANES
        self.embed_count = D // 2 // LANES
        self.cuts = [0]
        for rows in (
            self.stem_rows * self.stem_count,
            self.embed_rows * self.embed_count,
            self.token_rows,
            self.flat_rows,
        ):
            self.cuts.append(self.cuts[-1] + rows)

    def half_flat(self, flat):
        padded = pad_to(flat, flat.ndim - 1, 2 * self.flat_rows * LANES)
        return padded.reshape(flat.shape[:-1] + (2, self.flat_rows, LANES))

    def pieces(self, value):
        one, two, three, four = (
            value[..., a:b, :] for a, b in zip(self.cuts[:-1], self.cuts[1:], strict=True)
        )
        return (
            unstack_columns(one, self.stem_count),
            unstack_columns(two, self.embed_count),
            three,
            four,
        )


def half_columns(value, core, axis=-1):
    axis = axis % value.ndim
    size = value.shape[axis] // 2
    return lax.dynamic_slice_in_dim(value, core * size, size, axis)


def adamw(weight, grad, first, second, rate):
    first_new = beta_one * first + (1.0 - beta_one) * grad
    second_new = beta_two * second + (1.0 - beta_two) * grad * grad
    first_hat = first_new / (1.0 - beta_one**STEP)
    second_hat = second_new / (1.0 - beta_two**STEP)
    new_weight = weight - rate * (
        first_hat / (jnp.sqrt(second_hat) + adam_eps) + decay_rate * weight
    )
    return (new_weight, first_new, second_new)


def body(
    images,
    labels,
    background,
    patients,
    *state,
):
    masters, firsts, seconds = state[:9], state[9:18], state[18:]
    stem_w, embed_w, token_params, qkv_w, out_w, mlp_in_w, mlp_out_w, skip_w, decoder_w = masters
    n_dp = lax.axis_size("dp")
    n_mp = lax.axis_size("mp")
    mp_id = lax.axis_index("mp")
    core = mp_id & 1
    slices = images.shape[0] // n_mp
    rows = slices * PAD
    shared = Shared(stem_w, embed_w, token_params, decoder_w)
    attn_cut = qkv_w.shape[1]

    core_id = core.reshape(1)
    token_t = pad_to(token_params.T, 1, 2 * LANES)
    aligned = shared.stem_rows % 16 == 0 and shared.token_rows % 16 == 0
    mlp_block = jnp.concatenate([mlp_in_w, mlp_out_w.T], axis=1).astype(bf16)
    mlp_all = lax.all_gather(mlp_block, ("mp", "dp"), axis=0, tiled=True).reshape(n_mp, D, -1)
    if aligned:
        first_block = pack(
            core_id, stem_w, embed_w, token_t, shared.half_flat(decoder_w), shared.cuts[-1]
        )
    else:
        dec_half = lax.dynamic_index_in_dim(shared.half_flat(decoder_w), core, 0, keepdims=False)
        first_block = jnp.concatenate(
            [
                stack_columns(half_columns(stem_w, core), LANES),
                stack_columns(half_columns(embed_w, core), LANES),
                half_columns(token_t, core),
                dec_half,
            ],
            axis=0,
        ).astype(bf16)
    attn_block = jnp.concatenate([qkv_w, out_w.T], axis=1).astype(bf16)
    skip_block = half_columns(skip_w, core).astype(bf16)

    first, split, skip = Gather(first_block), Gather(attn_block), Gather(skip_block)
    order = list(reversed(range(log_two(n_dp))))
    for bit in order[3:]:
        for part in (first, split, skip):
            part.step("dp", bit)
    top, middle_bit, last = order[:3]
    first.start("dp", top)
    split.start("dp", top)
    token = first.finish()
    first.start("dp", last)
    token = split.finish(after=(token,))
    split.start("dp", middle_bit)
    skip.value = run_gate(skip.value, token)
    skip.start("dp", top)
    token = first.finish(after=(token,))
    first.start("dp", middle_bit)
    token = split.finish(after=(token,))
    split.start("dp", last)
    token = skip.finish(after=(token,))
    skip.start("dp", middle_bit)
    token = split.finish(after=(token,))
    split.start("mp", 1)
    token = first.finish(after=(token,))
    first_own = first.value
    token = skip.finish(after=(token,))
    skip.start("dp", last)
    token = split.finish(after=(token,))
    attn_weights = split.value
    first_pair = [
        value.reshape(n_dp, -1, LANES) for value in (first_own, swap(first_own, "mp", 0))
    ]
    by_core = lambda pair: [
        jnp.where(core == 0, pair[0], pair[1]), jnp.where(core == 0, pair[1], pair[0])
    ]
    dec_parts = by_core([value[:, shared.cuts[3] :] for value in first_pair])
    if aligned:
        stem_b, embed_b, table = unpack(core_id, *first_pair)
    else:
        both = [shared.pieces(value) for value in by_core(first_pair)]
        side = lambda k: jnp.concatenate([both[0][k], both[1][k]], axis=-1)
        stem_b = side(0).reshape(PIXELS, C_STEM)
        embed_b = side(1).reshape(C_STEM, D)
        table = side(2).reshape(D, 2 * LANES).T.astype(f32)
    dec_flat = jnp.stack(dec_parts, axis=1).reshape(n_dp, -1)[:, : shared.flat].reshape(-1)
    dec_b, one_b, two_b, three_b, head_b = split_decoder(dec_flat)

    attn_all = (attn_weights, swap(attn_weights, "mp", 0))

    take = lambda value: lax.dynamic_slice_in_dim(value, mp_id * slices, slices, 0)
    pixels = pad_to(take(images), 1, PAD).reshape(rows, PIXELS)
    label_own = jnp.pad(take(labels), ((0, 0), (0, PAD - PATCHES), (0, 0)), constant_values=-1)
    label_own = label_own.reshape(rows, PIXELS)
    keep = (1 - take(background)).astype(f32)
    owner = (take(patients)[:, None] == jnp.arange(PATIENTS, dtype=jnp.int32)).astype(f32)

    hidden, slope_stem, embed, normed, triple, context = enter(
        pixels, stem_b, embed_b, table, attn_all, attn_cut
    )
    skip_weights = skip.finish(after=(hidden,))
    skip_all = (skip_weights, swap(skip_weights, "mp", 0))
    resid, normed2, slope_mlp, inner, resid2, final_low = middle(
        context, embed, table, attn_all, mlp_all
    )
    three_four = block_diag(three_b, 4)
    big_head = big_head_of(head_b)
    slope0, level0, slope_skips, level1, level2, level3, logits, stats = leave(
        core_id, hidden, final_low, skip_all, dec_b, one_b, two_b, three_four, big_head, label_own
    )

    sums = jnp.sum(stats.reshape(slices, 3 * CLASSES + 1, 8 * LANES), axis=-1)
    class_sums = sums[:, : 3 * CLASSES]
    pat_sums = jnp.sum(owner[:, :, None] * class_sums[:, None, :], axis=0)
    cross_sum = jnp.sum(keep * sums[:, 3 * CLASSES])
    packed = jnp.concatenate(
        [pat_sums.reshape(-1), cross_sum[None], jnp.sum(keep)[None]]
    )
    packed = pad_to(packed, 0, 4 * LANES).reshape(4, LANES)
    packed = butterfly(packed).reshape(-1)
    pat_all = packed[: PATIENTS * 3 * CLASSES].reshape(PATIENTS, CLASSES, 3)
    ce_total = packed[PATIENTS * 3 * CLASSES]
    pixel_count = packed[PATIENTS * 3 * CLASSES + 1] * (PATCHES * PIXELS)
    pat_over, pat_pred, pat_true = pat_all[..., 0], pat_all[..., 1], pat_all[..., 2]
    denominator = pat_pred + pat_true + dice_eps
    dice = (2.0 * pat_over + dice_eps) / denominator
    count_floor = jnp.maximum(pixel_count, 1.0)
    loss = ce_total / count_floor + 1.0 - jnp.mean(dice)
    cells = PATIENTS * CLASSES
    over_coef = -2.0 / (cells * denominator)
    pred_coef = (2.0 * pat_over + dice_eps) / (cells * denominator * denominator)
    pick_own = lambda table: jnp.sum(owner[:, :, None] * table[None], axis=1)
    coef = jnp.concatenate(
        [pick_own(over_coef), pick_own(pred_coef), (keep / count_floor)[:, None]], axis=1
    )

    def x_sum(value):
        value = lax.reduce_precision(value, 8, 7).astype(bf16)
        return value.astype(f32) + swap(value, "mp", 1).astype(f32)

    def core_pair(send, own):
        return Scatter(own, swap(send, "mp", 0))

    grad_logits, grad_skips = leave_back(
        coef, logits, label_own, slope_skips, big_head, three_four, two_b
    )
    skip_send, skip_keep = skip_grad(core_id, hidden, grad_skips)
    grad_pre0, grad_resid2, grad_resid2_low, sums_f = turn(
        grad_skips, one_b, slope0, dec_b, resid2, table, after=(skip_send,)
    )
    low_bits = list(range(log_two(n_dp)))
    skip_part = core_pair(skip_send, skip_keep)
    token = skip_part.step("dp", low_bits[0], bf16, after=(grad_pre0,))
    down_send, down_keep = half_grad(core_id, grad_resid2_low, inner, after=(token,))
    grad_pre, grad_resid, grad_resid_low, grad_context, sums_2 = middle_back(
        grad_resid2_low, mlp_all, slope_mlp, resid, table, grad_resid2, attn_all,
        after=(down_send,),
    )
    down = core_pair(down_send, down_keep)
    token = down.step("dp", low_bits[0], bf16, after=(grad_pre,))
    token = skip_part.step("dp", low_bits[1], after=(token,))
    in_send, in_keep = half_grad(core_id, normed2, grad_pre, after=(token,))
    grad_triple = attn_back(triple, grad_context, after=(in_send,))
    into = core_pair(in_send, in_keep)
    token = into.step("mp", 1, bf16, after=(grad_triple,))
    token = skip_part.step("dp", low_bits[2], after=(token,))
    attn_send, attn_keep = attn_grad(
        normed, grad_triple, grad_resid_low, context, after=(token,)
    )
    token = down.step("dp", low_bits[1], after=(attn_send,))
    decoder_halves = decoder_grad(
        level3, grad_logits, level2, level1, grad_skips, level0, final_low, grad_pre0,
        n_dp, shared.flat_rows, after=(token,),
    )
    token = decoder_halves
    grad_embed_low, grad_pre_stem, grad_pos, sums_1 = enter_back(
        core_id, grad_triple, attn_all, embed, table, grad_resid, embed_b, grad_skips, skip_all,
        slope_stem, after=(token,),
    )
    attn = core_pair(attn_send, attn_keep)
    token = attn.step("mp", 1, bf16, after=(grad_embed_low,))
    token = into.step("dp", low_bits[0], after=(token,))
    token = down.step("dp", low_bits[2], after=(token,))
    if aligned:
        first_send, first_keep = first_grad(
            core_id, pixels, grad_pre_stem, hidden, grad_embed_low, grad_pos, sums_1, sums_2,
            sums_f, decoder_halves, shared.cuts[-1], after=(token,),
        )
    else:
        gains = jnp.concatenate([sums_1, sums_2, sums_f], axis=0).reshape(6, 8, D).sum(axis=1)
        grad_token = pad_to(jnp.concatenate([grad_pos[:PATCHES], gains], axis=0).T, 1, 2 * LANES)

        def first_half(which):
            blocks = lambda value: value.reshape(n_dp, -1, value.shape[-1])
            stem_part = t_matmul(pixels, half_columns(grad_pre_stem, which))
            embed_part = t_matmul(hidden, half_columns(grad_embed_low, which))
            return jnp.concatenate(
                [
                    stack_columns(blocks(stem_part), LANES),
                    stack_columns(blocks(embed_part), LANES),
                    blocks(half_columns(grad_token, which)),
                    lax.dynamic_index_in_dim(decoder_halves, which, 0, keepdims=False).astype(f32),
                ],
                axis=1,
            ).astype(bf16)

        first_send, first_keep = first_half(1 - core), first_half(core)
    wide = lambda value: value.reshape(-1, LANES)
    first = core_pair(wide(first_send), wide(first_keep))
    token = into.step("dp", low_bits[1], after=(first_send,))
    token = first.step("dp", low_bits[0], after=(token,))
    token = down.step("mp", 1, after=(token,))
    token = attn.step("dp", low_bits[0], after=(token,))
    token = into.step("dp", low_bits[2], after=(token,))
    token = first.step("dp", low_bits[1], after=(token,))
    token = attn.step("dp", low_bits[1], after=(token,))
    token = first.step("dp", low_bits[2], after=(token,))
    token = attn.step("dp", low_bits[2], after=(token,))
    for bit in low_bits[3:]:
        for part in (skip_part, down, into, first, attn):
            part.step("dp", bit)
    down_own, in_own, attn_own = down.total(), into.total(), attn.total()
    first_half_sum = x_sum(first.total())
    skip_half = x_sum(skip_part.total())

    square = lambda value: jnp.sum(value * value)
    n_copies = n_mp // 2
    local = (
        square(down_own)
        + square(in_own)
        + square(attn_own)
        + (square(skip_half) + square(first_half_sum)) / n_copies
    )
    total = butterfly(jnp.broadcast_to(local, (8, LANES)))[0, 0]
    grad_norm = jnp.sqrt(total)
    factor = jnp.minimum(1.0, clip_limit / (grad_norm + 1e-06))

    red_skip = jnp.concatenate(by_core([skip_half, swap(skip_half, "mp", 0)]), axis=1)
    own = [shared.pieces(part) for part in by_core([first_half_sum, swap(first_half_sum, "mp", 0)])]
    red_stem = jnp.concatenate([own[0][0], own[1][0]], axis=-1)
    red_embed = jnp.concatenate([own[0][1], own[1][1]], axis=-1)
    red_token = jnp.concatenate([own[0][2], own[1][2]], axis=-1)[:, : PATCHES + 6].T
    red_decoder = jnp.concatenate([own[0][3], own[1][3]], axis=0).reshape(-1)[: shared.flat]
    red_qkv = attn_own[:, :attn_cut]
    red_out = attn_own[:, attn_cut:].T
    red_in = in_own
    red_down = down_own.T
    reduced = (
        red_stem, red_embed, red_token, red_qkv, red_out, red_in, red_down, red_skip, red_decoder,
    )
    rates = [learn_rate] * 9
    rates[2] = token_rate
    results = [
        adamw(weight, grad * factor, first, second, rate)
        for weight, grad, first, second, rate in zip(
            masters, reduced, firsts, seconds, rates, strict=True
        )
    ]
    news = [item[0] for item in results]
    moms = [item[1] for item in results]
    secs = [item[2] for item in results]
    return (loss, pixel_count, grad_norm, *news, *moms, *secs)


def solution(mesh):
    weights = (
        P("dp", None),
        P("dp", None),
        P(None, "dp"),
        P("dp", "mp"),
        P("mp", "dp"),
        P("dp", "mp"),
        P("mp", "dp"),
        P("dp", None),
        P("dp"),
    )
    placed = (P("dp", None, None), P("dp", None, None), P("dp"), P("dp")) + weights * 3
    outs = (P(), P(), P()) + weights * 3
    return jax.shard_map(body, mesh=mesh, in_specs=placed, out_specs=outs, check_vma=False)
```

```python
import jax
import jax.numpy as jnp
from jax import lax
from jax.experimental import pallas as pl
from jax.experimental.pallas import tpu as pltpu
from jax.sharding import PartitionSpec as P

D = 768
HEAD_DIM = 64
PATCHES = 196
PAD = 208
PIXELS = 256
C_STEM = 1024
CHAN_A = 256
CHAN_B = 128
CHAN_C = 64
CHAN_D = 16
CLASSES = 9
PATIENTS = 16
STEP = 10
GROUP = 32
LANES = 128

norm_eps = 1e-06
dice_eps = 1e-05
clip_limit = 0.002
learn_rate = 0.05
token_rate = 0.5
beta_one = 0.9
beta_two = 0.999
adam_eps = 1e-08
decay_rate = 0.01
highest = lax.Precision.HIGHEST
bf16 = jnp.bfloat16
f32 = jnp.float32
MIB = 1024 * 1024


def layer_norm(inputs, gain, shift):
    center = inputs - jnp.mean(inputs, axis=-1, keepdims=True)
    spread = jnp.mean(center * center, axis=-1, keepdims=True)
    return center * lax.rsqrt(spread + norm_eps) * gain + shift


def matmul(left, right):
    return jnp.dot(left, right, preferred_element_type=f32)


def matmul_t(left, right):
    return lax.dot_general(left, right, (((1,), (1,)), ((), ())), preferred_element_type=f32)


def t_matmul(left, right):
    return lax.dot_general(left, right, (((0,), (0,)), ((), ())), preferred_element_type=f32)


FULL = pl.BlockSpec(memory_space=pltpu.VMEM)
SCALAR = pl.BlockSpec(memory_space=pltpu.SMEM)
BLOCK = 256
CHUNK = 16
GELU_SCALE = 0.7978845608028654
GELU_CUBE = 0.044715


def cost(micros):
    return pl.CostEstimate(
        flops=int(micros * 3e9), bytes_accessed=int(micros * 9e6), transcendentals=0
    )


def params():
    return pltpu.CompilerParams(vmem_limit_bytes=32 * MIB)


def run_after(kernel, count, after):
    extra = len(after)

    def ordered(*refs):
        kernel(*refs[:count], *refs[count + extra :])

    return ordered, [pl.BlockSpec(memory_space=pl.ANY)] * extra


def swap(value, axis, bit):
    size = lax.axis_size(axis)
    return lax.ppermute(value, axis, [(i, i ^ (1 << bit)) for i in range(size)])


def my_bit(axis, bit):
    return (lax.axis_index(axis) >> bit) & 1


def log_two(size):
    return size.bit_length() - 1


def gather_kernel(lanes, mine_ref, own_ref, other_ref, out_ref):
    mine = mine_ref[0]
    for which, source_ref in ((mine, own_ref), (1 - mine, other_ref)):
        if lanes:
            width = own_ref.shape[1]
            out_ref[:, pl.ds(pl.multiple_of(which * width, LANES), width)] = source_ref[...]
        else:
            for a in range(out_ref.shape[0]):
                out_ref[a, which] = source_ref[a]


def gate_kernel(value_ref, *refs):
    pass


def run_gate(value, *tokens):
    anywhere = pl.BlockSpec(memory_space=pl.ANY)
    return pl.pallas_call(
        gate_kernel,
        in_specs=[anywhere] * (1 + len(tokens)),
        out_specs=anywhere,
        out_shape=jax.ShapeDtypeStruct(value.shape, value.dtype),
        input_output_aliases={0: 0},
        name="gate",
    )(value, *tokens)


class Gather:
    def __init__(self, block):
        self.value = block
        self.bits = []
        self.pending = None

    def start(self, axis, bit):
        self.pending = (axis, bit, swap(self.value, axis, bit))
        return self.value

    def finish(self, after=()):
        axis, bit, other = self.pending
        rows, columns = self.value.shape
        lanes = axis == "mp"
        if lanes:
            shape, out = (rows, columns), (rows, 2 * columns)
        else:
            ahead = 2 ** sum(b > bit for b in self.bits)
            self.bits.append(bit)
            shape = (ahead, rows // ahead, columns)
            out = (ahead, 2, rows // ahead, columns)
        kernel, waits = run_after(lambda *refs: gather_kernel(lanes, *refs), 3, after)
        value = pl.pallas_call(
            kernel,
            in_specs=[SCALAR] + [FULL] * 2 + waits,
            out_specs=FULL,
            out_shape=jax.ShapeDtypeStruct(out, self.value.dtype),
            compiler_params=params(),
            cost_estimate=cost(0.1),
            name="gather_step",
        )(my_bit(axis, bit).reshape(1), self.value.reshape(shape), other.reshape(shape), *after)
        self.value = value.reshape(-1, value.shape[-1])
        return self.value

    def step(self, axis, bit, after=()):
        self.start(axis, bit)
        return self.finish(after)


def scatter_kernel(lanes, mine_ref, *refs):
    terms, (send_ref, keep_ref) = refs[:-2], refs[-2:]
    mine = mine_ref[0]
    for which, out_ref in ((1 - mine, send_ref), (mine, keep_ref)):
        if lanes:
            width = out_ref.shape[1]
            cols = pl.ds(pl.multiple_of(which * width, LANES), width)
            total = sum(term[:, cols].astype(f32) for term in terms)
            out_ref[...] = total.astype(out_ref.dtype)
        else:
            total = sum(term[0, which].astype(f32) for term in terms)
            out_ref[0] = total.astype(out_ref.dtype)


class Scatter:
    def __init__(self, *terms):
        self.bits = list(reversed(range(log_two(lax.axis_size("dp")))))
        self.terms = list(terms)
        self.send = None

    def step(self, axis, bit, kept_type=f32, after=()):
        rows, columns = self.terms[0].shape
        lanes = axis == "mp"
        if lanes:
            shape, half = (rows, columns), (rows, columns // 2)
            steps = max(rows // (LANES + CHUNK), 1)
            steps = next(k for k in range(steps, 0, -1) if rows % (k * CHUNK) == 0 or k == 1)
            block = lambda size: pl.BlockSpec((rows // steps, size[1]), lambda i: (i, 0))
        else:
            steps = 2 ** self.bits.index(bit)
            self.bits.remove(bit)
            shape = (steps, 2, rows // (2 * steps), columns)
            half = (steps, rows // (2 * steps), columns)
            block = lambda size: pl.BlockSpec(
                (1,) + size[1:], lambda i: (i,) + (0,) * (len(size) - 1)
            )
        count = len(self.terms)
        body_kernel = lambda *refs: scatter_kernel(lanes, *refs)
        kernel, waits = run_after(body_kernel, 1 + count, after)
        send, kept = pl.pallas_call(
            kernel,
            grid=(steps,),
            in_specs=[SCALAR] + [block(shape)] * count + waits,
            out_specs=[block(half)] * 2,
            out_shape=[jax.ShapeDtypeStruct(half, bf16), jax.ShapeDtypeStruct(half, kept_type)],
            compiler_params=params(),
            cost_estimate=cost(0.1),
            name="scatter_step",
        )(my_bit(axis, bit).reshape(1), *[term.reshape(shape) for term in self.terms], *after)
        flat = lambda value: value.reshape(-1, value.shape[-1])
        self.send = flat(send)
        self.terms = [flat(kept), swap(self.send, axis, bit)]
        return self.send

    def total(self):
        return sum(term.astype(f32) for term in self.terms)


def butterfly(value):
    def hop(value, moves):
        size = lax.axis_size("dp") * lax.axis_size("mp")
        get = lambda move: lax.ppermute(value, ("dp", "mp"), [(i, i ^ move) for i in range(size)])
        if len(moves) == 1:
            return value + get(moves[0])
        one, two = moves
        first, second, third = get(one), get(two), get(one | two)
        return (value + first) + (second + third)

    value = hop(value, (1,))
    bits = log_two(lax.axis_size("dp"))
    moves = [2] + [4 << bit for bit in range(bits)]
    for i in range(0, len(moves), 2):
        value = hop(value, tuple(moves[i : i + 2]))
    return value


def gelu_pair(value):
    square = value * value
    wave = jnp.tanh(value * (GELU_SCALE + (GELU_SCALE * GELU_CUBE) * square))
    half = 0.5 + 0.5 * wave
    inner = GELU_SCALE + (3.0 * GELU_SCALE * GELU_CUBE) * square
    return value * half, half + 0.5 * value * (1.0 - wave * wave) * inner


def norm_rows(x_ref, gain, shift, out_ref):
    @pl.loop(0, x_ref.shape[0] // CHUNK, unroll=13)
    def _(i):
        rows = pl.ds(pl.multiple_of(i * CHUNK, CHUNK), CHUNK)
        out_ref[rows, :] = layer_norm(x_ref[rows, :], gain, shift).astype(out_ref.dtype)


def norm_back_rows(x_ref, gain, grad_ref, extra_ref, out_ref, low_ref, sum_ref):
    sum_ref[...] = jnp.zeros_like(sum_ref)

    @pl.loop(0, x_ref.shape[0] // CHUNK, unroll=13)
    def _(i):
        rows = pl.ds(pl.multiple_of(i * CHUNK, CHUNK), CHUNK)
        value = x_ref[rows, :]
        grad = grad_ref[rows, :]
        center = value - jnp.mean(value, axis=-1, keepdims=True)
        scale = lax.rsqrt(jnp.mean(center * center, axis=-1, keepdims=True) + norm_eps)
        hat = center * scale
        for k, term in enumerate((grad * hat, grad)):
            sum_ref[8 * k : 8 * k + 8, :] += term[:8] + term[8:]
        pull = grad * gain
        mean_one = jnp.mean(pull, axis=-1, keepdims=True)
        mean_two = jnp.mean(pull * hat, axis=-1, keepdims=True)
        result = scale * (pull - mean_one - hat * mean_two)
        if extra_ref is not None:
            result = result + extra_ref[rows, :]
        out_ref[rows, :] = result
        low_ref[rows, :] = result.astype(bf16)


def gelu_blocks(width):
    return [slice(j, j + BLOCK) for j in range(0, width, BLOCK)]


def soft_rows(scores, column):
    scores = jnp.where(column < PATCHES, scores * HEAD_DIM ** (-0.5), -jnp.inf)
    top = jnp.max(scores, axis=-1, keepdims=True)
    weight = jnp.exp(scores - top)
    return weight * (1.0 / jnp.sum(weight, axis=-1, keepdims=True))


def enter_kernel(
    pixels_ref, stem_ref, embed_w_ref, token_ref, own_ref, other_ref,
    hidden_ref, slope_ref, embed_ref, normed_ref, tri_ref, ctx_ref,
):
    for cols in gelu_blocks(C_STEM):
        value, slope = gelu_pair(matmul(pixels_ref[...], stem_ref[:, cols]))
        hidden_ref[:, cols] = value.astype(bf16)
        slope_ref[:, cols] = slope.astype(bf16)
    slices = pixels_ref.shape[0] // PAD
    for cols in gelu_blocks(D):
        value = matmul(hidden_ref[...], embed_w_ref[:, cols])
        for s in range(slices):
            rows = slice(s * PAD, (s + 1) * PAD)
            embed_ref[rows, cols] = value[rows] + token_ref[:PAD, cols]
    gain, shift = token_ref[PATCHES : PATCHES + 1, :], token_ref[PATCHES + 1 : PATCHES + 2, :]
    norm_rows(embed_ref, gain, shift, normed_ref)
    width = tri_ref.shape[2]
    heads = width // (3 * HEAD_DIM)
    stride = width + width // 3
    column = lax.broadcasted_iota(jnp.int32, (PAD, PAD), 1)
    for p in range(tri_ref.shape[0]):
        start = (p % 2) * stride
        weight_ref = (own_ref, other_ref)[p // 2]
        tri_ref[p] = matmul(normed_ref[...], weight_ref[:, start : start + width]).astype(bf16)

    @pl.loop(0, tri_ref.shape[0])
    def _(p):
        for s in range(slices):
            rows = slice(s * PAD, (s + 1) * PAD)
            for h in range(heads):
                base = h * 3 * HEAD_DIM
                queries = tri_ref[p, rows, base : base + HEAD_DIM]
                keys_low = tri_ref[p, rows, base + HEAD_DIM : base + 2 * HEAD_DIM]
                values = tri_ref[p, rows, base + 2 * HEAD_DIM : base + 3 * HEAD_DIM]
                attend = soft_rows(matmul_t(queries, keys_low), column)
                context = matmul(attend.astype(bf16), values)
                ctx_ref[p, rows, h * HEAD_DIM : (h + 1) * HEAD_DIM] = context.astype(bf16)


def enter(pixels, stem_b, embed_b, tokens, attn_all, width):
    rows = pixels.shape[0]
    parts = 4
    return pl.pallas_call(
        enter_kernel,
        in_specs=[FULL] * 6,
        out_specs=[FULL] * 6,
        out_shape=[
            jax.ShapeDtypeStruct((rows, C_STEM), bf16),
            jax.ShapeDtypeStruct((rows, C_STEM), bf16),
            jax.ShapeDtypeStruct((rows, D), f32),
            jax.ShapeDtypeStruct((rows, D), bf16),
            jax.ShapeDtypeStruct((parts, rows, width), bf16),
            jax.ShapeDtypeStruct((parts, rows, width // 3), bf16),
        ],
        compiler_params=params(),
        cost_estimate=cost(20),
        name="enter",
    )(pixels, stem_b, embed_b, tokens, *attn_all)


def middle_kernel(
    ctx_ref, embed_ref, token_ref, own_ref, other_ref, mlp_ref,
    resid_ref, normed2_ref, slope_ref, inner_ref, resid2_ref, final_ref,
):
    p = pl.program_id(0)

    @pl.when(p == 0)
    def _():
        part = ctx_ref.shape[2]
        stride = 4 * part
        for q in range(ctx_ref.shape[0]):
            start = (q % 2) * stride + 3 * part
            weight_ref = (own_ref, other_ref)[q // 2]
            term = matmul_t(ctx_ref[q], weight_ref[:, start : start + part])
            if q == 0:
                resid_ref[...] = embed_ref[...] + term
            else:
                resid_ref[...] += term
        gain, shift = token_ref[PATCHES + 2 : PATCHES + 3, :], token_ref[PATCHES + 3 : PATCHES + 4, :]
        norm_rows(resid_ref, gain, shift, normed2_ref)
        resid2_ref[...] = resid_ref[...]

    each = mlp_ref.shape[2] // 2
    for cols in gelu_blocks(each):
        value, slope = gelu_pair(matmul(normed2_ref[...], mlp_ref[0, :, cols]))
        inner_ref[0, :, cols] = value.astype(bf16)
        slope_ref[0, :, cols] = slope.astype(bf16)
    resid2_ref[...] += matmul_t(inner_ref[0], mlp_ref[0, :, each:])

    @pl.when(p == pl.num_programs(0) - 1)
    def _():
        gain, shift = token_ref[PATCHES + 4 : PATCHES + 5, :], token_ref[PATCHES + 5 : PATCHES + 6, :]
        norm_rows(resid2_ref, gain, shift, final_ref)


def whole_of(value):
    return pl.BlockSpec(value.shape, lambda *_: (0,) * len(value.shape))


def part_of(value):
    rest = len(value.shape) - 1
    return pl.BlockSpec((1,) + tuple(value.shape[1:]), lambda i, *_: (i,) + (0,) * rest)


def middle(context, embed, tokens, attn_all, mlp_all):
    rows = embed.shape[0]
    parts, _, width = mlp_all.shape
    each = width // 2
    outs = [
        jax.ShapeDtypeStruct((rows, D), f32),
        jax.ShapeDtypeStruct((rows, D), bf16),
        jax.ShapeDtypeStruct((parts, rows, each), bf16),
        jax.ShapeDtypeStruct((parts, rows, each), bf16),
        jax.ShapeDtypeStruct((rows, D), f32),
        jax.ShapeDtypeStruct((rows, D), bf16),
    ]
    values = (context, embed, tokens, *attn_all)
    return pl.pallas_call(
        middle_kernel,
        grid=(parts,),
        in_specs=[whole_of(value) for value in values] + [part_of(mlp_all)],
        out_specs=[(part_of if len(out.shape) == 3 else whole_of)(out) for out in outs],
        out_shape=outs,
        compiler_params=params(),
        cost_estimate=cost(26),
        name="middle",
    )(*values, mlp_all)


def class_probs(logits_ref, rows, group):
    width = CLASSES * LANES
    values = [
        logits_ref[rows, group * width + c * LANES : group * width + (c + 1) * LANES]
        for c in range(CLASSES)
    ]
    top = values[0]
    for value in values[1:]:
        top = jnp.maximum(top, value)
    weights = [jnp.exp(value - top) for value in values]
    total = weights[0]
    for weight in weights[1:]:
        total = total + weight
    scale = 1.0 / total
    return values, [weight * scale for weight in weights], top + jnp.log(total)


SPLIT_A = 4 * CHAN_B
SPLIT_B = SPLIT_A + 16 * CHAN_C
SKIPW = SPLIT_B + 64 * CHAN_D


def leave_kernel(
    core_ref, hidden_ref, final_ref, skip_own_ref, skip_other_ref, dec_ref, one_ref, two_ref, three_ref, head_ref, label_ref,
    slope0_ref, level0_ref, slope_ref, level1_ref, level2_ref, level3_ref, logits_ref, stats_ref,
    skips,
):
    value, slope = gelu_pair(matmul(final_ref[...], dec_ref[...]))
    level0_ref[...] = value.astype(bf16)
    slope0_ref[...] = slope

    half = skip_own_ref.shape[1]
    core = core_ref[0]
    for which, weight_ref in ((core, skip_own_ref), (1 - core, skip_other_ref)):
        for j in range(0, half, BLOCK):
            cols = pl.ds(pl.multiple_of(which * half + j, LANES), BLOCK)
            skips[:, cols] = matmul(hidden_ref[...], weight_ref[:, j : j + BLOCK])

    def stage(source, weight, out_ref, cols, skip_cols):
        pre = matmul(source, weight) + skips[:, skip_cols : skip_cols + BLOCK]
        value, slope = gelu_pair(pre)
        out_ref[:, cols : cols + BLOCK] = value.astype(bf16)
        slope_ref[:, skip_cols : skip_cols + BLOCK] = slope.astype(bf16)

    for i in range(2):
        stage(level0_ref[...], one_ref[:, i * BLOCK : (i + 1) * BLOCK], level1_ref, i * BLOCK, i * BLOCK)
    for i in range(4):
        stage(
            level1_ref[:, i * CHAN_B : (i + 1) * CHAN_B], two_ref[...], level2_ref, i * BLOCK,
            SPLIT_A + i * BLOCK,
        )
    for i in range(4):
        stage(
            level2_ref[:, i * BLOCK : (i + 1) * BLOCK], three_ref[...], level3_ref, i * BLOCK,
            SPLIT_B + i * BLOCK,
        )
    inner = head_ref.shape[0]
    width = head_ref.shape[1]
    groups = level3_ref.shape[1] // inner
    for g in range(groups):
        logits_ref[:, g * width : (g + 1) * width] = matmul(
            level3_ref[:, g * inner : (g + 1) * inner], head_ref[...]
        )
    stats_ref[...] = jnp.zeros_like(stats_ref)
    slices = stats_ref.shape[0]
    per_slice = PAD // CHUNK

    @pl.loop(0, slices)
    def _(s):
        @pl.loop(0, per_slice)
        def _(i):
            start = pl.multiple_of(s * PAD + i * CHUNK, CHUNK)
            rows = pl.ds(start, CHUNK)
            row_id = lax.broadcasted_iota(jnp.int32, (CHUNK, LANES), 0) + i * CHUNK
            inside = (row_id < PATCHES).astype(f32)
            for g in range(groups):
                values, probs, log_total = class_probs(logits_ref, rows, g)
                label = label_ref[rows, g * LANES : (g + 1) * LANES]
                cross = jnp.zeros((CHUNK, LANES), f32)
                for c in range(CLASSES):
                    hot = (label == c).astype(f32)
                    cross = cross + hot * (log_total - values[c])
                    for k, term in enumerate((hot * probs[c], inside * probs[c], hot)):
                        spot = 8 * (3 * c + k)
                        stats_ref[s, spot : spot + 8, :] += term[:8] + term[8:]
                spot = 8 * 3 * CLASSES
                stats_ref[s, spot : spot + 8, :] += cross[:8] + cross[8:]


def leave(core, hidden, final_low, skip_all, dec_b, one_b, two_b, three_four, big_head, labels):
    rows = hidden.shape[0]
    slices = rows // PAD
    stat_rows = 8 * (3 * CLASSES + 1)
    return pl.pallas_call(
        leave_kernel,
        in_specs=[SCALAR] + [FULL] * 10,
        out_specs=[FULL] * 8,
        out_shape=[
            jax.ShapeDtypeStruct((rows, CHAN_A), f32),
            jax.ShapeDtypeStruct((rows, CHAN_A), bf16),
            jax.ShapeDtypeStruct((rows, SKIPW), bf16),
            jax.ShapeDtypeStruct((rows, 4 * CHAN_B), bf16),
            jax.ShapeDtypeStruct((rows, 16 * CHAN_C), bf16),
            jax.ShapeDtypeStruct((rows, 64 * CHAN_D), bf16),
            jax.ShapeDtypeStruct((rows, CLASSES * PIXELS), f32),
            jax.ShapeDtypeStruct((slices, stat_rows, LANES), f32),
        ],
        scratch_shapes=[pltpu.VMEM((rows, SKIPW), f32)],
        compiler_params=params(),
        cost_estimate=cost(16),
        name="leave",
    )(core, hidden, final_low, *skip_all, dec_b, one_b, two_b, three_four, big_head, labels)


def leave_back_kernel(
    coef_ref, logits_ref, label_ref, slope_ref, head_ref, three_ref, two_ref,
    g_logits_ref, g_skips_ref,
):
    inner = head_ref.shape[0]
    width = head_ref.shape[1]
    groups = 64 * CHAN_D // inner
    slices = logits_ref.shape[0] // PAD

    @pl.loop(0, slices)
    def _(s):
        cross_scale = coef_ref[s, 2 * CLASSES]

        @pl.loop(0, PAD // CHUNK)
        def _(i):
            start = pl.multiple_of(s * PAD + i * CHUNK, CHUNK)
            rows = pl.ds(start, CHUNK)
            row_id = lax.broadcasted_iota(jnp.int32, (CHUNK, LANES), 0) + i * CHUNK
            inside = (row_id < PATCHES).astype(f32)
            for g in range(groups):
                _, probs, _ = class_probs(logits_ref, rows, g)
                label = label_ref[rows, g * LANES : (g + 1) * LANES]
                mean = jnp.zeros((CHUNK, LANES), f32)
                pulls = []
                for c in range(CLASSES):
                    pull = jnp.where(label == c, coef_ref[s, c], 0.0) + coef_ref[s, CLASSES + c]
                    pulls.append(pull)
                    mean = mean + probs[c] * pull
                mean = mean - cross_scale
                for c in range(CLASSES):
                    grad = probs[c] * (pulls[c] - mean)
                    grad = grad - jnp.where(label == c, cross_scale, 0.0)
                    spot = g * width + c * LANES
                    g_logits_ref[rows, spot : spot + LANES] = (grad * inside).astype(bf16)

    for i in range(4):
        g, part = (i * BLOCK) // inner, (i * BLOCK) % inner
        grad = matmul_t(g_logits_ref[:, g * width : (g + 1) * width], head_ref[part : part + BLOCK, :])
        cols = slice(SPLIT_B + i * BLOCK, SPLIT_B + (i + 1) * BLOCK)
        g_skips_ref[:, cols] = (grad * slope_ref[:, cols].astype(f32)).astype(bf16)
    for i in range(4):
        source = g_skips_ref[:, SPLIT_B + i * BLOCK : SPLIT_B + (i + 1) * BLOCK]
        cols = slice(SPLIT_A + i * BLOCK, SPLIT_A + (i + 1) * BLOCK)
        g_skips_ref[:, cols] = (matmul_t(source, three_ref[...]) * slope_ref[:, cols].astype(f32)).astype(bf16)
    for i in range(4):
        source = g_skips_ref[:, SPLIT_A + i * BLOCK : SPLIT_A + (i + 1) * BLOCK]
        cols = slice(i * CHAN_B, (i + 1) * CHAN_B)
        g_skips_ref[:, cols] = (matmul_t(source, two_ref[...]) * slope_ref[:, cols].astype(f32)).astype(bf16)


def leave_back(coef, logits, labels, slope, big_head, three_four, two_b):
    rows = logits.shape[0]
    return pl.pallas_call(
        leave_back_kernel,
        in_specs=[SCALAR] + [FULL] * 6,
        out_specs=[FULL] * 2,
        out_shape=[
            jax.ShapeDtypeStruct((rows, CLASSES * PIXELS), bf16),
            jax.ShapeDtypeStruct((rows, SKIPW), bf16),
        ],
        compiler_params=params(),
        cost_estimate=cost(10),
        name="leave_back",
    )(coef, logits, labels, slope, big_head, three_four, two_b)


def skip_grad_kernel(core_ref, hidden_ref, g_skips_ref, send_ref, keep_ref):
    half = send_ref.shape[1]
    core = core_ref[0]
    for which, out_ref in ((1 - core, send_ref), (core, keep_ref)):
        for j in range(0, half, half // 2):
            cols = pl.ds(pl.multiple_of(which * half + j, LANES), half // 2)
            out_ref[:, j : j + half // 2] = t_matmul(hidden_ref[...], g_skips_ref[:, cols]).astype(
                bf16
            )


def skip_grad(core, hidden, g_skips):
    shape = (hidden.shape[1], g_skips.shape[1] // 2)
    return pl.pallas_call(
        skip_grad_kernel,
        in_specs=[SCALAR] + [FULL] * 2,
        out_specs=[FULL] * 2,
        out_shape=[jax.ShapeDtypeStruct(shape, bf16)] * 2,
        compiler_params=params(),
        cost_estimate=cost(6),
        name="skip_grad",
    )(core, hidden, g_skips)


def turn_kernel(
    g_skips_ref, one_ref, slope0_ref, dec_ref, resid2_ref, token_ref,
    g_pre0_ref, g_resid2_ref, low_ref, sums_ref, g_final,
):
    grad = matmul_t(g_skips_ref[:, :SPLIT_A], one_ref[...])
    g_pre0_ref[...] = (grad * slope0_ref[...]).astype(bf16)
    g_final[...] = matmul_t(g_pre0_ref[...], dec_ref[...])
    norm_back_rows(
        resid2_ref, token_ref[PATCHES + 4 : PATCHES + 5, :], g_final, None, g_resid2_ref, low_ref, sums_ref
    )


def turn(g_skips, one_b, slope0, dec_b, resid2, tokens, after=()):
    rows = resid2.shape[0]
    kernel, waits = run_after(turn_kernel, 6, after)
    return pl.pallas_call(
        kernel,
        in_specs=[FULL] * 6 + waits,
        out_specs=[FULL] * 4,
        out_shape=[
            jax.ShapeDtypeStruct((rows, CHAN_A), bf16),
            jax.ShapeDtypeStruct((rows, D), f32),
            jax.ShapeDtypeStruct((rows, D), bf16),
            jax.ShapeDtypeStruct((16, D), f32),
        ],
        scratch_shapes=[pltpu.VMEM((rows, D), f32)],
        compiler_params=params(),
        cost_estimate=cost(11),
        name="turn",
    )(g_skips, one_b, slope0, dec_b, resid2, tokens, *after)


FLAT_DEC = D * CHAN_A // LANES
FLAT_ONE = FLAT_DEC + CHAN_A * 4 * CHAN_B // LANES
FLAT_TWO = FLAT_ONE + CHAN_B * 4 * CHAN_C // LANES
FLAT_THREE = FLAT_TWO + CHAN_C * 4 * CHAN_D // LANES


def decoder_grad_kernel(
    level3_ref, g_logits_ref, level2_ref, level1_ref, g_skips_ref, level0_ref, final_ref, g_pre0_ref,
    out_ref, flat_ref, square_ref,
):
    size = out_ref.shape[1]
    flat = (FLAT_THREE * LANES + 4 * CLASSES * CHAN_D) // size
    inner, width = GROUP * CHAN_D, CLASSES * LANES
    tail = flat_ref.shape[0] - FLAT_THREE
    flat_ref[FLAT_THREE:, :] = jnp.zeros((tail, LANES), f32)

    def spread(value, base, count):
        for j in range(count):
            flat_ref[pl.ds(base + j, value.shape[0], stride=count), :] = value[
                :, j * LANES : (j + 1) * LANES
            ]

    spread(t_matmul(final_ref[...], g_pre0_ref[...]), 0, CHAN_A // LANES)
    spread(t_matmul(level0_ref[...], g_skips_ref[:, :SPLIT_A]), FLAT_DEC, SPLIT_A // LANES)
    three = jnp.zeros((CHAN_C, 4 * CHAN_D), f32)
    two = jnp.zeros((CHAN_B, 4 * CHAN_C), f32)
    for i in range(4):
        big = t_matmul(
            level2_ref[:, i * BLOCK : (i + 1) * BLOCK],
            g_skips_ref[:, SPLIT_B + i * BLOCK : SPLIT_B + (i + 1) * BLOCK],
        )
        for k in range(4):
            at = slice(k * CHAN_C, (k + 1) * CHAN_C)
            three += big[at, at]
        two += t_matmul(
            level1_ref[:, i * CHAN_B : (i + 1) * CHAN_B],
            g_skips_ref[:, SPLIT_A + i * BLOCK : SPLIT_A + (i + 1) * BLOCK],
        )
    spread(two, FLAT_ONE, 4 * CHAN_C // LANES)
    square_ref[...] = three
    flat_ref[FLAT_TWO:FLAT_THREE, :] = jnp.concatenate(
        [square_ref[pl.ds(j, CHAN_C // 2, stride=2), :] for j in range(2)], axis=1
    )
    head = jnp.zeros((CHAN_D, width), f32)
    row = lax.broadcasted_iota(jnp.int32, (CHAN_D, width), 0)
    across = lax.broadcasted_iota(jnp.int32, (CHAN_D, width), 1)
    parent = (across // 4) % GROUP
    for g in range(level3_ref.shape[1] // inner):
        big = t_matmul(
            level3_ref[:, g * inner : (g + 1) * inner], g_logits_ref[:, g * width : (g + 1) * width]
        )
        for k in range(GROUP):
            head += jnp.where(parent == k, big[k * CHAN_D : (k + 1) * CHAN_D, :], 0.0)
    column = lax.broadcasted_iota(jnp.int32, (width, LANES), 0)
    target = lax.broadcasted_iota(jnp.int32, (width, LANES), 1)
    pick = target == (column % 4) * CLASSES + column // (GROUP * 4)
    small = jnp.dot(head, pick.astype(f32), precision=highest, preferred_element_type=f32)
    lane = lax.broadcasted_iota(jnp.int32, (1, LANES), 1)
    lines = [jnp.zeros((1, LANES), f32) for _ in range(8)]
    for k in range(CHAN_D):
        line, start = divmod(k * 4 * CLASSES, LANES)
        value = small[k : k + 1, :]
        if start:
            value = pltpu.roll(value, start, 1)
        lines[line] = lines[line] + jnp.where(lane >= start, value, 0.0)
        if start + 4 * CLASSES > LANES:
            lines[line + 1] = lines[line + 1] + jnp.where(
                lane < start + 4 * CLASSES - LANES, value, 0.0
            )
    flat_ref[FLAT_THREE : FLAT_THREE + 8, :] = jnp.concatenate(lines, axis=0)

    rows = out_ref.shape[2]
    line_id = lax.broadcasted_iota(jnp.int32, (rows, LANES), 0)
    lane_id = lax.broadcasted_iota(jnp.int32, (rows, LANES), 1)
    for d in range(size):
        for c in range(2):
            first, start = divmod(d * flat + c * rows * LANES, LANES)
            value = flat_ref[first : first + rows, :]
            if start:
                after = flat_ref[first + 1 : first + 1 + rows, :]
                value = jnp.where(
                    lane_id < LANES - start,
                    pltpu.roll(value, LANES - start, 1),
                    pltpu.roll(after, LANES - start, 1),
                )
            inside = (line_id + c * rows) * LANES + lane_id < flat
            out_ref[c, d] = jnp.where(inside, value, 0.0).astype(bf16)


def decoder_grad(
    level3, g_logits, level2, level1, g_skips, level0, final_low, g_pre0, size, rows, after=()
):
    kernel, waits = run_after(decoder_grad_kernel, 8, after)
    flat = (FLAT_THREE * LANES + 4 * CLASSES * CHAN_D) // size
    lines = (size - 1) * flat // LANES + 2 * rows + 8
    lines = -(-max(lines, FLAT_THREE + 8) // 8) * 8
    return pl.pallas_call(
        kernel,
        in_specs=[FULL] * 8 + waits,
        out_specs=FULL,
        out_shape=jax.ShapeDtypeStruct((2, size, rows, LANES), bf16),
        scratch_shapes=[pltpu.VMEM((lines, LANES), f32), pltpu.VMEM((CHAN_C, 4 * CHAN_D), f32)],
        compiler_params=params(),
        cost_estimate=cost(7),
        name="decoder_grad",
    )(level3, g_logits, level2, level1, g_skips, level0, final_low, g_pre0, *after)


def first_grad_kernel(
    core_ref, pixels_ref, g_stem_ref, hidden_ref, low_ref, pos_ref, sums1_ref, sums2_ref, sumsf_ref,
    dec_ref, send_ref, keep_ref, token_ref,
):
    core = core_ref[0]
    size = send_ref.shape[0]
    stem_rows, embed_rows, token_rows = PIXELS // size, C_STEM // size, D // size
    token_ref[...] = jnp.zeros_like(token_ref)
    token_ref[:PATCHES, :] = pos_ref[:PATCHES, :]
    for i, sums_ref in enumerate((sums1_ref, sums2_ref, sumsf_ref)):
        for k in range(2):
            at = PATCHES + 2 * i + k
            token_ref[at : at + 1, :] = jnp.sum(
                sums_ref[8 * k : 8 * k + 8, :], axis=0, keepdims=True
            )
    for which, out_ref in ((1 - core, send_ref), (core, keep_ref)):
        spot = 0
        half = C_STEM // 2
        for j in range(0, half, BLOCK):
            cols = pl.ds(pl.multiple_of(which * half + j, LANES), BLOCK)
            part = t_matmul(pixels_ref[...], g_stem_ref[:, cols]).astype(bf16)
            for k in range(0, BLOCK, LANES):
                for d in range(size):
                    out_ref[d, spot : spot + stem_rows, :] = part[
                        d * stem_rows : (d + 1) * stem_rows, k : k + LANES
                    ]
                spot += stem_rows
        half = D // 2
        cols = pl.ds(pl.multiple_of(which * half, LANES), half)
        part = t_matmul(hidden_ref[...], low_ref[:, cols]).astype(bf16)
        for k in range(0, half, LANES):
            for d in range(size):
                out_ref[d, spot : spot + embed_rows, :] = part[
                    d * embed_rows : (d + 1) * embed_rows, k : k + LANES
                ]
            spot += embed_rows
        turned = token_ref[pl.ds(pl.multiple_of(which * LANES, LANES), LANES), :].T.astype(bf16)
        for d in range(size):
            out_ref[d, spot : spot + token_rows, :] = turned[d * token_rows : (d + 1) * token_rows]
            out_ref[d, spot + token_rows :, :] = dec_ref[which, d]


def first_grad(core, pixels, g_stem, hidden, low, pos, sums1, sums2, sumsf, dec, rows, after=()):
    kernel, waits = run_after(first_grad_kernel, 10, after)
    shape = (dec.shape[1], rows, LANES)
    return pl.pallas_call(
        kernel,
        in_specs=[SCALAR] + [FULL] * 9 + waits,
        out_specs=[FULL] * 2,
        out_shape=[jax.ShapeDtypeStruct(shape, bf16)] * 2,
        scratch_shapes=[pltpu.VMEM((2 * LANES, D), f32)],
        compiler_params=params(),
        cost_estimate=cost(6),
        name="first_grad",
    )(core, pixels, g_stem, hidden, low, pos, sums1, sums2, sumsf, dec, *after)


def unpack_kernel(core_ref, own_ref, other_ref, stem_ref, embed_ref, token_ref, turned_ref):
    core = core_ref[0]
    size = own_ref.shape[0]
    stem_rows, embed_rows, token_rows = PIXELS // size, C_STEM // size, D // size
    for which, block_ref in ((core, own_ref), (1 - core, other_ref)):
        spot = 0
        for target_ref, rows, half in (
            (stem_ref, stem_rows, C_STEM // 2),
            (embed_ref, embed_rows, D // 2),
            (turned_ref, token_rows, LANES),
        ):
            for k in range(0, half, LANES):
                cols = pl.ds(pl.multiple_of(which * half + k, LANES), LANES)
                for d in range(size):
                    target_ref[d * rows : (d + 1) * rows, cols] = block_ref[
                        d, spot : spot + rows, :
                    ].astype(target_ref.dtype)
                spot += rows
    token_ref[...] = turned_ref[...].T


def unpack(core, own, other):
    return pl.pallas_call(
        unpack_kernel,
        in_specs=[SCALAR] + [FULL] * 2,
        out_specs=[FULL] * 3,
        out_shape=[
            jax.ShapeDtypeStruct((PIXELS, C_STEM), bf16),
            jax.ShapeDtypeStruct((C_STEM, D), bf16),
            jax.ShapeDtypeStruct((2 * LANES, D), f32),
        ],
        scratch_shapes=[pltpu.VMEM((D, 2 * LANES), f32)],
        compiler_params=params(),
        cost_estimate=cost(4),
        name="unpack",
    )(core, own, other)


def pack_kernel(core_ref, stem_ref, embed_ref, token_ref, dec_ref, out_ref):
    core = core_ref[0]
    spot = 0
    for source_ref in (stem_ref, embed_ref, token_ref):
        rows, half = source_ref.shape[0], source_ref.shape[1] // 2
        for k in range(0, half, LANES):
            cols = pl.ds(pl.multiple_of(core * half + k, LANES), LANES)
            out_ref[spot : spot + rows, :] = source_ref[:, cols].astype(bf16)
            spot += rows
    out_ref[spot:, :] = dec_ref[core].astype(bf16)


def pack(core, stem_w, embed_w, token_t, dec, rows):
    return pl.pallas_call(
        pack_kernel,
        in_specs=[SCALAR] + [FULL] * 4,
        out_specs=FULL,
        out_shape=jax.ShapeDtypeStruct((rows, LANES), bf16),
        compiler_params=params(),
        cost_estimate=cost(2),
        name="pack",
    )(core, stem_w, embed_w, token_t, dec)


def middle_back_kernel(
    low2_ref, mlp_ref, slope_ref, resid_ref, token_ref, g_resid2_ref, own_ref, other_ref,
    g_pre_ref, g_resid_ref, low_ref, g_ctx_ref, sums_ref, g_normed,
):
    p = pl.program_id(0)
    each = mlp_ref.shape[2] // 2
    for cols in gelu_blocks(each):
        down = mlp_ref[0, :, each + cols.start : each + cols.stop]
        grad = matmul(low2_ref[...], down) * slope_ref[0, :, cols].astype(f32)
        g_pre_ref[0, :, cols] = grad.astype(bf16)
    term = matmul_t(g_pre_ref[0], mlp_ref[0, :, :each])

    @pl.when(p == 0)
    def _():
        g_normed[...] = term

    @pl.when(p > 0)
    def _():
        g_normed[...] += term

    @pl.when(p == pl.num_programs(0) - 1)
    def _():
        norm_back_rows(
            resid_ref, token_ref[PATCHES + 2 : PATCHES + 3, :], g_normed, g_resid2_ref,
            g_resid_ref, low_ref, sums_ref,
        )
        part = g_ctx_ref.shape[2]
        for q in range(g_ctx_ref.shape[0]):
            start = (q % 2) * 4 * part + 3 * part
            weight_ref = (own_ref, other_ref)[q // 2]
            g_ctx_ref[q] = matmul(low_ref[...], weight_ref[:, start : start + part]).astype(bf16)


def middle_back(low2, mlp_all, slope, resid, tokens, g_resid2, attn_all, after=()):
    kernel, waits = run_after(middle_back_kernel, 8, after)
    rows = resid.shape[0]
    parts, _, each = slope.shape
    part = attn_all[0].shape[1] // 8
    outs = [
        jax.ShapeDtypeStruct((parts, rows, each), bf16),
        jax.ShapeDtypeStruct((rows, D), f32),
        jax.ShapeDtypeStruct((rows, D), bf16),
        jax.ShapeDtypeStruct((parts, rows, part), bf16),
        jax.ShapeDtypeStruct((16, D), f32),
    ]
    values = (resid, tokens, g_resid2, *attn_all)
    return pl.pallas_call(
        kernel,
        grid=(parts,),
        in_specs=[whole_of(low2), part_of(mlp_all), part_of(slope)]
        + [whole_of(value) for value in values]
        + waits,
        out_specs=[part_of(outs[0])] + [whole_of(out) for out in outs[1:]],
        out_shape=outs,
        scratch_shapes=[pltpu.VMEM((rows, D), f32)],
        compiler_params=params(),
        cost_estimate=cost(21),
        name="middle_back",
    )(low2, mlp_all, slope, *values, *after)


def half_grad_kernel(core_ref, left_ref, right_ref, send_ref, keep_ref):
    core = core_ref[0]
    each = right_ref.shape[2]
    for which, out_ref in ((1 - core, send_ref), (core, keep_ref)):
        for x in range(2):
            out_ref[:, x * each : (x + 1) * each] = t_matmul(
                left_ref[...], right_ref[2 * x + which]
            ).astype(bf16)


def half_grad(core, left, right, after=()):
    kernel, waits = run_after(half_grad_kernel, 3, after)
    shape = (left.shape[1], 2 * right.shape[2])
    return pl.pallas_call(
        kernel,
        in_specs=[SCALAR] + [FULL] * 2 + waits,
        out_specs=[FULL] * 2,
        out_shape=[jax.ShapeDtypeStruct(shape, bf16)] * 2,
        compiler_params=params(),
        cost_estimate=cost(6),
        name="half_grad",
    )(core, left, right, *after)


def attn_back_kernel(tri_ref, g_ctx_ref, g_tri_ref):
    slices = tri_ref.shape[1] // PAD
    heads = tri_ref.shape[2] // (3 * HEAD_DIM)
    column = lax.broadcasted_iota(jnp.int32, (PAD, PAD), 1)
    for s in range(slices):
        rows = slice(s * PAD, (s + 1) * PAD)
        for h in range(heads):
            base = h * 3 * HEAD_DIM
            queries = tri_ref[0, rows, base : base + HEAD_DIM]
            keys_low = tri_ref[0, rows, base + HEAD_DIM : base + 2 * HEAD_DIM]
            values = tri_ref[0, rows, base + 2 * HEAD_DIM : base + 3 * HEAD_DIM]
            gctx = g_ctx_ref[0, rows, h * HEAD_DIM : (h + 1) * HEAD_DIM]
            attend = soft_rows(matmul_t(queries, keys_low), column)
            g_attend = matmul_t(gctx, values)
            g_values = t_matmul(attend.astype(bf16), gctx)
            inner = jnp.sum(attend * g_attend, axis=-1, keepdims=True)
            g_scores = attend * (g_attend - inner) * HEAD_DIM ** (-0.5)
            g_low = g_scores.astype(bf16)
            g_tri_ref[0, rows, base : base + HEAD_DIM] = matmul(g_low, keys_low).astype(bf16)
            g_tri_ref[0, rows, base + HEAD_DIM : base + 2 * HEAD_DIM] = t_matmul(
                g_low, queries
            ).astype(bf16)
            g_tri_ref[0, rows, base + 2 * HEAD_DIM : base + 3 * HEAD_DIM] = g_values.astype(bf16)


def attn_back(triple, g_ctx, after=()):
    parts, rows, width = triple.shape
    whole = lambda size: pl.BlockSpec((1, rows, size), lambda i: (i, 0, 0))
    kernel, waits = run_after(attn_back_kernel, 2, after)
    return pl.pallas_call(
        kernel,
        grid=(parts,),
        in_specs=[whole(width), whole(width // 3)] + waits,
        out_specs=whole(width),
        out_shape=jax.ShapeDtypeStruct(triple.shape, bf16),
        compiler_params=params(),
        cost_estimate=cost(15),
        name="attn_back",
    )(triple, g_ctx, *after)


def attn_grad_kernel(normed_ref, g_tri_ref, low_ref, ctx_ref, send_ref, keep_ref):
    width = g_tri_ref.shape[2]
    stride = width + width // 3
    for which, out_ref in ((1, send_ref), (0, keep_ref)):
        for x in range(2):
            part = 2 * which + x
            at = x * stride
            out_ref[:, at : at + width] = t_matmul(normed_ref[...], g_tri_ref[part]).astype(
                out_ref.dtype
            )
            out_ref[:, at + width : at + stride] = t_matmul(low_ref[...], ctx_ref[part]).astype(
                out_ref.dtype
            )


def attn_grad(normed, g_tri, low, context, after=()):
    shape = (D, 2 * (g_tri.shape[2] + context.shape[2]))
    kernel, waits = run_after(attn_grad_kernel, 4, after)
    return pl.pallas_call(
        kernel,
        in_specs=[FULL] * 4 + waits,
        out_specs=[FULL] * 2,
        out_shape=[jax.ShapeDtypeStruct(shape, bf16)] * 2,
        compiler_params=params(),
        cost_estimate=cost(7),
        name="attn_grad",
    )(normed, g_tri, low, context, *after)


def enter_back_kernel(
    core_ref, g_tri_ref, own_ref, other_ref, embed_ref, token_ref, g_resid_ref, embed_w_ref,
    g_skips_ref, skip_own_ref, skip_other_ref, slope_ref, low_ref, g_stem_ref, g_pos_ref, sums_ref, g_normed, g_embed,
):
    width = g_tri_ref.shape[2]
    stride = width + width // 3
    for p in range(g_tri_ref.shape[0]):
        start = (p % 2) * stride
        weight_ref = (own_ref, other_ref)[p // 2]
        term = matmul_t(g_tri_ref[p], weight_ref[:, start : start + width])
        if p == 0:
            g_normed[...] = term
        else:
            g_normed[...] += term
    norm_back_rows(
        embed_ref, token_ref[PATCHES : PATCHES + 1, :], g_normed, g_resid_ref, g_embed, low_ref, sums_ref
    )
    pos = g_embed[:PAD, :]
    for s in range(1, embed_ref.shape[0] // PAD):
        pos = pos + g_embed[s * PAD : (s + 1) * PAD, :]
    g_pos_ref[...] = pos
    half = skip_own_ref.shape[1]
    core = core_ref[0]
    for cols in gelu_blocks(C_STEM):
        grad = matmul_t(low_ref[...], embed_w_ref[cols, :])
        for which, weight_ref in ((core, skip_own_ref), (1 - core, skip_other_ref)):
            part = pl.ds(pl.multiple_of(which * half, LANES), half)
            grad += matmul_t(g_skips_ref[:, part], weight_ref[cols, :])
        g_stem_ref[:, cols] = (grad * slope_ref[:, cols].astype(f32)).astype(bf16)


def enter_back(core, g_tri, attn_all, embed, tokens, g_resid, embed_b, g_skips, skip_all, slope, after=()):
    rows = embed.shape[0]
    kernel, waits = run_after(enter_back_kernel, 12, after)
    return pl.pallas_call(
        kernel,
        in_specs=[SCALAR] + [FULL] * 11 + waits,
        out_specs=[FULL] * 4,
        out_shape=[
            jax.ShapeDtypeStruct((rows, D), bf16),
            jax.ShapeDtypeStruct((rows, C_STEM), bf16),
            jax.ShapeDtypeStruct((PAD, D), f32),
            jax.ShapeDtypeStruct((16, D), f32),
        ],
        scratch_shapes=[pltpu.VMEM((rows, D), f32), pltpu.VMEM((rows, D), f32)],
        compiler_params=params(),
        cost_estimate=cost(21),
        name="enter_back",
    )(core, g_tri, *attn_all, embed, tokens, g_resid, embed_b, g_skips, *skip_all, slope, *after)


def split_decoder(flat):
    edge_one = D * CHAN_A
    edge_two = edge_one + CHAN_A * 4 * CHAN_B
    edge_three = edge_two + CHAN_B * 4 * CHAN_C
    edge_four = edge_three + CHAN_C * 4 * CHAN_D
    return (
        flat[:edge_one].reshape(D, CHAN_A),
        flat[edge_one:edge_two].reshape(CHAN_A, 4 * CHAN_B),
        flat[edge_two:edge_three].reshape(CHAN_B, 4 * CHAN_C),
        flat[edge_three:edge_four].reshape(CHAN_C, 4 * CHAN_D),
        flat[edge_four:].reshape(CHAN_D, 4 * CLASSES),
    )


def same_block(rows, columns, inner, outer):
    row = lax.broadcasted_iota(jnp.int32, (rows, columns), 0) // inner
    column = lax.broadcasted_iota(jnp.int32, (rows, columns), 1) // outer
    return row == column


def block_diag(weight, parents):
    inner, outer = weight.shape
    mask = same_block(parents * inner, parents * outer, inner, outer)
    tiled = jnp.tile(weight, (parents, parents))
    return jnp.where(mask, tiled, jnp.zeros_like(tiled))


def head_masks():
    wide = CLASSES * GROUP * 4
    column = lax.broadcasted_iota(jnp.int32, (4 * CLASSES, wide), 1)
    source = lax.broadcasted_iota(jnp.int32, (4 * CLASSES, wide), 0)
    pick = source == (column % 4) * CLASSES + column // (GROUP * 4)
    row = lax.broadcasted_iota(jnp.int32, (GROUP * CHAN_D, wide), 0)
    across = lax.broadcasted_iota(jnp.int32, (GROUP * CHAN_D, wide), 1)
    mask = row // CHAN_D == (across // 4) % GROUP
    return pick, mask


def big_head_of(head_b):
    pick, mask = head_masks()
    spread = matmul(head_b, pick.astype(bf16)).astype(bf16)
    tiled = jnp.tile(spread, (GROUP, 1))
    return jnp.where(mask, tiled, jnp.zeros_like(tiled))


def stack_columns(value, width):
    count = value.shape[-1] // width
    return jnp.concatenate(
        [value[..., i * width : (i + 1) * width] for i in range(count)], axis=-2
    )


def unstack_columns(value, count):
    rows = value.shape[-2] // count
    return jnp.concatenate(
        [value[..., i * rows : (i + 1) * rows, :] for i in range(count)], axis=-1
    )


def pad_to(value, axis, size):
    widths = [(0, 0)] * value.ndim
    widths[axis] = (0, size - value.shape[axis])
    return jnp.pad(value, widths)


class Shared:
    def __init__(self, stem_w, embed_w, token_params, decoder_w):
        self.stem_rows = stem_w.shape[0]
        self.embed_rows = embed_w.shape[0]
        self.token_rows = token_params.shape[1]
        self.flat = decoder_w.shape[0]
        self.flat_rows = -(-self.flat // (2 * LANES * 16)) * 16
        self.stem_count = C_STEM // 2 // LANES
        self.embed_count = D // 2 // LANES
        self.cuts = [0]
        for rows in (
            self.stem_rows * self.stem_count,
            self.embed_rows * self.embed_count,
            self.token_rows,
            self.flat_rows,
        ):
            self.cuts.append(self.cuts[-1] + rows)

    def half_flat(self, flat):
        padded = pad_to(flat, flat.ndim - 1, 2 * self.flat_rows * LANES)
        return padded.reshape(flat.shape[:-1] + (2, self.flat_rows, LANES))

    def pieces(self, value):
        one, two, three, four = (
            value[..., a:b, :] for a, b in zip(self.cuts[:-1], self.cuts[1:], strict=True)
        )
        return (
            unstack_columns(one, self.stem_count),
            unstack_columns(two, self.embed_count),
            three,
            four,
        )


def half_columns(value, core, axis=-1):
    axis = axis % value.ndim
    size = value.shape[axis] // 2
    return lax.dynamic_slice_in_dim(value, core * size, size, axis)


def adamw(weight, grad, first, second, rate):
    first_new = beta_one * first + (1.0 - beta_one) * grad
    second_new = beta_two * second + (1.0 - beta_two) * grad * grad
    first_hat = first_new / (1.0 - beta_one**STEP)
    second_hat = second_new / (1.0 - beta_two**STEP)
    new_weight = weight - rate * (
        first_hat / (jnp.sqrt(second_hat) + adam_eps) + decay_rate * weight
    )
    return (new_weight, first_new, second_new)


def body(
    images,
    labels,
    background,
    patients,
    *state,
):
    masters, firsts, seconds = state[:9], state[9:18], state[18:]
    stem_w, embed_w, token_params, qkv_w, out_w, mlp_in_w, mlp_out_w, skip_w, decoder_w = masters
    n_dp = lax.axis_size("dp")
    n_mp = lax.axis_size("mp")
    mp_id = lax.axis_index("mp")
    core = mp_id & 1
    slices = images.shape[0] // n_mp
    rows = slices * PAD
    shared = Shared(stem_w, embed_w, token_params, decoder_w)
    attn_cut = qkv_w.shape[1]

    core_id = core.reshape(1)
    token_t = pad_to(token_params.T, 1, 2 * LANES)
    aligned = shared.stem_rows % 16 == 0 and shared.token_rows % 16 == 0
    mlp_block = jnp.concatenate([mlp_in_w, mlp_out_w.T], axis=1).astype(bf16)
    mlp_all = lax.all_gather(mlp_block, ("mp", "dp"), axis=0, tiled=True).reshape(n_mp, D, -1)
    if aligned:
        first_block = pack(
            core_id, stem_w, embed_w, token_t, shared.half_flat(decoder_w), shared.cuts[-1]
        )
    else:
        dec_half = lax.dynamic_index_in_dim(shared.half_flat(decoder_w), core, 0, keepdims=False)
        first_block = jnp.concatenate(
            [
                stack_columns(half_columns(stem_w, core), LANES),
                stack_columns(half_columns(embed_w, core), LANES),
                half_columns(token_t, core),
                dec_half,
            ],
            axis=0,
        ).astype(bf16)
    attn_block = jnp.concatenate([qkv_w, out_w.T], axis=1).astype(bf16)
    skip_block = half_columns(skip_w, core).astype(bf16)

    first, split, skip = Gather(first_block), Gather(attn_block), Gather(skip_block)
    order = list(reversed(range(log_two(n_dp))))
    for bit in order[3:]:
        for part in (first, split, skip):
            part.step("dp", bit)
    top, middle_bit, last = order[:3]
    first.start("dp", top)
    split.start("dp", top)
    token = first.finish()
    first.start("dp", last)
    token = split.finish(after=(token,))
    split.start("dp", middle_bit)
    skip.value = run_gate(skip.value, token)
    skip.start("dp", top)
    token = first.finish(after=(token,))
    first.start("dp", middle_bit)
    token = split.finish(after=(token,))
    split.start("dp", last)
    token = skip.finish(after=(token,))
    skip.start("dp", middle_bit)
    token = split.finish(after=(token,))
    split.start("mp", 1)
    token = first.finish(after=(token,))
    first_own = first.value
    token = skip.finish(after=(token,))
    skip.start("dp", last)
    token = split.finish(after=(token,))
    attn_weights = split.value
    first_pair = [
        value.reshape(n_dp, -1, LANES) for value in (first_own, swap(first_own, "mp", 0))
    ]
    by_core = lambda pair: [
        jnp.where(core == 0, pair[0], pair[1]), jnp.where(core == 0, pair[1], pair[0])
    ]
    dec_parts = by_core([value[:, shared.cuts[3] :] for value in first_pair])
    if aligned:
        stem_b, embed_b, table = unpack(core_id, *first_pair)
    else:
        both = [shared.pieces(value) for value in by_core(first_pair)]
        side = lambda k: jnp.concatenate([both[0][k], both[1][k]], axis=-1)
        stem_b = side(0).reshape(PIXELS, C_STEM)
        embed_b = side(1).reshape(C_STEM, D)
        table = side(2).reshape(D, 2 * LANES).T.astype(f32)
    dec_flat = jnp.stack(dec_parts, axis=1).reshape(n_dp, -1)[:, : shared.flat].reshape(-1)
    dec_b, one_b, two_b, three_b, head_b = split_decoder(dec_flat)

    attn_all = (attn_weights, swap(attn_weights, "mp", 0))

    take = lambda value: lax.dynamic_slice_in_dim(value, mp_id * slices, slices, 0)
    pixels = pad_to(take(images), 1, PAD).reshape(rows, PIXELS)
    label_own = jnp.pad(take(labels), ((0, 0), (0, PAD - PATCHES), (0, 0)), constant_values=-1)
    label_own = label_own.reshape(rows, PIXELS)
    keep = (1 - take(background)).astype(f32)
    owner = (take(patients)[:, None] == jnp.arange(PATIENTS, dtype=jnp.int32)).astype(f32)

    hidden, slope_stem, embed, normed, triple, context = enter(
        pixels, stem_b, embed_b, table, attn_all, attn_cut
    )
    skip_weights = skip.finish(after=(hidden,))
    skip_all = (skip_weights, swap(skip_weights, "mp", 0))
    resid, normed2, slope_mlp, inner, resid2, final_low = middle(
        context, embed, table, attn_all, mlp_all
    )
    three_four = block_diag(three_b, 4)
    big_head = big_head_of(head_b)
    slope0, level0, slope_skips, level1, level2, level3, logits, stats = leave(
        core_id, hidden, final_low, skip_all, dec_b, one_b, two_b, three_four, big_head, label_own
    )

    sums = jnp.sum(stats.reshape(slices, 3 * CLASSES + 1, 8 * LANES), axis=-1)
    class_sums = sums[:, : 3 * CLASSES]
    pat_sums = jnp.sum(owner[:, :, None] * class_sums[:, None, :], axis=0)
    cross_sum = jnp.sum(keep * sums[:, 3 * CLASSES])
    packed = jnp.concatenate(
        [pat_sums.reshape(-1), cross_sum[None], jnp.sum(keep)[None]]
    )
    packed = pad_to(packed, 0, 4 * LANES).reshape(4, LANES)
    packed = butterfly(packed).reshape(-1)
    pat_all = packed[: PATIENTS * 3 * CLASSES].reshape(PATIENTS, CLASSES, 3)
    ce_total = packed[PATIENTS * 3 * CLASSES]
    pixel_count = packed[PATIENTS * 3 * CLASSES + 1] * (PATCHES * PIXELS)
    pat_over, pat_pred, pat_true = pat_all[..., 0], pat_all[..., 1], pat_all[..., 2]
    denominator = pat_pred + pat_true + dice_eps
    dice = (2.0 * pat_over + dice_eps) / denominator
    count_floor = jnp.maximum(pixel_count, 1.0)
    loss = ce_total / count_floor + 1.0 - jnp.mean(dice)
    cells = PATIENTS * CLASSES
    over_coef = -2.0 / (cells * denominator)
    pred_coef = (2.0 * pat_over + dice_eps) / (cells * denominator * denominator)
    pick_own = lambda table: jnp.sum(owner[:, :, None] * table[None], axis=1)
    coef = jnp.concatenate(
        [pick_own(over_coef), pick_own(pred_coef), (keep / count_floor)[:, None]], axis=1
    )

    def x_sum(value):
        value = lax.reduce_precision(value, 8, 7).astype(bf16)
        return value.astype(f32) + swap(value, "mp", 1).astype(f32)

    def core_pair(send, own):
        return Scatter(own, swap(send, "mp", 0))

    grad_logits, grad_skips = leave_back(
        coef, logits, label_own, slope_skips, big_head, three_four, two_b
    )
    skip_send, skip_keep = skip_grad(core_id, hidden, grad_skips)
    grad_pre0, grad_resid2, grad_resid2_low, sums_f = turn(
        grad_skips, one_b, slope0, dec_b, resid2, table, after=(skip_send,)
    )
    low_bits = list(range(log_two(n_dp)))
    skip_part = core_pair(skip_send, skip_keep)
    token = skip_part.step("dp", low_bits[0], bf16, after=(grad_pre0,))
    down_send, down_keep = half_grad(core_id, grad_resid2_low, inner, after=(token,))
    grad_pre, grad_resid, grad_resid_low, grad_context, sums_2 = middle_back(
        grad_resid2_low, mlp_all, slope_mlp, resid, table, grad_resid2, attn_all,
        after=(down_send,),
    )
    down = core_pair(down_send, down_keep)
    token = down.step("dp", low_bits[0], bf16, after=(grad_pre,))
    token = skip_part.step("dp", low_bits[1], after=(token,))
    in_send, in_keep = half_grad(core_id, normed2, grad_pre, after=(token,))
    grad_triple = attn_back(triple, grad_context, after=(in_send,))
    into = core_pair(in_send, in_keep)
    token = into.step("mp", 1, bf16, after=(grad_triple,))
    token = skip_part.step("dp", low_bits[2], after=(token,))
    attn_send, attn_keep = attn_grad(
        normed, grad_triple, grad_resid_low, context, after=(token,)
    )
    token = down.step("dp", low_bits[1], after=(attn_send,))
    decoder_halves = decoder_grad(
        level3, grad_logits, level2, level1, grad_skips, level0, final_low, grad_pre0,
        n_dp, shared.flat_rows, after=(token,),
    )
    attn = core_pair(attn_send, attn_keep)
    token = attn.step("mp", 1, bf16, after=(decoder_halves,))
    grad_embed_low, grad_pre_stem, grad_pos, sums_1 = enter_back(
        core_id, grad_triple, attn_all, embed, table, grad_resid, embed_b, grad_skips, skip_all,
        slope_stem, after=(token,),
    )
    token = into.step("dp", low_bits[0], after=(grad_embed_low,))
    token = down.step("dp", low_bits[2], after=(token,))
    token = attn.step("dp", low_bits[0], after=(token,))
    if aligned:
        first_send, first_keep = first_grad(
            core_id, pixels, grad_pre_stem, hidden, grad_embed_low, grad_pos, sums_1, sums_2,
            sums_f, decoder_halves, shared.cuts[-1], after=(token,),
        )
    else:
        gains = jnp.concatenate([sums_1, sums_2, sums_f], axis=0).reshape(6, 8, D).sum(axis=1)
        grad_token = pad_to(jnp.concatenate([grad_pos[:PATCHES], gains], axis=0).T, 1, 2 * LANES)

        def first_half(which):
            blocks = lambda value: value.reshape(n_dp, -1, value.shape[-1])
            stem_part = t_matmul(pixels, half_columns(grad_pre_stem, which))
            embed_part = t_matmul(hidden, half_columns(grad_embed_low, which))
            return jnp.concatenate(
                [
                    stack_columns(blocks(stem_part), LANES),
                    stack_columns(blocks(embed_part), LANES),
                    blocks(half_columns(grad_token, which)),
                    lax.dynamic_index_in_dim(decoder_halves, which, 0, keepdims=False).astype(f32),
                ],
                axis=1,
            ).astype(bf16)

        first_send, first_keep = first_half(1 - core), first_half(core)
    wide = lambda value: value.reshape(-1, LANES)
    first = core_pair(wide(first_send), wide(first_keep))
    token = first.step("dp", low_bits[0], after=(first_send,))
    token = into.step("dp", low_bits[1], after=(token,))
    token = down.step("mp", 1, after=(token,))
    token = attn.step("dp", low_bits[1], after=(token,))
    token = first.step("dp", low_bits[1], after=(token,))
    token = into.step("dp", low_bits[2], after=(token,))
    token = attn.step("dp", low_bits[2], after=(token,))
    token = first.step("dp", low_bits[2], after=(token,))
    for bit in low_bits[3:]:
        for part in (skip_part, down, into, first, attn):
            part.step("dp", bit)
    down_own, in_own, attn_own = down.total(), into.total(), attn.total()
    first_half_sum = x_sum(first.total())
    skip_half = x_sum(skip_part.total())

    square = lambda value: jnp.sum(value * value)
    n_copies = n_mp // 2
    local = (
        square(down_own)
        + square(in_own)
        + square(attn_own)
        + (square(skip_half) + square(first_half_sum)) / n_copies
    )
    total = butterfly(jnp.broadcast_to(local, (8, LANES)))[0, 0]
    grad_norm = jnp.sqrt(total)
    factor = jnp.minimum(1.0, clip_limit / (grad_norm + 1e-06))

    red_skip = jnp.concatenate(by_core([skip_half, swap(skip_half, "mp", 0)]), axis=1)
    own = [shared.pieces(part) for part in by_core([first_half_sum, swap(first_half_sum, "mp", 0)])]
    red_stem = jnp.concatenate([own[0][0], own[1][0]], axis=-1)
    red_embed = jnp.concatenate([own[0][1], own[1][1]], axis=-1)
    red_token = jnp.concatenate([own[0][2], own[1][2]], axis=-1)[:, : PATCHES + 6].T
    red_decoder = jnp.concatenate([own[0][3], own[1][3]], axis=0).reshape(-1)[: shared.flat]
    red_qkv = attn_own[:, :attn_cut]
    red_out = attn_own[:, attn_cut:].T
    red_in = in_own
    red_down = down_own.T
    reduced = (
        red_stem, red_embed, red_token, red_qkv, red_out, red_in, red_down, red_skip, red_decoder,
    )
    rates = [learn_rate] * 9
    rates[2] = token_rate
    results = [
        adamw(weight, grad * factor, first, second, rate)
        for weight, grad, first, second, rate in zip(
            masters, reduced, firsts, seconds, rates, strict=True
        )
    ]
    news = [item[0] for item in results]
    moms = [item[1] for item in results]
    secs = [item[2] for item in results]
    return (loss, pixel_count, grad_norm, *news, *moms, *secs)


def solution(mesh):
    weights = (
        P("dp", None),
        P("dp", None),
        P(None, "dp"),
        P("dp", "mp"),
        P("mp", "dp"),
        P("dp", "mp"),
        P("mp", "dp"),
        P("dp", None),
        P("dp"),
    )
    placed = (P("dp", None, None), P("dp", None, None), P("dp"), P("dp")) + weights * 3
    outs = (P(), P(), P()) + weights * 3
    return jax.shard_map(body, mesh=mesh, in_specs=placed, out_specs=outs, check_vma=False)
```

```python
import jax
import jax.numpy as jnp
from jax import lax
from jax.experimental import pallas as pl
from jax.experimental.pallas import tpu as pltpu
from jax.sharding import PartitionSpec as P

D = 768
HEAD_DIM = 64
PATCHES = 196
PAD = 208
PIXELS = 256
C_STEM = 1024
CHAN_A = 256
CHAN_B = 128
CHAN_C = 64
CHAN_D = 16
CLASSES = 9
PATIENTS = 16
STEP = 10
GROUP = 32
LANES = 128

norm_eps = 1e-06
dice_eps = 1e-05
clip_limit = 0.002
learn_rate = 0.05
token_rate = 0.5
beta_one = 0.9
beta_two = 0.999
adam_eps = 1e-08
decay_rate = 0.01
highest = lax.Precision.HIGHEST
bf16 = jnp.bfloat16
f32 = jnp.float32
MIB = 1024 * 1024


def layer_norm(inputs, gain, shift):
    center = inputs - jnp.mean(inputs, axis=-1, keepdims=True)
    spread = jnp.mean(center * center, axis=-1, keepdims=True)
    return center * lax.rsqrt(spread + norm_eps) * gain + shift


def matmul(left, right):
    return jnp.dot(left, right, preferred_element_type=f32)


def matmul_t(left, right):
    return lax.dot_general(left, right, (((1,), (1,)), ((), ())), preferred_element_type=f32)


def t_matmul(left, right):
    return lax.dot_general(left, right, (((0,), (0,)), ((), ())), preferred_element_type=f32)


FULL = pl.BlockSpec(memory_space=pltpu.VMEM)
SCALAR = pl.BlockSpec(memory_space=pltpu.SMEM)
BLOCK = 256
CHUNK = 16
GELU_SCALE = 0.7978845608028654
GELU_CUBE = 0.044715


def cost(micros):
    return pl.CostEstimate(
        flops=int(micros * 2e9), bytes_accessed=int(micros * 6e6), transcendentals=0
    )


def params():
    return pltpu.CompilerParams(vmem_limit_bytes=32 * MIB)


def run_after(kernel, count, after):
    extra = len(after)

    def ordered(*refs):
        kernel(*refs[:count], *refs[count + extra :])

    return ordered, [pl.BlockSpec(memory_space=pl.ANY)] * extra


def swap(value, axis, bit):
    size = lax.axis_size(axis)
    return lax.ppermute(value, axis, [(i, i ^ (1 << bit)) for i in range(size)])


def my_bit(axis, bit):
    return (lax.axis_index(axis) >> bit) & 1


def log_two(size):
    return size.bit_length() - 1


def gather_kernel(lanes, mine_ref, own_ref, other_ref, out_ref):
    mine = mine_ref[0]
    for which, source_ref in ((mine, own_ref), (1 - mine, other_ref)):
        if lanes:
            width = own_ref.shape[1]
            out_ref[:, pl.ds(pl.multiple_of(which * width, LANES), width)] = source_ref[...]
        else:
            for a in range(out_ref.shape[0]):
                out_ref[a, which] = source_ref[a]


def gate_kernel(value_ref, *refs):
    pass


def run_gate(value, *tokens):
    anywhere = pl.BlockSpec(memory_space=pl.ANY)
    return pl.pallas_call(
        gate_kernel,
        in_specs=[anywhere] * (1 + len(tokens)),
        out_specs=anywhere,
        out_shape=jax.ShapeDtypeStruct(value.shape, value.dtype),
        input_output_aliases={0: 0},
        name="gate",
    )(value, *tokens)


class Gather:
    def __init__(self, block):
        self.value = block
        self.bits = []
        self.pending = None

    def start(self, axis, bit):
        self.pending = (axis, bit, swap(self.value, axis, bit))
        return self.value

    def finish(self, after=()):
        axis, bit, other = self.pending
        rows, columns = self.value.shape
        lanes = axis == "mp"
        if lanes:
            shape, out = (rows, columns), (rows, 2 * columns)
        else:
            ahead = 2 ** sum(b > bit for b in self.bits)
            self.bits.append(bit)
            shape = (ahead, rows // ahead, columns)
            out = (ahead, 2, rows // ahead, columns)
        kernel, waits = run_after(lambda *refs: gather_kernel(lanes, *refs), 3, after)
        value = pl.pallas_call(
            kernel,
            in_specs=[SCALAR] + [FULL] * 2 + waits,
            out_specs=FULL,
            out_shape=jax.ShapeDtypeStruct(out, self.value.dtype),
            compiler_params=params(),
            cost_estimate=cost(0.1),
            name="gather_step",
        )(my_bit(axis, bit).reshape(1), self.value.reshape(shape), other.reshape(shape), *after)
        self.value = value.reshape(-1, value.shape[-1])
        return self.value

    def step(self, axis, bit, after=()):
        self.start(axis, bit)
        return self.finish(after)


def scatter_kernel(lanes, mine_ref, *refs):
    terms, (send_ref, keep_ref) = refs[:-2], refs[-2:]
    mine = mine_ref[0]
    for which, out_ref in ((1 - mine, send_ref), (mine, keep_ref)):
        if lanes:
            width = out_ref.shape[1]
            cols = pl.ds(pl.multiple_of(which * width, LANES), width)
            total = sum(term[:, cols].astype(f32) for term in terms)
            out_ref[...] = total.astype(out_ref.dtype)
        else:
            total = sum(term[0, which].astype(f32) for term in terms)
            out_ref[0] = total.astype(out_ref.dtype)


class Scatter:
    def __init__(self, *terms):
        self.bits = list(reversed(range(log_two(lax.axis_size("dp")))))
        self.terms = list(terms)
        self.send = None

    def step(self, axis, bit, kept_type=f32, after=()):
        rows, columns = self.terms[0].shape
        lanes = axis == "mp"
        if lanes:
            shape, half = (rows, columns), (rows, columns // 2)
            steps = max(rows // (LANES + CHUNK), 1)
            steps = next(k for k in range(steps, 0, -1) if rows % (k * CHUNK) == 0 or k == 1)
            block = lambda size: pl.BlockSpec((rows // steps, size[1]), lambda i: (i, 0))
        else:
            steps = 2 ** self.bits.index(bit)
            self.bits.remove(bit)
            shape = (steps, 2, rows // (2 * steps), columns)
            half = (steps, rows // (2 * steps), columns)
            block = lambda size: pl.BlockSpec(
                (1,) + size[1:], lambda i: (i,) + (0,) * (len(size) - 1)
            )
        count = len(self.terms)
        body_kernel = lambda *refs: scatter_kernel(lanes, *refs)
        kernel, waits = run_after(body_kernel, 1 + count, after)
        send, kept = pl.pallas_call(
            kernel,
            grid=(steps,),
            in_specs=[SCALAR] + [block(shape)] * count + waits,
            out_specs=[block(half)] * 2,
            out_shape=[jax.ShapeDtypeStruct(half, bf16), jax.ShapeDtypeStruct(half, kept_type)],
            compiler_params=params(),
            cost_estimate=cost(0.1),
            name="scatter_step",
        )(my_bit(axis, bit).reshape(1), *[term.reshape(shape) for term in self.terms], *after)
        flat = lambda value: value.reshape(-1, value.shape[-1])
        self.send = flat(send)
        self.terms = [flat(kept), swap(self.send, axis, bit)]
        return self.send

    def total(self):
        return sum(term.astype(f32) for term in self.terms)


def butterfly(value):
    def hop(value, moves):
        size = lax.axis_size("dp") * lax.axis_size("mp")
        get = lambda move: lax.ppermute(value, ("dp", "mp"), [(i, i ^ move) for i in range(size)])
        if len(moves) == 1:
            return value + get(moves[0])
        one, two = moves
        first, second, third = get(one), get(two), get(one | two)
        return (value + first) + (second + third)

    value = hop(value, (1,))
    bits = log_two(lax.axis_size("dp"))
    moves = [2] + [4 << bit for bit in range(bits)]
    for i in range(0, len(moves), 2):
        value = hop(value, tuple(moves[i : i + 2]))
    return value


def gelu_pair(value):
    square = value * value
    wave = jnp.tanh(value * (GELU_SCALE + (GELU_SCALE * GELU_CUBE) * square))
    half = 0.5 + 0.5 * wave
    inner = GELU_SCALE + (3.0 * GELU_SCALE * GELU_CUBE) * square
    return value * half, half + 0.5 * value * (1.0 - wave * wave) * inner


def norm_rows(x_ref, gain, shift, out_ref):
    @pl.loop(0, x_ref.shape[0] // CHUNK, unroll=13)
    def _(i):
        rows = pl.ds(pl.multiple_of(i * CHUNK, CHUNK), CHUNK)
        out_ref[rows, :] = layer_norm(x_ref[rows, :], gain, shift).astype(out_ref.dtype)


def norm_back_rows(x_ref, gain, grad_ref, extra_ref, out_ref, low_ref, sum_ref):
    sum_ref[...] = jnp.zeros_like(sum_ref)

    @pl.loop(0, x_ref.shape[0] // CHUNK, unroll=13)
    def _(i):
        rows = pl.ds(pl.multiple_of(i * CHUNK, CHUNK), CHUNK)
        value = x_ref[rows, :]
        grad = grad_ref[rows, :]
        center = value - jnp.mean(value, axis=-1, keepdims=True)
        scale = lax.rsqrt(jnp.mean(center * center, axis=-1, keepdims=True) + norm_eps)
        hat = center * scale
        for k, term in enumerate((grad * hat, grad)):
            sum_ref[8 * k : 8 * k + 8, :] += term[:8] + term[8:]
        pull = grad * gain
        mean_one = jnp.mean(pull, axis=-1, keepdims=True)
        mean_two = jnp.mean(pull * hat, axis=-1, keepdims=True)
        result = scale * (pull - mean_one - hat * mean_two)
        if extra_ref is not None:
            result = result + extra_ref[rows, :]
        out_ref[rows, :] = result
        low_ref[rows, :] = result.astype(bf16)


def gelu_blocks(width):
    return [slice(j, j + BLOCK) for j in range(0, width, BLOCK)]


def soft_rows(scores, column):
    scores = jnp.where(column < PATCHES, scores * HEAD_DIM ** (-0.5), -jnp.inf)
    top = jnp.max(scores, axis=-1, keepdims=True)
    weight = jnp.exp(scores - top)
    return weight * (1.0 / jnp.sum(weight, axis=-1, keepdims=True))


def enter_kernel(
    pixels_ref, stem_ref, embed_w_ref, token_ref, own_ref, other_ref,
    hidden_ref, slope_ref, embed_ref, normed_ref, tri_ref, ctx_ref,
):
    for cols in gelu_blocks(C_STEM):
        value, slope = gelu_pair(matmul(pixels_ref[...], stem_ref[:, cols]))
        hidden_ref[:, cols] = value.astype(bf16)
        slope_ref[:, cols] = slope.astype(bf16)
    slices = pixels_ref.shape[0] // PAD
    for cols in gelu_blocks(D):
        value = matmul(hidden_ref[...], embed_w_ref[:, cols])
        for s in range(slices):
            rows = slice(s * PAD, (s + 1) * PAD)
            embed_ref[rows, cols] = value[rows] + token_ref[:PAD, cols]
    gain, shift = token_ref[PATCHES : PATCHES + 1, :], token_ref[PATCHES + 1 : PATCHES + 2, :]
    norm_rows(embed_ref, gain, shift, normed_ref)
    width = tri_ref.shape[2]
    heads = width // (3 * HEAD_DIM)
    stride = width + width // 3
    column = lax.broadcasted_iota(jnp.int32, (PAD, PAD), 1)
    for p in range(tri_ref.shape[0]):
        start = (p % 2) * stride
        weight_ref = (own_ref, other_ref)[p // 2]
        tri_ref[p] = matmul(normed_ref[...], weight_ref[:, start : start + width]).astype(bf16)

    @pl.loop(0, tri_ref.shape[0])
    def _(p):
        for s in range(slices):
            rows = slice(s * PAD, (s + 1) * PAD)
            for h in range(heads):
                base = h * 3 * HEAD_DIM
                queries = tri_ref[p, rows, base : base + HEAD_DIM]
                keys_low = tri_ref[p, rows, base + HEAD_DIM : base + 2 * HEAD_DIM]
                values = tri_ref[p, rows, base + 2 * HEAD_DIM : base + 3 * HEAD_DIM]
                attend = soft_rows(matmul_t(queries, keys_low), column)
                context = matmul(attend.astype(bf16), values)
                ctx_ref[p, rows, h * HEAD_DIM : (h + 1) * HEAD_DIM] = context.astype(bf16)


def enter(pixels, stem_b, embed_b, tokens, attn_all, width):
    rows = pixels.shape[0]
    parts = 4
    return pl.pallas_call(
        enter_kernel,
        in_specs=[FULL] * 6,
        out_specs=[FULL] * 6,
        out_shape=[
            jax.ShapeDtypeStruct((rows, C_STEM), bf16),
            jax.ShapeDtypeStruct((rows, C_STEM), bf16),
            jax.ShapeDtypeStruct((rows, D), f32),
            jax.ShapeDtypeStruct((rows, D), bf16),
            jax.ShapeDtypeStruct((parts, rows, width), bf16),
            jax.ShapeDtypeStruct((parts, rows, width // 3), bf16),
        ],
        compiler_params=params(),
        cost_estimate=cost(13),
        name="enter",
    )(pixels, stem_b, embed_b, tokens, *attn_all)


def middle_kernel(
    ctx_ref, embed_ref, token_ref, own_ref, other_ref, mlp_ref,
    resid_ref, normed2_ref, slope_ref, inner_ref, resid2_ref, final_ref,
):
    p = pl.program_id(0)

    @pl.when(p == 0)
    def _():
        part = ctx_ref.shape[2]
        stride = 4 * part
        for q in range(ctx_ref.shape[0]):
            start = (q % 2) * stride + 3 * part
            weight_ref = (own_ref, other_ref)[q // 2]
            term = matmul_t(ctx_ref[q], weight_ref[:, start : start + part])
            if q == 0:
                resid_ref[...] = embed_ref[...] + term
            else:
                resid_ref[...] += term
        gain, shift = token_ref[PATCHES + 2 : PATCHES + 3, :], token_ref[PATCHES + 3 : PATCHES + 4, :]
        norm_rows(resid_ref, gain, shift, normed2_ref)
        resid2_ref[...] = resid_ref[...]

    each = mlp_ref.shape[2] // 2
    for cols in gelu_blocks(each):
        value, slope = gelu_pair(matmul(normed2_ref[...], mlp_ref[0, :, cols]))
        inner_ref[0, :, cols] = value.astype(bf16)
        slope_ref[0, :, cols] = slope.astype(bf16)
    resid2_ref[...] += matmul_t(inner_ref[0], mlp_ref[0, :, each:])

    @pl.when(p == pl.num_programs(0) - 1)
    def _():
        gain, shift = token_ref[PATCHES + 4 : PATCHES + 5, :], token_ref[PATCHES + 5 : PATCHES + 6, :]
        norm_rows(resid2_ref, gain, shift, final_ref)


def whole_of(value):
    return pl.BlockSpec(value.shape, lambda *_: (0,) * len(value.shape))


def part_of(value):
    rest = len(value.shape) - 1
    return pl.BlockSpec((1,) + tuple(value.shape[1:]), lambda i, *_: (i,) + (0,) * rest)


def middle(context, embed, tokens, attn_all, mlp_all):
    rows = embed.shape[0]
    parts, _, width = mlp_all.shape
    each = width // 2
    outs = [
        jax.ShapeDtypeStruct((rows, D), f32),
        jax.ShapeDtypeStruct((rows, D), bf16),
        jax.ShapeDtypeStruct((parts, rows, each), bf16),
        jax.ShapeDtypeStruct((parts, rows, each), bf16),
        jax.ShapeDtypeStruct((rows, D), f32),
        jax.ShapeDtypeStruct((rows, D), bf16),
    ]
    values = (context, embed, tokens, *attn_all)
    return pl.pallas_call(
        middle_kernel,
        grid=(parts,),
        in_specs=[whole_of(value) for value in values] + [part_of(mlp_all)],
        out_specs=[(part_of if len(out.shape) == 3 else whole_of)(out) for out in outs],
        out_shape=outs,
        compiler_params=params(),
        cost_estimate=cost(13),
        name="middle",
    )(*values, mlp_all)


def class_probs(logits_ref, rows, group):
    width = CLASSES * LANES
    values = [
        logits_ref[rows, group * width + c * LANES : group * width + (c + 1) * LANES]
        for c in range(CLASSES)
    ]
    top = values[0]
    for value in values[1:]:
        top = jnp.maximum(top, value)
    weights = [jnp.exp(value - top) for value in values]
    total = weights[0]
    for weight in weights[1:]:
        total = total + weight
    scale = 1.0 / total
    return values, [weight * scale for weight in weights], top + jnp.log(total)


SPLIT_A = 4 * CHAN_B
SPLIT_B = SPLIT_A + 16 * CHAN_C
SKIPW = SPLIT_B + 64 * CHAN_D


def leave_kernel(
    core_ref, hidden_ref, final_ref, skip_own_ref, skip_other_ref, dec_ref, one_ref, two_ref, three_ref, head_ref, label_ref,
    slope0_ref, level0_ref, slope_ref, level1_ref, level2_ref, level3_ref, logits_ref, stats_ref,
    skips,
):
    value, slope = gelu_pair(matmul(final_ref[...], dec_ref[...]))
    level0_ref[...] = value.astype(bf16)
    slope0_ref[...] = slope

    half = skip_own_ref.shape[1]
    core = core_ref[0]
    for which, weight_ref in ((core, skip_own_ref), (1 - core, skip_other_ref)):
        for j in range(0, half, BLOCK):
            cols = pl.ds(pl.multiple_of(which * half + j, LANES), BLOCK)
            skips[:, cols] = matmul(hidden_ref[...], weight_ref[:, j : j + BLOCK])

    def stage(source, weight, out_ref, cols, skip_cols):
        pre = matmul(source, weight) + skips[:, skip_cols : skip_cols + BLOCK]
        value, slope = gelu_pair(pre)
        out_ref[:, cols : cols + BLOCK] = value.astype(bf16)
        slope_ref[:, skip_cols : skip_cols + BLOCK] = slope.astype(bf16)

    for i in range(2):
        stage(level0_ref[...], one_ref[:, i * BLOCK : (i + 1) * BLOCK], level1_ref, i * BLOCK, i * BLOCK)
    for i in range(4):
        stage(
            level1_ref[:, i * CHAN_B : (i + 1) * CHAN_B], two_ref[...], level2_ref, i * BLOCK,
            SPLIT_A + i * BLOCK,
        )
    for i in range(4):
        stage(
            level2_ref[:, i * BLOCK : (i + 1) * BLOCK], three_ref[...], level3_ref, i * BLOCK,
            SPLIT_B + i * BLOCK,
        )
    inner = head_ref.shape[0]
    width = head_ref.shape[1]
    groups = level3_ref.shape[1] // inner
    for g in range(groups):
        logits_ref[:, g * width : (g + 1) * width] = matmul(
            level3_ref[:, g * inner : (g + 1) * inner], head_ref[...]
        )
    stats_ref[...] = jnp.zeros_like(stats_ref)
    slices = stats_ref.shape[0]
    per_slice = PAD // CHUNK

    @pl.loop(0, slices)
    def _(s):
        @pl.loop(0, per_slice)
        def _(i):
            start = pl.multiple_of(s * PAD + i * CHUNK, CHUNK)
            rows = pl.ds(start, CHUNK)
            row_id = lax.broadcasted_iota(jnp.int32, (CHUNK, LANES), 0) + i * CHUNK
            inside = (row_id < PATCHES).astype(f32)
            for g in range(groups):
                values, probs, log_total = class_probs(logits_ref, rows, g)
                label = label_ref[rows, g * LANES : (g + 1) * LANES]
                cross = jnp.zeros((CHUNK, LANES), f32)
                for c in range(CLASSES):
                    hot = (label == c).astype(f32)
                    cross = cross + hot * (log_total - values[c])
                    for k, term in enumerate((hot * probs[c], inside * probs[c], hot)):
                        spot = 8 * (3 * c + k)
                        stats_ref[s, spot : spot + 8, :] += term[:8] + term[8:]
                spot = 8 * 3 * CLASSES
                stats_ref[s, spot : spot + 8, :] += cross[:8] + cross[8:]


def leave(core, hidden, final_low, skip_all, dec_b, one_b, two_b, three_four, big_head, labels):
    rows = hidden.shape[0]
    slices = rows // PAD
    stat_rows = 8 * (3 * CLASSES + 1)
    return pl.pallas_call(
        leave_kernel,
        in_specs=[SCALAR] + [FULL] * 10,
        out_specs=[FULL] * 8,
        out_shape=[
            jax.ShapeDtypeStruct((rows, CHAN_A), f32),
            jax.ShapeDtypeStruct((rows, CHAN_A), bf16),
            jax.ShapeDtypeStruct((rows, SKIPW), bf16),
            jax.ShapeDtypeStruct((rows, 4 * CHAN_B), bf16),
            jax.ShapeDtypeStruct((rows, 16 * CHAN_C), bf16),
            jax.ShapeDtypeStruct((rows, 64 * CHAN_D), bf16),
            jax.ShapeDtypeStruct((rows, CLASSES * PIXELS), f32),
            jax.ShapeDtypeStruct((slices, stat_rows, LANES), f32),
        ],
        scratch_shapes=[pltpu.VMEM((rows, SKIPW), f32)],
        compiler_params=params(),
        cost_estimate=cost(12),
        name="leave",
    )(core, hidden, final_low, *skip_all, dec_b, one_b, two_b, three_four, big_head, labels)


def leave_back_kernel(
    coef_ref, logits_ref, label_ref, slope_ref, head_ref, three_ref, two_ref,
    g_logits_ref, g_skips_ref,
):
    inner = head_ref.shape[0]
    width = head_ref.shape[1]
    groups = 64 * CHAN_D // inner
    slices = logits_ref.shape[0] // PAD

    @pl.loop(0, slices)
    def _(s):
        cross_scale = coef_ref[s, 2 * CLASSES]

        @pl.loop(0, PAD // CHUNK)
        def _(i):
            start = pl.multiple_of(s * PAD + i * CHUNK, CHUNK)
            rows = pl.ds(start, CHUNK)
            row_id = lax.broadcasted_iota(jnp.int32, (CHUNK, LANES), 0) + i * CHUNK
            inside = (row_id < PATCHES).astype(f32)
            for g in range(groups):
                _, probs, _ = class_probs(logits_ref, rows, g)
                label = label_ref[rows, g * LANES : (g + 1) * LANES]
                mean = jnp.zeros((CHUNK, LANES), f32)
                pulls = []
                for c in range(CLASSES):
                    pull = jnp.where(label == c, coef_ref[s, c], 0.0) + coef_ref[s, CLASSES + c]
                    pulls.append(pull)
                    mean = mean + probs[c] * pull
                mean = mean - cross_scale
                for c in range(CLASSES):
                    grad = probs[c] * (pulls[c] - mean)
                    grad = grad - jnp.where(label == c, cross_scale, 0.0)
                    spot = g * width + c * LANES
                    g_logits_ref[rows, spot : spot + LANES] = (grad * inside).astype(bf16)

    for i in range(4):
        g, part = (i * BLOCK) // inner, (i * BLOCK) % inner
        grad = matmul_t(g_logits_ref[:, g * width : (g + 1) * width], head_ref[part : part + BLOCK, :])
        cols = slice(SPLIT_B + i * BLOCK, SPLIT_B + (i + 1) * BLOCK)
        g_skips_ref[:, cols] = (grad * slope_ref[:, cols].astype(f32)).astype(bf16)
    for i in range(4):
        source = g_skips_ref[:, SPLIT_B + i * BLOCK : SPLIT_B + (i + 1) * BLOCK]
        cols = slice(SPLIT_A + i * BLOCK, SPLIT_A + (i + 1) * BLOCK)
        g_skips_ref[:, cols] = (matmul_t(source, three_ref[...]) * slope_ref[:, cols].astype(f32)).astype(bf16)
    for i in range(4):
        source = g_skips_ref[:, SPLIT_A + i * BLOCK : SPLIT_A + (i + 1) * BLOCK]
        cols = slice(i * CHAN_B, (i + 1) * CHAN_B)
        g_skips_ref[:, cols] = (matmul_t(source, two_ref[...]) * slope_ref[:, cols].astype(f32)).astype(bf16)


def leave_back(coef, logits, labels, slope, big_head, three_four, two_b):
    rows = logits.shape[0]
    return pl.pallas_call(
        leave_back_kernel,
        in_specs=[SCALAR] + [FULL] * 6,
        out_specs=[FULL] * 2,
        out_shape=[
            jax.ShapeDtypeStruct((rows, CLASSES * PIXELS), bf16),
            jax.ShapeDtypeStruct((rows, SKIPW), bf16),
        ],
        compiler_params=params(),
        cost_estimate=cost(6),
        name="leave_back",
    )(coef, logits, labels, slope, big_head, three_four, two_b)


def skip_grad_kernel(core_ref, hidden_ref, g_skips_ref, send_ref, keep_ref):
    half = send_ref.shape[1]
    core = core_ref[0]
    for which, out_ref in ((1 - core, send_ref), (core, keep_ref)):
        for j in range(0, half, half // 2):
            cols = pl.ds(pl.multiple_of(which * half + j, LANES), half // 2)
            out_ref[:, j : j + half // 2] = t_matmul(hidden_ref[...], g_skips_ref[:, cols]).astype(
                bf16
            )


def skip_grad(core, hidden, g_skips):
    shape = (hidden.shape[1], g_skips.shape[1] // 2)
    return pl.pallas_call(
        skip_grad_kernel,
        in_specs=[SCALAR] + [FULL] * 2,
        out_specs=[FULL] * 2,
        out_shape=[jax.ShapeDtypeStruct(shape, bf16)] * 2,
        compiler_params=params(),
        cost_estimate=cost(3.5),
        name="skip_grad",
    )(core, hidden, g_skips)


def turn_kernel(
    g_skips_ref, one_ref, slope0_ref, dec_ref, resid2_ref, token_ref,
    g_pre0_ref, g_resid2_ref, low_ref, sums_ref, g_final,
):
    grad = matmul_t(g_skips_ref[:, :SPLIT_A], one_ref[...])
    g_pre0_ref[...] = (grad * slope0_ref[...]).astype(bf16)
    g_final[...] = matmul_t(g_pre0_ref[...], dec_ref[...])
    norm_back_rows(
        resid2_ref, token_ref[PATCHES + 4 : PATCHES + 5, :], g_final, None, g_resid2_ref, low_ref, sums_ref
    )


def turn(g_skips, one_b, slope0, dec_b, resid2, tokens, after=()):
    rows = resid2.shape[0]
    kernel, waits = run_after(turn_kernel, 6, after)
    return pl.pallas_call(
        kernel,
        in_specs=[FULL] * 6 + waits,
        out_specs=[FULL] * 4,
        out_shape=[
            jax.ShapeDtypeStruct((rows, CHAN_A), bf16),
            jax.ShapeDtypeStruct((rows, D), f32),
            jax.ShapeDtypeStruct((rows, D), bf16),
            jax.ShapeDtypeStruct((16, D), f32),
        ],
        scratch_shapes=[pltpu.VMEM((rows, D), f32)],
        compiler_params=params(),
        cost_estimate=cost(3),
        name="turn",
    )(g_skips, one_b, slope0, dec_b, resid2, tokens, *after)


FLAT_DEC = D * CHAN_A // LANES
FLAT_ONE = FLAT_DEC + CHAN_A * 4 * CHAN_B // LANES
FLAT_TWO = FLAT_ONE + CHAN_B * 4 * CHAN_C // LANES
FLAT_THREE = FLAT_TWO + CHAN_C * 4 * CHAN_D // LANES


def decoder_grad_kernel(
    level3_ref, g_logits_ref, level2_ref, level1_ref, g_skips_ref, level0_ref, final_ref, g_pre0_ref,
    out_ref, flat_ref, square_ref,
):
    size = out_ref.shape[1]
    flat = (FLAT_THREE * LANES + 4 * CLASSES * CHAN_D) // size
    inner, width = GROUP * CHAN_D, CLASSES * LANES
    tail = flat_ref.shape[0] - FLAT_THREE
    flat_ref[FLAT_THREE:, :] = jnp.zeros((tail, LANES), f32)

    def spread(value, base, count):
        for j in range(count):
            flat_ref[pl.ds(base + j, value.shape[0], stride=count), :] = value[
                :, j * LANES : (j + 1) * LANES
            ]

    spread(t_matmul(final_ref[...], g_pre0_ref[...]), 0, CHAN_A // LANES)
    spread(t_matmul(level0_ref[...], g_skips_ref[:, :SPLIT_A]), FLAT_DEC, SPLIT_A // LANES)
    three = jnp.zeros((CHAN_C, 4 * CHAN_D), f32)
    two = jnp.zeros((CHAN_B, 4 * CHAN_C), f32)
    for i in range(4):
        big = t_matmul(
            level2_ref[:, i * BLOCK : (i + 1) * BLOCK],
            g_skips_ref[:, SPLIT_B + i * BLOCK : SPLIT_B + (i + 1) * BLOCK],
        )
        for k in range(4):
            at = slice(k * CHAN_C, (k + 1) * CHAN_C)
            three += big[at, at]
        two += t_matmul(
            level1_ref[:, i * CHAN_B : (i + 1) * CHAN_B],
            g_skips_ref[:, SPLIT_A + i * BLOCK : SPLIT_A + (i + 1) * BLOCK],
        )
    spread(two, FLAT_ONE, 4 * CHAN_C // LANES)
    square_ref[...] = three
    flat_ref[FLAT_TWO:FLAT_THREE, :] = jnp.concatenate(
        [square_ref[pl.ds(j, CHAN_C // 2, stride=2), :] for j in range(2)], axis=1
    )
    head = jnp.zeros((CHAN_D, width), f32)
    row = lax.broadcasted_iota(jnp.int32, (CHAN_D, width), 0)
    across = lax.broadcasted_iota(jnp.int32, (CHAN_D, width), 1)
    parent = (across // 4) % GROUP
    for g in range(level3_ref.shape[1] // inner):
        big = t_matmul(
            level3_ref[:, g * inner : (g + 1) * inner], g_logits_ref[:, g * width : (g + 1) * width]
        )
        for k in range(GROUP):
            head += jnp.where(parent == k, big[k * CHAN_D : (k + 1) * CHAN_D, :], 0.0)
    column = lax.broadcasted_iota(jnp.int32, (width, LANES), 0)
    target = lax.broadcasted_iota(jnp.int32, (width, LANES), 1)
    pick = target == (column % 4) * CLASSES + column // (GROUP * 4)
    small = jnp.dot(head, pick.astype(f32), precision=highest, preferred_element_type=f32)
    lane = lax.broadcasted_iota(jnp.int32, (1, LANES), 1)
    lines = [jnp.zeros((1, LANES), f32) for _ in range(8)]
    for k in range(CHAN_D):
        line, start = divmod(k * 4 * CLASSES, LANES)
        value = small[k : k + 1, :]
        if start:
            value = pltpu.roll(value, start, 1)
        lines[line] = lines[line] + jnp.where(lane >= start, value, 0.0)
        if start + 4 * CLASSES > LANES:
            lines[line + 1] = lines[line + 1] + jnp.where(
                lane < start + 4 * CLASSES - LANES, value, 0.0
            )
    flat_ref[FLAT_THREE : FLAT_THREE + 8, :] = jnp.concatenate(lines, axis=0)

    rows = out_ref.shape[2]
    line_id = lax.broadcasted_iota(jnp.int32, (rows, LANES), 0)
    lane_id = lax.broadcasted_iota(jnp.int32, (rows, LANES), 1)
    for d in range(size):
        for c in range(2):
            first, start = divmod(d * flat + c * rows * LANES, LANES)
            value = flat_ref[first : first + rows, :]
            if start:
                after = flat_ref[first + 1 : first + 1 + rows, :]
                value = jnp.where(
                    lane_id < LANES - start,
                    pltpu.roll(value, LANES - start, 1),
                    pltpu.roll(after, LANES - start, 1),
                )
            inside = (line_id + c * rows) * LANES + lane_id < flat
            out_ref[c, d] = jnp.where(inside, value, 0.0).astype(bf16)


def decoder_grad(
    level3, g_logits, level2, level1, g_skips, level0, final_low, g_pre0, size, rows, after=()
):
    kernel, waits = run_after(decoder_grad_kernel, 8, after)
    flat = (FLAT_THREE * LANES + 4 * CLASSES * CHAN_D) // size
    lines = (size - 1) * flat // LANES + 2 * rows + 8
    lines = -(-max(lines, FLAT_THREE + 8) // 8) * 8
    return pl.pallas_call(
        kernel,
        in_specs=[FULL] * 8 + waits,
        out_specs=FULL,
        out_shape=jax.ShapeDtypeStruct((2, size, rows, LANES), bf16),
        scratch_shapes=[pltpu.VMEM((lines, LANES), f32), pltpu.VMEM((CHAN_C, 4 * CHAN_D), f32)],
        compiler_params=params(),
        cost_estimate=cost(3),
        name="decoder_grad",
    )(level3, g_logits, level2, level1, g_skips, level0, final_low, g_pre0, *after)


def first_grad_kernel(
    core_ref, pixels_ref, g_stem_ref, hidden_ref, low_ref, pos_ref, sums1_ref, sums2_ref, sumsf_ref,
    dec_ref, send_ref, keep_ref, token_ref,
):
    core = core_ref[0]
    size = send_ref.shape[0]
    stem_rows, embed_rows, token_rows = PIXELS // size, C_STEM // size, D // size
    token_ref[...] = jnp.zeros_like(token_ref)
    token_ref[:PATCHES, :] = pos_ref[:PATCHES, :]
    for i, sums_ref in enumerate((sums1_ref, sums2_ref, sumsf_ref)):
        for k in range(2):
            at = PATCHES + 2 * i + k
            token_ref[at : at + 1, :] = jnp.sum(
                sums_ref[8 * k : 8 * k + 8, :], axis=0, keepdims=True
            )
    for which, out_ref in ((1 - core, send_ref), (core, keep_ref)):
        spot = 0
        half = C_STEM // 2
        for j in range(0, half, BLOCK):
            cols = pl.ds(pl.multiple_of(which * half + j, LANES), BLOCK)
            part = t_matmul(pixels_ref[...], g_stem_ref[:, cols]).astype(bf16)
            for k in range(0, BLOCK, LANES):
                for d in range(size):
                    out_ref[d, spot : spot + stem_rows, :] = part[
                        d * stem_rows : (d + 1) * stem_rows, k : k + LANES
                    ]
                spot += stem_rows
        half = D // 2
        cols = pl.ds(pl.multiple_of(which * half, LANES), half)
        part = t_matmul(hidden_ref[...], low_ref[:, cols]).astype(bf16)
        for k in range(0, half, LANES):
            for d in range(size):
                out_ref[d, spot : spot + embed_rows, :] = part[
                    d * embed_rows : (d + 1) * embed_rows, k : k + LANES
                ]
            spot += embed_rows
        turned = token_ref[pl.ds(pl.multiple_of(which * LANES, LANES), LANES), :].T.astype(bf16)
        for d in range(size):
            out_ref[d, spot : spot + token_rows, :] = turned[d * token_rows : (d + 1) * token_rows]
            out_ref[d, spot + token_rows :, :] = dec_ref[which, d]


def first_grad(core, pixels, g_stem, hidden, low, pos, sums1, sums2, sumsf, dec, rows, after=()):
    kernel, waits = run_after(first_grad_kernel, 10, after)
    shape = (dec.shape[1], rows, LANES)
    return pl.pallas_call(
        kernel,
        in_specs=[SCALAR] + [FULL] * 9 + waits,
        out_specs=[FULL] * 2,
        out_shape=[jax.ShapeDtypeStruct(shape, bf16)] * 2,
        scratch_shapes=[pltpu.VMEM((2 * LANES, D), f32)],
        compiler_params=params(),
        cost_estimate=cost(2),
        name="first_grad",
    )(core, pixels, g_stem, hidden, low, pos, sums1, sums2, sumsf, dec, *after)


def unpack_kernel(core_ref, own_ref, other_ref, stem_ref, embed_ref, token_ref, turned_ref):
    core = core_ref[0]
    size = own_ref.shape[0]
    stem_rows, embed_rows, token_rows = PIXELS // size, C_STEM // size, D // size
    for which, block_ref in ((core, own_ref), (1 - core, other_ref)):
        spot = 0
        for target_ref, rows, half in (
            (stem_ref, stem_rows, C_STEM // 2),
            (embed_ref, embed_rows, D // 2),
            (turned_ref, token_rows, LANES),
        ):
            for k in range(0, half, LANES):
                cols = pl.ds(pl.multiple_of(which * half + k, LANES), LANES)
                for d in range(size):
                    target_ref[d * rows : (d + 1) * rows, cols] = block_ref[
                        d, spot : spot + rows, :
                    ].astype(target_ref.dtype)
                spot += rows
    token_ref[...] = turned_ref[...].T


def unpack(core, own, other):
    return pl.pallas_call(
        unpack_kernel,
        in_specs=[SCALAR] + [FULL] * 2,
        out_specs=[FULL] * 3,
        out_shape=[
            jax.ShapeDtypeStruct((PIXELS, C_STEM), bf16),
            jax.ShapeDtypeStruct((C_STEM, D), bf16),
            jax.ShapeDtypeStruct((2 * LANES, D), f32),
        ],
        scratch_shapes=[pltpu.VMEM((D, 2 * LANES), f32)],
        compiler_params=params(),
        cost_estimate=cost(3),
        name="unpack",
    )(core, own, other)


def pack_kernel(core_ref, stem_ref, embed_ref, token_ref, dec_ref, out_ref):
    core = core_ref[0]
    spot = 0
    for source_ref in (stem_ref, embed_ref, token_ref):
        rows, half = source_ref.shape[0], source_ref.shape[1] // 2
        for k in range(0, half, LANES):
            cols = pl.ds(pl.multiple_of(core * half + k, LANES), LANES)
            out_ref[spot : spot + rows, :] = source_ref[:, cols].astype(bf16)
            spot += rows
    out_ref[spot:, :] = dec_ref[core].astype(bf16)


def pack(core, stem_w, embed_w, token_t, dec, rows):
    return pl.pallas_call(
        pack_kernel,
        in_specs=[SCALAR] + [FULL] * 4,
        out_specs=FULL,
        out_shape=jax.ShapeDtypeStruct((rows, LANES), bf16),
        compiler_params=params(),
        cost_estimate=cost(2),
        name="pack",
    )(core, stem_w, embed_w, token_t, dec)


def middle_back_kernel(
    low2_ref, mlp_ref, slope_ref, resid_ref, token_ref, g_resid2_ref, own_ref, other_ref,
    g_pre_ref, g_resid_ref, low_ref, g_ctx_ref, sums_ref, g_normed,
):
    p = pl.program_id(0)
    each = mlp_ref.shape[2] // 2
    for cols in gelu_blocks(each):
        down = mlp_ref[0, :, each + cols.start : each + cols.stop]
        grad = matmul(low2_ref[...], down) * slope_ref[0, :, cols].astype(f32)
        g_pre_ref[0, :, cols] = grad.astype(bf16)
    term = matmul_t(g_pre_ref[0], mlp_ref[0, :, :each])

    @pl.when(p == 0)
    def _():
        g_normed[...] = term

    @pl.when(p > 0)
    def _():
        g_normed[...] += term

    @pl.when(p == pl.num_programs(0) - 1)
    def _():
        norm_back_rows(
            resid_ref, token_ref[PATCHES + 2 : PATCHES + 3, :], g_normed, g_resid2_ref,
            g_resid_ref, low_ref, sums_ref,
        )
        part = g_ctx_ref.shape[2]
        for q in range(g_ctx_ref.shape[0]):
            start = (q % 2) * 4 * part + 3 * part
            weight_ref = (own_ref, other_ref)[q // 2]
            g_ctx_ref[q] = matmul(low_ref[...], weight_ref[:, start : start + part]).astype(bf16)


def middle_back(low2, mlp_all, slope, resid, tokens, g_resid2, attn_all, after=()):
    kernel, waits = run_after(middle_back_kernel, 8, after)
    rows = resid.shape[0]
    parts, _, each = slope.shape
    part = attn_all[0].shape[1] // 8
    outs = [
        jax.ShapeDtypeStruct((parts, rows, each), bf16),
        jax.ShapeDtypeStruct((rows, D), f32),
        jax.ShapeDtypeStruct((rows, D), bf16),
        jax.ShapeDtypeStruct((parts, rows, part), bf16),
        jax.ShapeDtypeStruct((16, D), f32),
    ]
    values = (resid, tokens, g_resid2, *attn_all)
    return pl.pallas_call(
        kernel,
        grid=(parts,),
        in_specs=[whole_of(low2), part_of(mlp_all), part_of(slope)]
        + [whole_of(value) for value in values]
        + waits,
        out_specs=[part_of(outs[0])] + [whole_of(out) for out in outs[1:]],
        out_shape=outs,
        scratch_shapes=[pltpu.VMEM((rows, D), f32)],
        compiler_params=params(),
        cost_estimate=cost(11),
        name="middle_back",
    )(low2, mlp_all, slope, *values, *after)


def half_grad_kernel(core_ref, left_ref, right_ref, send_ref, keep_ref):
    core = core_ref[0]
    each = right_ref.shape[2]
    for which, out_ref in ((1 - core, send_ref), (core, keep_ref)):
        for x in range(2):
            out_ref[:, x * each : (x + 1) * each] = t_matmul(
                left_ref[...], right_ref[2 * x + which]
            ).astype(bf16)


def half_grad(core, left, right, after=()):
    kernel, waits = run_after(half_grad_kernel, 3, after)
    shape = (left.shape[1], 2 * right.shape[2])
    return pl.pallas_call(
        kernel,
        in_specs=[SCALAR] + [FULL] * 2 + waits,
        out_specs=[FULL] * 2,
        out_shape=[jax.ShapeDtypeStruct(shape, bf16)] * 2,
        compiler_params=params(),
        cost_estimate=cost(2.7),
        name="half_grad",
    )(core, left, right, *after)


def attn_back_kernel(tri_ref, g_ctx_ref, g_tri_ref):
    slices = tri_ref.shape[1] // PAD
    heads = tri_ref.shape[2] // (3 * HEAD_DIM)
    column = lax.broadcasted_iota(jnp.int32, (PAD, PAD), 1)
    for s in range(slices):
        rows = slice(s * PAD, (s + 1) * PAD)
        for h in range(heads):
            base = h * 3 * HEAD_DIM
            queries = tri_ref[0, rows, base : base + HEAD_DIM]
            keys_low = tri_ref[0, rows, base + HEAD_DIM : base + 2 * HEAD_DIM]
            values = tri_ref[0, rows, base + 2 * HEAD_DIM : base + 3 * HEAD_DIM]
            gctx = g_ctx_ref[0, rows, h * HEAD_DIM : (h + 1) * HEAD_DIM]
            attend = soft_rows(matmul_t(queries, keys_low), column)
            g_attend = matmul_t(gctx, values)
            g_values = t_matmul(attend.astype(bf16), gctx)
            inner = jnp.sum(attend * g_attend, axis=-1, keepdims=True)
            g_scores = attend * (g_attend - inner) * HEAD_DIM ** (-0.5)
            g_low = g_scores.astype(bf16)
            g_tri_ref[0, rows, base : base + HEAD_DIM] = matmul(g_low, keys_low).astype(bf16)
            g_tri_ref[0, rows, base + HEAD_DIM : base + 2 * HEAD_DIM] = t_matmul(
                g_low, queries
            ).astype(bf16)
            g_tri_ref[0, rows, base + 2 * HEAD_DIM : base + 3 * HEAD_DIM] = g_values.astype(bf16)


def attn_back(triple, g_ctx, after=()):
    parts, rows, width = triple.shape
    whole = lambda size: pl.BlockSpec((1, rows, size), lambda i: (i, 0, 0))
    kernel, waits = run_after(attn_back_kernel, 2, after)
    return pl.pallas_call(
        kernel,
        grid=(parts,),
        in_specs=[whole(width), whole(width // 3)] + waits,
        out_specs=whole(width),
        out_shape=jax.ShapeDtypeStruct(triple.shape, bf16),
        compiler_params=params(),
        cost_estimate=cost(13.5),
        name="attn_back",
    )(triple, g_ctx, *after)


def attn_grad_kernel(normed_ref, g_tri_ref, low_ref, ctx_ref, send_ref, keep_ref):
    width = g_tri_ref.shape[2]
    stride = width + width // 3
    for which, out_ref in ((1, send_ref), (0, keep_ref)):
        for x in range(2):
            part = 2 * which + x
            at = x * stride
            out_ref[:, at : at + width] = t_matmul(normed_ref[...], g_tri_ref[part]).astype(
                out_ref.dtype
            )
            out_ref[:, at + width : at + stride] = t_matmul(low_ref[...], ctx_ref[part]).astype(
                out_ref.dtype
            )


def attn_grad(normed, g_tri, low, context, after=()):
    shape = (D, 2 * (g_tri.shape[2] + context.shape[2]))
    kernel, waits = run_after(attn_grad_kernel, 4, after)
    return pl.pallas_call(
        kernel,
        in_specs=[FULL] * 4 + waits,
        out_specs=[FULL] * 2,
        out_shape=[jax.ShapeDtypeStruct(shape, bf16)] * 2,
        compiler_params=params(),
        cost_estimate=cost(3.6),
        name="attn_grad",
    )(normed, g_tri, low, context, *after)


def enter_back_kernel(
    core_ref, g_tri_ref, own_ref, other_ref, embed_ref, token_ref, g_resid_ref, embed_w_ref,
    g_skips_ref, skip_own_ref, skip_other_ref, slope_ref, low_ref, g_stem_ref, g_pos_ref, sums_ref, g_normed, g_embed,
):
    width = g_tri_ref.shape[2]
    stride = width + width // 3
    for p in range(g_tri_ref.shape[0]):
        start = (p % 2) * stride
        weight_ref = (own_ref, other_ref)[p // 2]
        term = matmul_t(g_tri_ref[p], weight_ref[:, start : start + width])
        if p == 0:
            g_normed[...] = term
        else:
            g_normed[...] += term
    norm_back_rows(
        embed_ref, token_ref[PATCHES : PATCHES + 1, :], g_normed, g_resid_ref, g_embed, low_ref, sums_ref
    )
    pos = g_embed[:PAD, :]
    for s in range(1, embed_ref.shape[0] // PAD):
        pos = pos + g_embed[s * PAD : (s + 1) * PAD, :]
    g_pos_ref[...] = pos
    half = skip_own_ref.shape[1]
    core = core_ref[0]
    for cols in gelu_blocks(C_STEM):
        grad = matmul_t(low_ref[...], embed_w_ref[cols, :])
        for which, weight_ref in ((core, skip_own_ref), (1 - core, skip_other_ref)):
            part = pl.ds(pl.multiple_of(which * half, LANES), half)
            grad += matmul_t(g_skips_ref[:, part], weight_ref[cols, :])
        g_stem_ref[:, cols] = (grad * slope_ref[:, cols].astype(f32)).astype(bf16)


def enter_back(core, g_tri, attn_all, embed, tokens, g_resid, embed_b, g_skips, skip_all, slope, after=()):
    rows = embed.shape[0]
    kernel, waits = run_after(enter_back_kernel, 12, after)
    return pl.pallas_call(
        kernel,
        in_specs=[SCALAR] + [FULL] * 11 + waits,
        out_specs=[FULL] * 4,
        out_shape=[
            jax.ShapeDtypeStruct((rows, D), bf16),
            jax.ShapeDtypeStruct((rows, C_STEM), bf16),
            jax.ShapeDtypeStruct((PAD, D), f32),
            jax.ShapeDtypeStruct((16, D), f32),
        ],
        scratch_shapes=[pltpu.VMEM((rows, D), f32), pltpu.VMEM((rows, D), f32)],
        compiler_params=params(),
        cost_estimate=cost(10.4),
        name="enter_back",
    )(core, g_tri, *attn_all, embed, tokens, g_resid, embed_b, g_skips, *skip_all, slope, *after)


def split_decoder(flat):
    edge_one = D * CHAN_A
    edge_two = edge_one + CHAN_A * 4 * CHAN_B
    edge_three = edge_two + CHAN_B * 4 * CHAN_C
    edge_four = edge_three + CHAN_C * 4 * CHAN_D
    return (
        flat[:edge_one].reshape(D, CHAN_A),
        flat[edge_one:edge_two].reshape(CHAN_A, 4 * CHAN_B),
        flat[edge_two:edge_three].reshape(CHAN_B, 4 * CHAN_C),
        flat[edge_three:edge_four].reshape(CHAN_C, 4 * CHAN_D),
        flat[edge_four:].reshape(CHAN_D, 4 * CLASSES),
    )


def same_block(rows, columns, inner, outer):
    row = lax.broadcasted_iota(jnp.int32, (rows, columns), 0) // inner
    column = lax.broadcasted_iota(jnp.int32, (rows, columns), 1) // outer
    return row == column


def block_diag(weight, parents):
    inner, outer = weight.shape
    mask = same_block(parents * inner, parents * outer, inner, outer)
    tiled = jnp.tile(weight, (parents, parents))
    return jnp.where(mask, tiled, jnp.zeros_like(tiled))


def head_masks():
    wide = CLASSES * GROUP * 4
    column = lax.broadcasted_iota(jnp.int32, (4 * CLASSES, wide), 1)
    source = lax.broadcasted_iota(jnp.int32, (4 * CLASSES, wide), 0)
    pick = source == (column % 4) * CLASSES + column // (GROUP * 4)
    row = lax.broadcasted_iota(jnp.int32, (GROUP * CHAN_D, wide), 0)
    across = lax.broadcasted_iota(jnp.int32, (GROUP * CHAN_D, wide), 1)
    mask = row // CHAN_D == (across // 4) % GROUP
    return pick, mask


def big_head_of(head_b):
    pick, mask = head_masks()
    spread = matmul(head_b, pick.astype(bf16)).astype(bf16)
    tiled = jnp.tile(spread, (GROUP, 1))
    return jnp.where(mask, tiled, jnp.zeros_like(tiled))


def stack_columns(value, width):
    count = value.shape[-1] // width
    return jnp.concatenate(
        [value[..., i * width : (i + 1) * width] for i in range(count)], axis=-2
    )


def unstack_columns(value, count):
    rows = value.shape[-2] // count
    return jnp.concatenate(
        [value[..., i * rows : (i + 1) * rows, :] for i in range(count)], axis=-1
    )


def pad_to(value, axis, size):
    widths = [(0, 0)] * value.ndim
    widths[axis] = (0, size - value.shape[axis])
    return jnp.pad(value, widths)


class Shared:
    def __init__(self, stem_w, embed_w, token_params, decoder_w):
        self.stem_rows = stem_w.shape[0]
        self.embed_rows = embed_w.shape[0]
        self.token_rows = token_params.shape[1]
        self.flat = decoder_w.shape[0]
        self.flat_rows = -(-self.flat // (2 * LANES * 16)) * 16
        self.stem_count = C_STEM // 2 // LANES
        self.embed_count = D // 2 // LANES
        self.cuts = [0]
        for rows in (
            self.stem_rows * self.stem_count,
            self.embed_rows * self.embed_count,
            self.token_rows,
            self.flat_rows,
        ):
            self.cuts.append(self.cuts[-1] + rows)

    def half_flat(self, flat):
        padded = pad_to(flat, flat.ndim - 1, 2 * self.flat_rows * LANES)
        return padded.reshape(flat.shape[:-1] + (2, self.flat_rows, LANES))

    def pieces(self, value):
        one, two, three, four = (
            value[..., a:b, :] for a, b in zip(self.cuts[:-1], self.cuts[1:], strict=True)
        )
        return (
            unstack_columns(one, self.stem_count),
            unstack_columns(two, self.embed_count),
            three,
            four,
        )


def half_columns(value, core, axis=-1):
    axis = axis % value.ndim
    size = value.shape[axis] // 2
    return lax.dynamic_slice_in_dim(value, core * size, size, axis)


def adamw(weight, grad, first, second, rate):
    first_new = beta_one * first + (1.0 - beta_one) * grad
    second_new = beta_two * second + (1.0 - beta_two) * grad * grad
    first_hat = first_new / (1.0 - beta_one**STEP)
    second_hat = second_new / (1.0 - beta_two**STEP)
    new_weight = weight - rate * (
        first_hat / (jnp.sqrt(second_hat) + adam_eps) + decay_rate * weight
    )
    return (new_weight, first_new, second_new)


def body(
    images,
    labels,
    background,
    patients,
    *state,
):
    masters, firsts, seconds = state[:9], state[9:18], state[18:]
    stem_w, embed_w, token_params, qkv_w, out_w, mlp_in_w, mlp_out_w, skip_w, decoder_w = masters
    n_dp = lax.axis_size("dp")
    n_mp = lax.axis_size("mp")
    mp_id = lax.axis_index("mp")
    core = mp_id & 1
    slices = images.shape[0] // n_mp
    rows = slices * PAD
    shared = Shared(stem_w, embed_w, token_params, decoder_w)
    attn_cut = qkv_w.shape[1]

    core_id = core.reshape(1)
    token_t = pad_to(token_params.T, 1, 2 * LANES)
    aligned = shared.stem_rows % 16 == 0 and shared.token_rows % 16 == 0
    mlp_block = jnp.concatenate([mlp_in_w, mlp_out_w.T], axis=1).astype(bf16)
    mlp_all = lax.all_gather(mlp_block, ("mp", "dp"), axis=0, tiled=True).reshape(n_mp, D, -1)
    if aligned:
        first_block = pack(
            core_id, stem_w, embed_w, token_t, shared.half_flat(decoder_w), shared.cuts[-1]
        )
    else:
        dec_half = lax.dynamic_index_in_dim(shared.half_flat(decoder_w), core, 0, keepdims=False)
        first_block = jnp.concatenate(
            [
                stack_columns(half_columns(stem_w, core), LANES),
                stack_columns(half_columns(embed_w, core), LANES),
                half_columns(token_t, core),
                dec_half,
            ],
            axis=0,
        ).astype(bf16)
    attn_block = jnp.concatenate([qkv_w, out_w.T], axis=1).astype(bf16)
    skip_block = half_columns(skip_w, core).astype(bf16)

    first, split, skip = Gather(first_block), Gather(attn_block), Gather(skip_block)
    order = list(reversed(range(log_two(n_dp))))
    for bit in order[3:]:
        for part in (first, split, skip):
            part.step("dp", bit)
    top, middle_bit, last = order[:3]
    first.start("dp", top)
    split.start("dp", top)
    token = first.finish()
    first.start("dp", last)
    token = split.finish(after=(token,))
    split.start("dp", middle_bit)
    skip.value = run_gate(skip.value, token)
    skip.start("dp", top)
    token = first.finish(after=(token,))
    first.start("dp", middle_bit)
    token = split.finish(after=(token,))
    split.start("dp", last)
    token = skip.finish(after=(token,))
    skip.start("dp", middle_bit)
    token = split.finish(after=(token,))
    split.start("mp", 1)
    token = first.finish(after=(token,))
    first_own = first.value
    token = skip.finish(after=(token,))
    skip.start("dp", last)
    token = split.finish(after=(token,))
    attn_weights = split.value
    first_pair = [
        value.reshape(n_dp, -1, LANES) for value in (first_own, swap(first_own, "mp", 0))
    ]
    by_core = lambda pair: [
        jnp.where(core == 0, pair[0], pair[1]), jnp.where(core == 0, pair[1], pair[0])
    ]
    dec_parts = by_core([value[:, shared.cuts[3] :] for value in first_pair])
    if aligned:
        stem_b, embed_b, table = unpack(core_id, *first_pair)
    else:
        both = [shared.pieces(value) for value in by_core(first_pair)]
        side = lambda k: jnp.concatenate([both[0][k], both[1][k]], axis=-1)
        stem_b = side(0).reshape(PIXELS, C_STEM)
        embed_b = side(1).reshape(C_STEM, D)
        table = side(2).reshape(D, 2 * LANES).T.astype(f32)
    dec_flat = jnp.stack(dec_parts, axis=1).reshape(n_dp, -1)[:, : shared.flat].reshape(-1)
    dec_b, one_b, two_b, three_b, head_b = split_decoder(dec_flat)

    attn_all = (attn_weights, swap(attn_weights, "mp", 0))

    take = lambda value: lax.dynamic_slice_in_dim(value, mp_id * slices, slices, 0)
    pixels = pad_to(take(images), 1, PAD).reshape(rows, PIXELS)
    label_own = jnp.pad(take(labels), ((0, 0), (0, PAD - PATCHES), (0, 0)), constant_values=-1)
    label_own = label_own.reshape(rows, PIXELS)
    keep = (1 - take(background)).astype(f32)
    owner = (take(patients)[:, None] == jnp.arange(PATIENTS, dtype=jnp.int32)).astype(f32)

    hidden, slope_stem, embed, normed, triple, context = enter(
        pixels, stem_b, embed_b, table, attn_all, attn_cut
    )
    skip_weights = skip.finish(after=(hidden,))
    skip_all = (skip_weights, swap(skip_weights, "mp", 0))
    resid, normed2, slope_mlp, inner, resid2, final_low = middle(
        context, embed, table, attn_all, mlp_all
    )
    three_four = block_diag(three_b, 4)
    big_head = big_head_of(head_b)
    slope0, level0, slope_skips, level1, level2, level3, logits, stats = leave(
        core_id, hidden, final_low, skip_all, dec_b, one_b, two_b, three_four, big_head, label_own
    )

    sums = jnp.sum(stats.reshape(slices, 3 * CLASSES + 1, 8 * LANES), axis=-1)
    class_sums = sums[:, : 3 * CLASSES]
    pat_sums = jnp.sum(owner[:, :, None] * class_sums[:, None, :], axis=0)
    cross_sum = jnp.sum(keep * sums[:, 3 * CLASSES])
    packed = jnp.concatenate(
        [pat_sums.reshape(-1), cross_sum[None], jnp.sum(keep)[None]]
    )
    packed = pad_to(packed, 0, 4 * LANES).reshape(4, LANES)
    packed = butterfly(packed).reshape(-1)
    pat_all = packed[: PATIENTS * 3 * CLASSES].reshape(PATIENTS, CLASSES, 3)
    ce_total = packed[PATIENTS * 3 * CLASSES]
    pixel_count = packed[PATIENTS * 3 * CLASSES + 1] * (PATCHES * PIXELS)
    pat_over, pat_pred, pat_true = pat_all[..., 0], pat_all[..., 1], pat_all[..., 2]
    denominator = pat_pred + pat_true + dice_eps
    dice = (2.0 * pat_over + dice_eps) / denominator
    count_floor = jnp.maximum(pixel_count, 1.0)
    loss = ce_total / count_floor + 1.0 - jnp.mean(dice)
    cells = PATIENTS * CLASSES
    over_coef = -2.0 / (cells * denominator)
    pred_coef = (2.0 * pat_over + dice_eps) / (cells * denominator * denominator)
    pick_own = lambda table: jnp.sum(owner[:, :, None] * table[None], axis=1)
    coef = jnp.concatenate(
        [pick_own(over_coef), pick_own(pred_coef), (keep / count_floor)[:, None]], axis=1
    )

    def x_sum(value):
        value = lax.reduce_precision(value, 8, 7).astype(bf16)
        return value.astype(f32) + swap(value, "mp", 1).astype(f32)

    def core_pair(send, own):
        return Scatter(own, swap(send, "mp", 0))

    grad_logits, grad_skips = leave_back(
        coef, logits, label_own, slope_skips, big_head, three_four, two_b
    )
    skip_send, skip_keep = skip_grad(core_id, hidden, grad_skips)
    grad_pre0, grad_resid2, grad_resid2_low, sums_f = turn(
        grad_skips, one_b, slope0, dec_b, resid2, table, after=(skip_send,)
    )
    low_bits = list(range(log_two(n_dp)))
    bit_y, bit_one, bit_two = low_bits[:3]
    skip_part = core_pair(skip_send, skip_keep)
    token = skip_part.step("dp", bit_y, bf16, after=(grad_pre0,))
    down_send, down_keep = half_grad(core_id, grad_resid2_low, inner, after=(token,))
    grad_pre, grad_resid, grad_resid_low, grad_context, sums_2 = middle_back(
        grad_resid2_low, mlp_all, slope_mlp, resid, table, grad_resid2, attn_all,
        after=(down_send,),
    )
    down = core_pair(down_send, down_keep)
    token = down.step("dp", bit_y, bf16, after=(grad_pre,))
    in_send, in_keep = half_grad(core_id, normed2, grad_pre, after=(token,))
    grad_triple = attn_back(triple, grad_context, after=(in_send,))
    into = core_pair(in_send, in_keep)
    token = into.step("mp", 1, bf16, after=(grad_triple,))
    token = skip_part.step("dp", bit_one, after=(token,))
    attn_send, attn_keep = attn_grad(
        normed, grad_triple, grad_resid_low, context, after=(token,)
    )
    decoder_halves = decoder_grad(
        level3, grad_logits, level2, level1, grad_skips, level0, final_low, grad_pre0,
        n_dp, shared.flat_rows, after=(attn_send,),
    )
    grad_embed_low, grad_pre_stem, grad_pos, sums_1 = enter_back(
        core_id, grad_triple, attn_all, embed, table, grad_resid, embed_b, grad_skips, skip_all,
        slope_stem, after=(decoder_halves,),
    )
    attn = core_pair(attn_send, attn_keep)
    token = attn.step("mp", 1, bf16, after=(grad_embed_low,))
    token = down.step("dp", bit_one, after=(token,))
    token = skip_part.step("dp", bit_two, after=(token,))
    token = into.step("dp", bit_y, after=(token,))
    if aligned:
        first_send, first_keep = first_grad(
            core_id, pixels, grad_pre_stem, hidden, grad_embed_low, grad_pos, sums_1, sums_2,
            sums_f, decoder_halves, shared.cuts[-1], after=(token,),
        )
    else:
        gains = jnp.concatenate([sums_1, sums_2, sums_f], axis=0).reshape(6, 8, D).sum(axis=1)
        grad_token = pad_to(jnp.concatenate([grad_pos[:PATCHES], gains], axis=0).T, 1, 2 * LANES)

        def first_half(which):
            blocks = lambda value: value.reshape(n_dp, -1, value.shape[-1])
            stem_part = t_matmul(pixels, half_columns(grad_pre_stem, which))
            embed_part = t_matmul(hidden, half_columns(grad_embed_low, which))
            return jnp.concatenate(
                [
                    stack_columns(blocks(stem_part), LANES),
                    stack_columns(blocks(embed_part), LANES),
                    blocks(half_columns(grad_token, which)),
                    lax.dynamic_index_in_dim(decoder_halves, which, 0, keepdims=False).astype(f32),
                ],
                axis=1,
            ).astype(bf16)

        first_send, first_keep = first_half(1 - core), first_half(core)
    wide = lambda value: value.reshape(-1, LANES)
    first = core_pair(wide(first_send), wide(first_keep))
    token = first_send
    token = first.step("dp", bit_y, after=(token,))
    token = down.step("dp", bit_two, after=(token,))
    token = into.step("dp", bit_one, after=(token,))
    for bit in low_bits[3:]:
        skip_part.step("dp", bit)
    skip_half = run_gate(skip_part.total(), token)
    skip_half = x_sum(skip_half)
    token = attn.step("dp", bit_y, after=(token,))
    token = into.step("dp", bit_two, after=(token,))
    token = down.step("mp", 1, after=(token,))
    token = first.step("dp", bit_one, after=(token,))
    token = attn.step("dp", bit_one, after=(token,))
    token = first.step("dp", bit_two, after=(token,))
    token = attn.step("dp", bit_two, after=(token,))
    for bit in low_bits[3:]:
        for part in (down, into, first, attn):
            part.step("dp", bit)
    down_own, in_own, attn_own = down.total(), into.total(), attn.total()
    first_half_sum = x_sum(first.total())

    square = lambda value: jnp.sum(value * value)
    n_copies = n_mp // 2
    local = (
        square(down_own)
        + square(in_own)
        + square(attn_own)
        + (square(skip_half) + square(first_half_sum)) / n_copies
    )
    total = butterfly(jnp.broadcast_to(local, (8, LANES)))[0, 0]
    grad_norm = jnp.sqrt(total)
    factor = jnp.minimum(1.0, clip_limit / (grad_norm + 1e-06))

    red_skip = jnp.concatenate(by_core([skip_half, swap(skip_half, "mp", 0)]), axis=1)
    own = [shared.pieces(part) for part in by_core([first_half_sum, swap(first_half_sum, "mp", 0)])]
    red_stem = jnp.concatenate([own[0][0], own[1][0]], axis=-1)
    red_embed = jnp.concatenate([own[0][1], own[1][1]], axis=-1)
    red_token = jnp.concatenate([own[0][2], own[1][2]], axis=-1)[:, : PATCHES + 6].T
    red_decoder = jnp.concatenate([own[0][3], own[1][3]], axis=0).reshape(-1)[: shared.flat]
    red_qkv = attn_own[:, :attn_cut]
    red_out = attn_own[:, attn_cut:].T
    red_in = in_own
    red_down = down_own.T
    reduced = (
        red_stem, red_embed, red_token, red_qkv, red_out, red_in, red_down, red_skip, red_decoder,
    )
    rates = [learn_rate] * 9
    rates[2] = token_rate
    results = [
        adamw(weight, grad * factor, first, second, rate)
        for weight, grad, first, second, rate in zip(
            masters, reduced, firsts, seconds, rates, strict=True
        )
    ]
    news = [item[0] for item in results]
    moms = [item[1] for item in results]
    secs = [item[2] for item in results]
    return (loss, pixel_count, grad_norm, *news, *moms, *secs)


def solution(mesh):
    weights = (
        P("dp", None),
        P("dp", None),
        P(None, "dp"),
        P("dp", "mp"),
        P("mp", "dp"),
        P("dp", "mp"),
        P("mp", "dp"),
        P("dp", None),
        P("dp"),
    )
    placed = (P("dp", None, None), P("dp", None, None), P("dp"), P("dp")) + weights * 3
    outs = (P(), P(), P()) + weights * 3
    return jax.shard_map(body, mesh=mesh, in_specs=placed, out_specs=outs, check_vma=False)
```

```python
import jax
import jax.numpy as jnp
import numpy as np
from jax import lax
from jax.experimental import pallas as pl
from jax.experimental.pallas import tpu as pltpu
from jax.sharding import PartitionSpec as P

D = 768
HEAD_DIM = 64
PATCHES = 196
PAD = 208
PIXELS = 256
C_STEM = 1024
CHAN_A = 256
CHAN_B = 128
CHAN_C = 64
CHAN_D = 16
CLASSES = 9
PATIENTS = 16
STEP = 10
GROUP = 32
LANES = 128

norm_eps = 1e-06
dice_eps = 1e-05
clip_limit = 0.002
learn_rate = 0.05
token_rate = 0.5
beta_one = 0.9
beta_two = 0.999
adam_eps = 1e-08
decay_rate = 0.01
highest = lax.Precision.HIGHEST
bf16 = jnp.bfloat16
f32 = jnp.float32
MIB = 1024 * 1024


def layer_norm(inputs, gain, shift):
    center = inputs - jnp.mean(inputs, axis=-1, keepdims=True)
    spread = jnp.mean(center * center, axis=-1, keepdims=True)
    return center * lax.rsqrt(spread + norm_eps) * gain + shift


def matmul(left, right):
    return jnp.dot(left, right, preferred_element_type=f32)


def matmul_t(left, right):
    return lax.dot_general(left, right, (((1,), (1,)), ((), ())), preferred_element_type=f32)


def t_matmul(left, right):
    return lax.dot_general(left, right, (((0,), (0,)), ((), ())), preferred_element_type=f32)


FULL = pl.BlockSpec(memory_space=pltpu.VMEM)
SCALAR = pl.BlockSpec(memory_space=pltpu.SMEM)
BLOCK = 256
CHUNK = 16
GELU_SCALE = 0.7978845608028654
GELU_CUBE = 0.044715


def cost(micros):
    return pl.CostEstimate(
        flops=int(micros * 2e9), bytes_accessed=int(micros * 6e6), transcendentals=0
    )


def params(size=27):
    return pltpu.CompilerParams(vmem_limit_bytes=size * MIB)


def run_after(kernel, count, after):
    extra = len(after)

    def ordered(*refs):
        kernel(*refs[:count], *refs[count + extra :])

    return ordered, [pl.BlockSpec(memory_space=pl.ANY)] * extra


def swap(value, axis, bit):
    size = lax.axis_size(axis)
    return lax.ppermute(value, axis, [(i, i ^ (1 << bit)) for i in range(size)])


def my_bit(axis, bit):
    return (lax.axis_index(axis) >> bit) & 1


def log_two(size):
    return size.bit_length() - 1


def gather_kernel(lanes, mine_ref, own_ref, other_ref, out_ref):
    mine = mine_ref[0]
    for which, source_ref in ((mine, own_ref), (1 - mine, other_ref)):
        if lanes:
            width = own_ref.shape[1]
            out_ref[:, pl.ds(pl.multiple_of(which * width, LANES), width)] = source_ref[...]
        else:
            for a in range(out_ref.shape[0]):
                out_ref[a, which] = source_ref[a]


def gate_kernel(value_ref, *refs):
    pass


def run_gate(value, *tokens):
    anywhere = pl.BlockSpec(memory_space=pl.ANY)
    return pl.pallas_call(
        gate_kernel,
        in_specs=[anywhere] * (1 + len(tokens)),
        out_specs=anywhere,
        out_shape=jax.ShapeDtypeStruct(value.shape, value.dtype),
        input_output_aliases={0: 0},
        name="gate",
    )(value, *tokens)


class Gather:
    def __init__(self, block):
        self.value = block
        self.bits = []
        self.pending = None

    def start(self, axis, bit):
        self.pending = (axis, bit, swap(self.value, axis, bit))
        return self.value

    def finish(self, after=()):
        axis, bit, other = self.pending
        rows, columns = self.value.shape
        lanes = axis == "mp"
        if lanes:
            shape, out = (rows, columns), (rows, 2 * columns)
        else:
            ahead = 2 ** sum(b > bit for b in self.bits)
            self.bits.append(bit)
            shape = (ahead, rows // ahead, columns)
            out = (ahead, 2, rows // ahead, columns)
        kernel, waits = run_after(lambda *refs: gather_kernel(lanes, *refs), 3, after)
        value = pl.pallas_call(
            kernel,
            in_specs=[SCALAR] + [FULL] * 2 + waits,
            out_specs=FULL,
            out_shape=jax.ShapeDtypeStruct(out, self.value.dtype),
            compiler_params=params(12),
            cost_estimate=cost(0.1),
            name="gather_step",
        )(my_bit(axis, bit).reshape(1), self.value.reshape(shape), other.reshape(shape), *after)
        self.value = value.reshape(-1, value.shape[-1])
        return self.value

    def step(self, axis, bit, after=()):
        self.start(axis, bit)
        return self.finish(after)


def scatter_kernel(lanes, mine_ref, *refs):
    terms, (send_ref, keep_ref) = refs[:-2], refs[-2:]
    mine = mine_ref[0]
    for which, out_ref in ((1 - mine, send_ref), (mine, keep_ref)):
        if lanes:
            width = out_ref.shape[1]
            cols = pl.ds(pl.multiple_of(which * width, LANES), width)
            total = sum(term[:, cols].astype(f32) for term in terms)
            out_ref[...] = total.astype(out_ref.dtype)
        else:
            total = sum(term[0, which].astype(f32) for term in terms)
            out_ref[0] = total.astype(out_ref.dtype)


class Scatter:
    def __init__(self, *terms):
        self.bits = list(reversed(range(log_two(lax.axis_size("dp")))))
        self.terms = list(terms)
        self.send = None

    def step(self, axis, bit, kept_type=f32, after=()):
        rows, columns = self.terms[0].shape
        lanes = axis == "mp"
        if lanes:
            shape, half = (rows, columns), (rows, columns // 2)
            steps = max(rows // (LANES + CHUNK), 1)
            steps = next(k for k in range(steps, 0, -1) if rows % (k * CHUNK) == 0 or k == 1)
            block = lambda size: pl.BlockSpec((rows // steps, size[1]), lambda i: (i, 0))
        else:
            steps = 2 ** self.bits.index(bit)
            self.bits.remove(bit)
            shape = (steps, 2, rows // (2 * steps), columns)
            half = (steps, rows // (2 * steps), columns)
            block = lambda size: pl.BlockSpec(
                (1,) + size[1:], lambda i: (i,) + (0,) * (len(size) - 1)
            )
        count = len(self.terms)
        body_kernel = lambda *refs: scatter_kernel(lanes, *refs)
        kernel, waits = run_after(body_kernel, 1 + count, after)
        send, kept = pl.pallas_call(
            kernel,
            grid=(steps,),
            in_specs=[SCALAR] + [block(shape)] * count + waits,
            out_specs=[block(half)] * 2,
            out_shape=[jax.ShapeDtypeStruct(half, bf16), jax.ShapeDtypeStruct(half, kept_type)],
            compiler_params=params(12),
            cost_estimate=cost(0.1),
            name="scatter_step",
        )(my_bit(axis, bit).reshape(1), *[term.reshape(shape) for term in self.terms], *after)
        flat = lambda value: value.reshape(-1, value.shape[-1])
        self.send = flat(send)
        self.terms = [flat(kept), swap(self.send, axis, bit)]
        return self.send

    def total(self):
        return sum(term.astype(f32) for term in self.terms)


def butterfly(value):
    def hop(value, moves):
        size = lax.axis_size("dp") * lax.axis_size("mp")
        get = lambda move: lax.ppermute(value, ("dp", "mp"), [(i, i ^ move) for i in range(size)])
        if len(moves) == 1:
            return value + get(moves[0])
        one, two = moves
        first, second, third = get(one), get(two), get(one | two)
        return (value + first) + (second + third)

    value = hop(value, (1,))
    bits = log_two(lax.axis_size("dp"))
    moves = [2] + [4 << bit for bit in range(bits)]
    for i in range(0, len(moves), 2):
        value = hop(value, tuple(moves[i : i + 2]))
    return value


def gelu_pair(value):
    square = value * value
    wave = jnp.tanh(value * (GELU_SCALE + (GELU_SCALE * GELU_CUBE) * square))
    half = 0.5 + 0.5 * wave
    inner = GELU_SCALE + (3.0 * GELU_SCALE * GELU_CUBE) * square
    return value * half, half + 0.5 * value * (1.0 - wave * wave) * inner


def norm_rows(x_ref, gain, shift, out_ref):
    @pl.loop(0, x_ref.shape[0] // CHUNK, unroll=13)
    def _(i):
        rows = pl.ds(pl.multiple_of(i * CHUNK, CHUNK), CHUNK)
        out_ref[rows, :] = layer_norm(x_ref[rows, :], gain, shift).astype(out_ref.dtype)


def norm_back_rows(x_ref, gain, grad_ref, extra_ref, out_ref, low_ref, sum_ref):
    sum_ref[...] = jnp.zeros_like(sum_ref)

    @pl.loop(0, x_ref.shape[0] // CHUNK, unroll=13)
    def _(i):
        rows = pl.ds(pl.multiple_of(i * CHUNK, CHUNK), CHUNK)
        value = x_ref[rows, :]
        grad = grad_ref[rows, :]
        center = value - jnp.mean(value, axis=-1, keepdims=True)
        scale = lax.rsqrt(jnp.mean(center * center, axis=-1, keepdims=True) + norm_eps)
        hat = center * scale
        for k, term in enumerate((grad * hat, grad)):
            sum_ref[8 * k : 8 * k + 8, :] += term[:8] + term[8:]
        pull = grad * gain
        mean_one = jnp.mean(pull, axis=-1, keepdims=True)
        mean_two = jnp.mean(pull * hat, axis=-1, keepdims=True)
        result = scale * (pull - mean_one - hat * mean_two)
        if extra_ref is not None:
            result = result + extra_ref[rows, :]
        out_ref[rows, :] = result
        low_ref[rows, :] = result.astype(bf16)


def gelu_blocks(width):
    return [slice(j, j + BLOCK) for j in range(0, width, BLOCK)]


def soft_rows(scores, column):
    scores = jnp.where(column < PATCHES, scores * HEAD_DIM ** (-0.5), -jnp.inf)
    top = jnp.max(scores, axis=-1, keepdims=True)
    weight = jnp.exp(scores - top)
    return weight * (1.0 / jnp.sum(weight, axis=-1, keepdims=True))


def enter_kernel(
    pixels_ref, stem_ref, embed_w_ref, token_ref, own_ref, other_ref,
    hidden_ref, slope_ref, embed_ref, normed_ref, tri_ref, ctx_ref,
):
    for cols in gelu_blocks(C_STEM):
        value, slope = gelu_pair(matmul(pixels_ref[...], stem_ref[:, cols]))
        hidden_ref[:, cols] = value.astype(bf16)
        slope_ref[:, cols] = slope.astype(bf16)
    slices = pixels_ref.shape[0] // PAD
    for cols in gelu_blocks(D):
        value = matmul(hidden_ref[...], embed_w_ref[:, cols])
        for s in range(slices):
            rows = slice(s * PAD, (s + 1) * PAD)
            embed_ref[rows, cols] = value[rows] + token_ref[:PAD, cols]
    gain, shift = token_ref[PATCHES : PATCHES + 1, :], token_ref[PATCHES + 1 : PATCHES + 2, :]
    norm_rows(embed_ref, gain, shift, normed_ref)
    width = tri_ref.shape[2]
    heads = width // (3 * HEAD_DIM)
    stride = width + width // 3
    column = lax.broadcasted_iota(jnp.int32, (PAD, PAD), 1)
    for p in range(tri_ref.shape[0]):
        start = (p % 2) * stride
        weight_ref = (own_ref, other_ref)[p // 2]
        tri_ref[p] = matmul(normed_ref[...], weight_ref[:, start : start + width]).astype(bf16)

    @pl.loop(0, tri_ref.shape[0])
    def _(p):
        for s in range(slices):
            rows = slice(s * PAD, (s + 1) * PAD)
            for h in range(heads):
                base = h * 3 * HEAD_DIM
                queries = tri_ref[p, rows, base : base + HEAD_DIM]
                keys_low = tri_ref[p, rows, base + HEAD_DIM : base + 2 * HEAD_DIM]
                values = tri_ref[p, rows, base + 2 * HEAD_DIM : base + 3 * HEAD_DIM]
                attend = soft_rows(matmul_t(queries, keys_low), column)
                context = matmul(attend.astype(bf16), values)
                ctx_ref[p, rows, h * HEAD_DIM : (h + 1) * HEAD_DIM] = context.astype(bf16)


def enter(pixels, stem_b, embed_b, tokens, attn_all, width):
    rows = pixels.shape[0]
    parts = 4
    return pl.pallas_call(
        enter_kernel,
        in_specs=[FULL] * 6,
        out_specs=[FULL] * 6,
        out_shape=[
            jax.ShapeDtypeStruct((rows, C_STEM), bf16),
            jax.ShapeDtypeStruct((rows, C_STEM), bf16),
            jax.ShapeDtypeStruct((rows, D), f32),
            jax.ShapeDtypeStruct((rows, D), bf16),
            jax.ShapeDtypeStruct((parts, rows, width), bf16),
            jax.ShapeDtypeStruct((parts, rows, width // 3), bf16),
        ],
        compiler_params=params(),
        cost_estimate=cost(13),
        name="enter",
    )(pixels, stem_b, embed_b, tokens, *attn_all)


def middle_kernel(
    ctx_ref, embed_ref, token_ref, own_ref, other_ref, mlp_ref,
    resid_ref, normed2_ref, slope_ref, inner_ref, resid2_ref, final_ref,
):
    p = pl.program_id(0)

    @pl.when(p == 0)
    def _():
        part = ctx_ref.shape[2]
        stride = 4 * part
        for q in range(ctx_ref.shape[0]):
            start = (q % 2) * stride + 3 * part
            weight_ref = (own_ref, other_ref)[q // 2]
            term = matmul_t(ctx_ref[q], weight_ref[:, start : start + part])
            if q == 0:
                resid_ref[...] = embed_ref[...] + term
            else:
                resid_ref[...] += term
        gain, shift = token_ref[PATCHES + 2 : PATCHES + 3, :], token_ref[PATCHES + 3 : PATCHES + 4, :]
        norm_rows(resid_ref, gain, shift, normed2_ref)
        resid2_ref[...] = resid_ref[...]

    each = mlp_ref.shape[2] // 2
    for cols in gelu_blocks(each):
        value, slope = gelu_pair(matmul(normed2_ref[...], mlp_ref[0, :, cols]))
        inner_ref[0, :, cols] = value.astype(bf16)
        slope_ref[0, :, cols] = slope.astype(bf16)
    resid2_ref[...] += matmul_t(inner_ref[0], mlp_ref[0, :, each:])

    @pl.when(p == pl.num_programs(0) - 1)
    def _():
        gain, shift = token_ref[PATCHES + 4 : PATCHES + 5, :], token_ref[PATCHES + 5 : PATCHES + 6, :]
        norm_rows(resid2_ref, gain, shift, final_ref)


def whole_of(value):
    return pl.BlockSpec(value.shape, lambda *_: (0,) * len(value.shape))


def part_of(value):
    rest = len(value.shape) - 1
    return pl.BlockSpec((1,) + tuple(value.shape[1:]), lambda i, *_: (i,) + (0,) * rest)


def middle(context, embed, tokens, attn_all, mlp_all):
    rows = embed.shape[0]
    parts, _, width = mlp_all.shape
    each = width // 2
    outs = [
        jax.ShapeDtypeStruct((rows, D), f32),
        jax.ShapeDtypeStruct((rows, D), bf16),
        jax.ShapeDtypeStruct((parts, rows, each), bf16),
        jax.ShapeDtypeStruct((parts, rows, each), bf16),
        jax.ShapeDtypeStruct((rows, D), f32),
        jax.ShapeDtypeStruct((rows, D), bf16),
    ]
    values = (context, embed, tokens, *attn_all)
    return pl.pallas_call(
        middle_kernel,
        grid=(parts,),
        in_specs=[whole_of(value) for value in values] + [part_of(mlp_all)],
        out_specs=[(part_of if len(out.shape) == 3 else whole_of)(out) for out in outs],
        out_shape=outs,
        compiler_params=params(),
        cost_estimate=cost(2),
        name="middle",
    )(*values, mlp_all)


def class_probs(logits_ref, rows, group):
    width = CLASSES * LANES
    values = [
        logits_ref[rows, group * width + c * LANES : group * width + (c + 1) * LANES]
        for c in range(CLASSES)
    ]
    top = values[0]
    for value in values[1:]:
        top = jnp.maximum(top, value)
    weights = [jnp.exp(value - top) for value in values]
    total = weights[0]
    for weight in weights[1:]:
        total = total + weight
    scale = 1.0 / total
    return values, [weight * scale for weight in weights], top + jnp.log(total)


SPLIT_A = 4 * CHAN_B
SPLIT_B = SPLIT_A + 16 * CHAN_C
SKIPW = SPLIT_B + 64 * CHAN_D


def leave_kernel(
    core_ref, hidden_ref, final_ref, skip_own_ref, skip_other_ref, dec_ref, one_ref, two_ref, three_ref, head_ref, label_ref,
    slope0_ref, level0_ref, slope_ref, level1_ref, level2_ref, level3_ref, logits_ref, stats_ref,
    skips,
):
    value, slope = gelu_pair(matmul(final_ref[...], dec_ref[...]))
    level0_ref[...] = value.astype(bf16)
    slope0_ref[...] = slope

    half = skip_own_ref.shape[1]
    core = core_ref[0]
    for which, weight_ref in ((core, skip_own_ref), (1 - core, skip_other_ref)):
        for j in range(0, half, BLOCK):
            cols = pl.ds(pl.multiple_of(which * half + j, LANES), BLOCK)
            skips[:, cols] = matmul(hidden_ref[...], weight_ref[:, j : j + BLOCK])

    def stage(source, weight, out_ref, cols, skip_cols):
        pre = matmul(source, weight) + skips[:, skip_cols : skip_cols + BLOCK]
        value, slope = gelu_pair(pre)
        out_ref[:, cols : cols + BLOCK] = value.astype(bf16)
        slope_ref[:, skip_cols : skip_cols + BLOCK] = slope.astype(bf16)

    for i in range(2):
        stage(level0_ref[...], one_ref[:, i * BLOCK : (i + 1) * BLOCK], level1_ref, i * BLOCK, i * BLOCK)
    for i in range(4):
        stage(
            level1_ref[:, i * CHAN_B : (i + 1) * CHAN_B], two_ref[...], level2_ref, i * BLOCK,
            SPLIT_A + i * BLOCK,
        )
    for i in range(4):
        stage(
            level2_ref[:, i * BLOCK : (i + 1) * BLOCK], three_ref[...], level3_ref, i * BLOCK,
            SPLIT_B + i * BLOCK,
        )
    inner = head_ref.shape[0]
    width = head_ref.shape[1]
    groups = level3_ref.shape[1] // inner
    for g in range(groups):
        logits_ref[:, g * width : (g + 1) * width] = matmul(
            level3_ref[:, g * inner : (g + 1) * inner], head_ref[...]
        )
    stats_ref[...] = jnp.zeros_like(stats_ref)
    slices = stats_ref.shape[0]
    per_slice = PAD // CHUNK

    @pl.loop(0, slices)
    def _(s):
        @pl.loop(0, per_slice)
        def _(i):
            start = pl.multiple_of(s * PAD + i * CHUNK, CHUNK)
            rows = pl.ds(start, CHUNK)
            row_id = lax.broadcasted_iota(jnp.int32, (CHUNK, LANES), 0) + i * CHUNK
            inside = (row_id < PATCHES).astype(f32)
            for g in range(groups):
                values, probs, log_total = class_probs(logits_ref, rows, g)
                label = label_ref[rows, g * LANES : (g + 1) * LANES]
                cross = jnp.zeros((CHUNK, LANES), f32)
                for c in range(CLASSES):
                    hot = (label == c).astype(f32)
                    cross = cross + hot * (log_total - values[c])
                    for k, term in enumerate((hot * probs[c], inside * probs[c], hot)):
                        spot = 8 * (3 * c + k)
                        stats_ref[s, spot : spot + 8, :] += term[:8] + term[8:]
                spot = 8 * 3 * CLASSES
                stats_ref[s, spot : spot + 8, :] += cross[:8] + cross[8:]


def leave(core, hidden, final_low, skip_all, dec_b, one_b, two_b, three_four, big_head, labels):
    rows = hidden.shape[0]
    slices = rows // PAD
    stat_rows = 8 * (3 * CLASSES + 1)
    return pl.pallas_call(
        leave_kernel,
        in_specs=[SCALAR] + [FULL] * 10,
        out_specs=[FULL] * 8,
        out_shape=[
            jax.ShapeDtypeStruct((rows, CHAN_A), f32),
            jax.ShapeDtypeStruct((rows, CHAN_A), bf16),
            jax.ShapeDtypeStruct((rows, SKIPW), bf16),
            jax.ShapeDtypeStruct((rows, 4 * CHAN_B), bf16),
            jax.ShapeDtypeStruct((rows, 16 * CHAN_C), bf16),
            jax.ShapeDtypeStruct((rows, 64 * CHAN_D), bf16),
            jax.ShapeDtypeStruct((rows, CLASSES * PIXELS), f32),
            jax.ShapeDtypeStruct((slices, stat_rows, LANES), f32),
        ],
        scratch_shapes=[pltpu.VMEM((rows, SKIPW), f32)],
        compiler_params=params(),
        cost_estimate=cost(12),
        name="leave",
    )(core, hidden, final_low, *skip_all, dec_b, one_b, two_b, three_four, big_head, labels)


def leave_back_kernel(
    coef_ref, logits_ref, label_ref, slope_ref, head_ref, three_ref, two_ref,
    g_logits_ref, g_skips_ref,
):
    inner = head_ref.shape[0]
    width = head_ref.shape[1]
    groups = 64 * CHAN_D // inner
    slices = logits_ref.shape[0] // PAD

    @pl.loop(0, slices)
    def _(s):
        cross_scale = coef_ref[s, 2 * CLASSES]

        @pl.loop(0, PAD // CHUNK)
        def _(i):
            start = pl.multiple_of(s * PAD + i * CHUNK, CHUNK)
            rows = pl.ds(start, CHUNK)
            row_id = lax.broadcasted_iota(jnp.int32, (CHUNK, LANES), 0) + i * CHUNK
            inside = (row_id < PATCHES).astype(f32)
            for g in range(groups):
                _, probs, _ = class_probs(logits_ref, rows, g)
                label = label_ref[rows, g * LANES : (g + 1) * LANES]
                mean = jnp.zeros((CHUNK, LANES), f32)
                pulls = []
                for c in range(CLASSES):
                    pull = jnp.where(label == c, coef_ref[s, c], 0.0) + coef_ref[s, CLASSES + c]
                    pulls.append(pull)
                    mean = mean + probs[c] * pull
                mean = mean - cross_scale
                for c in range(CLASSES):
                    grad = probs[c] * (pulls[c] - mean)
                    grad = grad - jnp.where(label == c, cross_scale, 0.0)
                    spot = g * width + c * LANES
                    g_logits_ref[rows, spot : spot + LANES] = (grad * inside).astype(bf16)

    for i in range(4):
        g, part = (i * BLOCK) // inner, (i * BLOCK) % inner
        grad = matmul_t(g_logits_ref[:, g * width : (g + 1) * width], head_ref[part : part + BLOCK, :])
        cols = slice(SPLIT_B + i * BLOCK, SPLIT_B + (i + 1) * BLOCK)
        g_skips_ref[:, cols] = (grad * slope_ref[:, cols].astype(f32)).astype(bf16)
    for i in range(4):
        source = g_skips_ref[:, SPLIT_B + i * BLOCK : SPLIT_B + (i + 1) * BLOCK]
        cols = slice(SPLIT_A + i * BLOCK, SPLIT_A + (i + 1) * BLOCK)
        g_skips_ref[:, cols] = (matmul_t(source, three_ref[...]) * slope_ref[:, cols].astype(f32)).astype(bf16)
    for i in range(4):
        source = g_skips_ref[:, SPLIT_A + i * BLOCK : SPLIT_A + (i + 1) * BLOCK]
        cols = slice(i * CHAN_B, (i + 1) * CHAN_B)
        g_skips_ref[:, cols] = (matmul_t(source, two_ref[...]) * slope_ref[:, cols].astype(f32)).astype(bf16)


def leave_back(coef, logits, labels, slope, big_head, three_four, two_b):
    rows = logits.shape[0]
    return pl.pallas_call(
        leave_back_kernel,
        in_specs=[SCALAR] + [FULL] * 6,
        out_specs=[FULL] * 2,
        out_shape=[
            jax.ShapeDtypeStruct((rows, CLASSES * PIXELS), bf16),
            jax.ShapeDtypeStruct((rows, SKIPW), bf16),
        ],
        compiler_params=params(),
        cost_estimate=cost(6),
        name="leave_back",
    )(coef, logits, labels, slope, big_head, three_four, two_b)


def skip_grad_kernel(core_ref, hidden_ref, g_skips_ref, send_ref, keep_ref):
    half = send_ref.shape[1]
    core = core_ref[0]
    for which, out_ref in ((1 - core, send_ref), (core, keep_ref)):
        for j in range(0, half, half // 2):
            cols = pl.ds(pl.multiple_of(which * half + j, LANES), half // 2)
            out_ref[:, j : j + half // 2] = t_matmul(hidden_ref[...], g_skips_ref[:, cols]).astype(
                bf16
            )


def skip_grad(core, hidden, g_skips):
    shape = (hidden.shape[1], g_skips.shape[1] // 2)
    return pl.pallas_call(
        skip_grad_kernel,
        in_specs=[SCALAR] + [FULL] * 2,
        out_specs=[FULL] * 2,
        out_shape=[jax.ShapeDtypeStruct(shape, bf16)] * 2,
        compiler_params=params(),
        cost_estimate=cost(3.5),
        name="skip_grad",
    )(core, hidden, g_skips)


def turn_kernel(
    g_skips_ref, one_ref, slope0_ref, dec_ref, resid2_ref, token_ref,
    g_pre0_ref, g_resid2_ref, low_ref, sums_ref, g_final,
):
    grad = matmul_t(g_skips_ref[:, :SPLIT_A], one_ref[...])
    g_pre0_ref[...] = (grad * slope0_ref[...]).astype(bf16)
    g_final[...] = matmul_t(g_pre0_ref[...], dec_ref[...])
    norm_back_rows(
        resid2_ref, token_ref[PATCHES + 4 : PATCHES + 5, :], g_final, None, g_resid2_ref, low_ref, sums_ref
    )


def turn(g_skips, one_b, slope0, dec_b, resid2, tokens, after=()):
    rows = resid2.shape[0]
    kernel, waits = run_after(turn_kernel, 6, after)
    return pl.pallas_call(
        kernel,
        in_specs=[FULL] * 6 + waits,
        out_specs=[FULL] * 4,
        out_shape=[
            jax.ShapeDtypeStruct((rows, CHAN_A), bf16),
            jax.ShapeDtypeStruct((rows, D), f32),
            jax.ShapeDtypeStruct((rows, D), bf16),
            jax.ShapeDtypeStruct((16, D), f32),
        ],
        scratch_shapes=[pltpu.VMEM((rows, D), f32)],
        compiler_params=params(),
        cost_estimate=cost(3),
        name="turn",
    )(g_skips, one_b, slope0, dec_b, resid2, tokens, *after)


FLAT_DEC = D * CHAN_A // LANES
FLAT_ONE = FLAT_DEC + CHAN_A * 4 * CHAN_B // LANES
FLAT_TWO = FLAT_ONE + CHAN_B * 4 * CHAN_C // LANES
FLAT_THREE = FLAT_TWO + CHAN_C * 4 * CHAN_D // LANES


def decoder_grad_kernel(
    level3_ref, g_logits_ref, level2_ref, level1_ref, g_skips_ref, level0_ref, final_ref, g_pre0_ref,
    out_ref, flat_ref, square_ref,
):
    size = out_ref.shape[1]
    flat = (FLAT_THREE * LANES + 4 * CLASSES * CHAN_D) // size
    inner, width = GROUP * CHAN_D, CLASSES * LANES
    tail = flat_ref.shape[0] - FLAT_THREE
    flat_ref[FLAT_THREE:, :] = jnp.zeros((tail, LANES), f32)

    def spread(value, base, count):
        for j in range(count):
            flat_ref[pl.ds(base + j, value.shape[0], stride=count), :] = value[
                :, j * LANES : (j + 1) * LANES
            ]

    spread(t_matmul(final_ref[...], g_pre0_ref[...]), 0, CHAN_A // LANES)
    spread(t_matmul(level0_ref[...], g_skips_ref[:, :SPLIT_A]), FLAT_DEC, SPLIT_A // LANES)
    three = jnp.zeros((CHAN_C, 4 * CHAN_D), f32)
    two = jnp.zeros((CHAN_B, 4 * CHAN_C), f32)
    for i in range(4):
        big = t_matmul(
            level2_ref[:, i * BLOCK : (i + 1) * BLOCK],
            g_skips_ref[:, SPLIT_B + i * BLOCK : SPLIT_B + (i + 1) * BLOCK],
        )
        for k in range(4):
            at = slice(k * CHAN_C, (k + 1) * CHAN_C)
            three += big[at, at]
        two += t_matmul(
            level1_ref[:, i * CHAN_B : (i + 1) * CHAN_B],
            g_skips_ref[:, SPLIT_A + i * BLOCK : SPLIT_A + (i + 1) * BLOCK],
        )
    spread(two, FLAT_ONE, 4 * CHAN_C // LANES)
    square_ref[...] = three
    flat_ref[FLAT_TWO:FLAT_THREE, :] = jnp.concatenate(
        [square_ref[pl.ds(j, CHAN_C // 2, stride=2), :] for j in range(2)], axis=1
    )
    head = jnp.zeros((CHAN_D, width), f32)
    row = lax.broadcasted_iota(jnp.int32, (CHAN_D, width), 0)
    across = lax.broadcasted_iota(jnp.int32, (CHAN_D, width), 1)
    parent = (across // 4) % GROUP
    for g in range(level3_ref.shape[1] // inner):
        big = t_matmul(
            level3_ref[:, g * inner : (g + 1) * inner], g_logits_ref[:, g * width : (g + 1) * width]
        )
        for k in range(GROUP):
            head += jnp.where(parent == k, big[k * CHAN_D : (k + 1) * CHAN_D, :], 0.0)
    column = lax.broadcasted_iota(jnp.int32, (width, LANES), 0)
    target = lax.broadcasted_iota(jnp.int32, (width, LANES), 1)
    pick = target == (column % 4) * CLASSES + column // (GROUP * 4)
    small = jnp.dot(head, pick.astype(f32), precision=highest, preferred_element_type=f32)
    lane = lax.broadcasted_iota(jnp.int32, (1, LANES), 1)
    lines = [jnp.zeros((1, LANES), f32) for _ in range(8)]
    for k in range(CHAN_D):
        line, start = divmod(k * 4 * CLASSES, LANES)
        value = small[k : k + 1, :]
        if start:
            value = pltpu.roll(value, start, 1)
        lines[line] = lines[line] + jnp.where(lane >= start, value, 0.0)
        if start + 4 * CLASSES > LANES:
            lines[line + 1] = lines[line + 1] + jnp.where(
                lane < start + 4 * CLASSES - LANES, value, 0.0
            )
    flat_ref[FLAT_THREE : FLAT_THREE + 8, :] = jnp.concatenate(lines, axis=0)

    rows = out_ref.shape[2]
    line_id = lax.broadcasted_iota(jnp.int32, (rows, LANES), 0)
    lane_id = lax.broadcasted_iota(jnp.int32, (rows, LANES), 1)
    for d in range(size):
        for c in range(2):
            first, start = divmod(d * flat + c * rows * LANES, LANES)
            value = flat_ref[first : first + rows, :]
            if start:
                after = flat_ref[first + 1 : first + 1 + rows, :]
                value = jnp.where(
                    lane_id < LANES - start,
                    pltpu.roll(value, LANES - start, 1),
                    pltpu.roll(after, LANES - start, 1),
                )
            inside = (line_id + c * rows) * LANES + lane_id < flat
            out_ref[c, d] = jnp.where(inside, value, 0.0).astype(bf16)


def decoder_grad(
    level3, g_logits, level2, level1, g_skips, level0, final_low, g_pre0, size, rows, after=()
):
    kernel, waits = run_after(decoder_grad_kernel, 8, after)
    flat = (FLAT_THREE * LANES + 4 * CLASSES * CHAN_D) // size
    lines = (size - 1) * flat // LANES + 2 * rows + 8
    lines = -(-max(lines, FLAT_THREE + 8) // 8) * 8
    return pl.pallas_call(
        kernel,
        in_specs=[FULL] * 8 + waits,
        out_specs=FULL,
        out_shape=jax.ShapeDtypeStruct((2, size, rows, LANES), bf16),
        scratch_shapes=[pltpu.VMEM((lines, LANES), f32), pltpu.VMEM((CHAN_C, 4 * CHAN_D), f32)],
        compiler_params=params(),
        cost_estimate=cost(3),
        name="decoder_grad",
    )(level3, g_logits, level2, level1, g_skips, level0, final_low, g_pre0, *after)


def first_grad_kernel(
    core_ref, pixels_ref, g_stem_ref, hidden_ref, low_ref, pos_ref, sums1_ref, sums2_ref, sumsf_ref,
    dec_ref, send_ref, keep_ref, token_ref,
):
    core = core_ref[0]
    size = send_ref.shape[0]
    stem_rows, embed_rows, token_rows = PIXELS // size, C_STEM // size, D // size
    token_ref[...] = jnp.zeros_like(token_ref)
    token_ref[:PATCHES, :] = pos_ref[:PATCHES, :]
    for i, sums_ref in enumerate((sums1_ref, sums2_ref, sumsf_ref)):
        for k in range(2):
            at = PATCHES + 2 * i + k
            token_ref[at : at + 1, :] = jnp.sum(
                sums_ref[8 * k : 8 * k + 8, :], axis=0, keepdims=True
            )
    for which, out_ref in ((1 - core, send_ref), (core, keep_ref)):
        spot = 0
        half = C_STEM // 2
        for j in range(0, half, BLOCK):
            cols = pl.ds(pl.multiple_of(which * half + j, LANES), BLOCK)
            part = t_matmul(pixels_ref[...], g_stem_ref[:, cols]).astype(bf16)
            for k in range(0, BLOCK, LANES):
                for d in range(size):
                    out_ref[d, spot : spot + stem_rows, :] = part[
                        d * stem_rows : (d + 1) * stem_rows, k : k + LANES
                    ]
                spot += stem_rows
        half = D // 2
        cols = pl.ds(pl.multiple_of(which * half, LANES), half)
        part = t_matmul(hidden_ref[...], low_ref[:, cols]).astype(bf16)
        for k in range(0, half, LANES):
            for d in range(size):
                out_ref[d, spot : spot + embed_rows, :] = part[
                    d * embed_rows : (d + 1) * embed_rows, k : k + LANES
                ]
            spot += embed_rows
        turned = token_ref[pl.ds(pl.multiple_of(which * LANES, LANES), LANES), :].T.astype(bf16)
        for d in range(size):
            out_ref[d, spot : spot + token_rows, :] = turned[d * token_rows : (d + 1) * token_rows]
            out_ref[d, spot + token_rows :, :] = dec_ref[which, d]


def first_grad(core, pixels, g_stem, hidden, low, pos, sums1, sums2, sumsf, dec, rows, after=()):
    kernel, waits = run_after(first_grad_kernel, 10, after)
    shape = (dec.shape[1], rows, LANES)
    return pl.pallas_call(
        kernel,
        in_specs=[SCALAR] + [FULL] * 9 + waits,
        out_specs=[FULL] * 2,
        out_shape=[jax.ShapeDtypeStruct(shape, bf16)] * 2,
        scratch_shapes=[pltpu.VMEM((2 * LANES, D), f32)],
        compiler_params=params(),
        cost_estimate=cost(2),
        name="first_grad",
    )(core, pixels, g_stem, hidden, low, pos, sums1, sums2, sumsf, dec, *after)


def unpack_kernel(core_ref, own_ref, other_ref, stem_ref, embed_ref, token_ref, turned_ref):
    core = core_ref[0]
    size = own_ref.shape[0]
    stem_rows, embed_rows, token_rows = PIXELS // size, C_STEM // size, D // size
    for which, block_ref in ((core, own_ref), (1 - core, other_ref)):
        spot = 0
        for target_ref, rows, half in (
            (stem_ref, stem_rows, C_STEM // 2),
            (embed_ref, embed_rows, D // 2),
            (turned_ref, token_rows, LANES),
        ):
            for k in range(0, half, LANES):
                cols = pl.ds(pl.multiple_of(which * half + k, LANES), LANES)
                for d in range(size):
                    target_ref[d * rows : (d + 1) * rows, cols] = block_ref[
                        d, spot : spot + rows, :
                    ].astype(target_ref.dtype)
                spot += rows
    token_ref[...] = turned_ref[...].T


def unpack(core, own, other):
    return pl.pallas_call(
        unpack_kernel,
        in_specs=[SCALAR] + [FULL] * 2,
        out_specs=[FULL] * 3,
        out_shape=[
            jax.ShapeDtypeStruct((PIXELS, C_STEM), bf16),
            jax.ShapeDtypeStruct((C_STEM, D), bf16),
            jax.ShapeDtypeStruct((2 * LANES, D), f32),
        ],
        scratch_shapes=[pltpu.VMEM((D, 2 * LANES), f32)],
        compiler_params=params(),
        cost_estimate=cost(3),
        name="unpack",
    )(core, own, other)


def pack_kernel(core_ref, stem_ref, embed_ref, token_ref, dec_ref, out_ref):
    core = core_ref[0]
    spot = 0
    for source_ref in (stem_ref, embed_ref, token_ref):
        rows, half = source_ref.shape[0], source_ref.shape[1] // 2
        for k in range(0, half, LANES):
            cols = pl.ds(pl.multiple_of(core * half + k, LANES), LANES)
            out_ref[spot : spot + rows, :] = source_ref[:, cols].astype(bf16)
            spot += rows
    out_ref[spot:, :] = dec_ref[core].astype(bf16)


def pack(core, stem_w, embed_w, token_t, dec, rows):
    return pl.pallas_call(
        pack_kernel,
        in_specs=[SCALAR] + [FULL] * 4,
        out_specs=FULL,
        out_shape=jax.ShapeDtypeStruct((rows, LANES), bf16),
        compiler_params=params(),
        cost_estimate=cost(2),
        name="pack",
    )(core, stem_w, embed_w, token_t, dec)


def middle_back_kernel(
    low2_ref, mlp_ref, slope_ref, resid_ref, token_ref, g_resid2_ref, own_ref, other_ref,
    g_pre_ref, g_resid_ref, low_ref, g_ctx_ref, sums_ref, g_normed,
):
    p = pl.program_id(0)
    each = mlp_ref.shape[2] // 2
    for cols in gelu_blocks(each):
        down = mlp_ref[0, :, each + cols.start : each + cols.stop]
        grad = matmul(low2_ref[...], down) * slope_ref[0, :, cols].astype(f32)
        g_pre_ref[0, :, cols] = grad.astype(bf16)
    term = matmul_t(g_pre_ref[0], mlp_ref[0, :, :each])

    @pl.when(p == 0)
    def _():
        g_normed[...] = term

    @pl.when(p > 0)
    def _():
        g_normed[...] += term

    @pl.when(p == pl.num_programs(0) - 1)
    def _():
        norm_back_rows(
            resid_ref, token_ref[PATCHES + 2 : PATCHES + 3, :], g_normed, g_resid2_ref,
            g_resid_ref, low_ref, sums_ref,
        )
        part = g_ctx_ref.shape[2]
        for q in range(g_ctx_ref.shape[0]):
            start = (q % 2) * 4 * part + 3 * part
            weight_ref = (own_ref, other_ref)[q // 2]
            g_ctx_ref[q] = matmul(low_ref[...], weight_ref[:, start : start + part]).astype(bf16)


def middle_back(low2, mlp_all, slope, resid, tokens, g_resid2, attn_all, after=()):
    kernel, waits = run_after(middle_back_kernel, 8, after)
    rows = resid.shape[0]
    parts, _, each = slope.shape
    part = attn_all[0].shape[1] // 8
    outs = [
        jax.ShapeDtypeStruct((parts, rows, each), bf16),
        jax.ShapeDtypeStruct((rows, D), f32),
        jax.ShapeDtypeStruct((rows, D), bf16),
        jax.ShapeDtypeStruct((parts, rows, part), bf16),
        jax.ShapeDtypeStruct((16, D), f32),
    ]
    values = (resid, tokens, g_resid2, *attn_all)
    return pl.pallas_call(
        kernel,
        grid=(parts,),
        in_specs=[whole_of(low2), part_of(mlp_all), part_of(slope)]
        + [whole_of(value) for value in values]
        + waits,
        out_specs=[part_of(outs[0])] + [whole_of(out) for out in outs[1:]],
        out_shape=outs,
        scratch_shapes=[pltpu.VMEM((rows, D), f32)],
        compiler_params=params(),
        cost_estimate=cost(11),
        name="middle_back",
    )(low2, mlp_all, slope, *values, *after)


def half_grad_kernel(core_ref, left_ref, right_ref, send_ref, keep_ref):
    core = core_ref[0]
    each = right_ref.shape[2]
    for which, out_ref in ((1 - core, send_ref), (core, keep_ref)):
        for x in range(2):
            out_ref[:, x * each : (x + 1) * each] = t_matmul(
                left_ref[...], right_ref[2 * x + which]
            ).astype(bf16)


def half_grad(core, left, right, after=()):
    kernel, waits = run_after(half_grad_kernel, 3, after)
    shape = (left.shape[1], 2 * right.shape[2])
    return pl.pallas_call(
        kernel,
        in_specs=[SCALAR] + [FULL] * 2 + waits,
        out_specs=[FULL] * 2,
        out_shape=[jax.ShapeDtypeStruct(shape, bf16)] * 2,
        compiler_params=params(),
        cost_estimate=cost(2.7),
        name="half_grad",
    )(core, left, right, *after)


def attn_back_kernel(tri_ref, g_ctx_ref, g_tri_ref):
    slices = tri_ref.shape[1] // PAD
    heads = tri_ref.shape[2] // (3 * HEAD_DIM)
    column = lax.broadcasted_iota(jnp.int32, (PAD, PAD), 1)
    for s in range(slices):
        rows = slice(s * PAD, (s + 1) * PAD)
        for h in range(heads):
            base = h * 3 * HEAD_DIM
            queries = tri_ref[0, rows, base : base + HEAD_DIM]
            keys_low = tri_ref[0, rows, base + HEAD_DIM : base + 2 * HEAD_DIM]
            values = tri_ref[0, rows, base + 2 * HEAD_DIM : base + 3 * HEAD_DIM]
            gctx = g_ctx_ref[0, rows, h * HEAD_DIM : (h + 1) * HEAD_DIM]
            attend = soft_rows(matmul_t(queries, keys_low), column)
            g_attend = matmul_t(gctx, values)
            g_values = t_matmul(attend.astype(bf16), gctx)
            inner = jnp.sum(attend * g_attend, axis=-1, keepdims=True)
            g_scores = attend * (g_attend - inner) * HEAD_DIM ** (-0.5)
            g_low = g_scores.astype(bf16)
            g_tri_ref[0, rows, base : base + HEAD_DIM] = matmul(g_low, keys_low).astype(bf16)
            g_tri_ref[0, rows, base + HEAD_DIM : base + 2 * HEAD_DIM] = t_matmul(
                g_low, queries
            ).astype(bf16)
            g_tri_ref[0, rows, base + 2 * HEAD_DIM : base + 3 * HEAD_DIM] = g_values.astype(bf16)


def attn_back(triple, g_ctx, after=()):
    parts, rows, width = triple.shape
    whole = lambda size: pl.BlockSpec((1, rows, size), lambda i: (i, 0, 0))
    kernel, waits = run_after(attn_back_kernel, 2, after)
    return pl.pallas_call(
        kernel,
        grid=(parts,),
        in_specs=[whole(width), whole(width // 3)] + waits,
        out_specs=whole(width),
        out_shape=jax.ShapeDtypeStruct(triple.shape, bf16),
        compiler_params=params(),
        cost_estimate=cost(13.5),
        name="attn_back",
    )(triple, g_ctx, *after)


def attn_grad_kernel(normed_ref, g_tri_ref, low_ref, ctx_ref, send_ref, keep_ref):
    width = g_tri_ref.shape[2]
    stride = width + width // 3
    for which, out_ref in ((1, send_ref), (0, keep_ref)):
        for x in range(2):
            part = 2 * which + x
            at = x * stride
            out_ref[:, at : at + width] = t_matmul(normed_ref[...], g_tri_ref[part]).astype(
                out_ref.dtype
            )
            out_ref[:, at + width : at + stride] = t_matmul(low_ref[...], ctx_ref[part]).astype(
                out_ref.dtype
            )


def attn_grad(normed, g_tri, low, context, after=()):
    shape = (D, 2 * (g_tri.shape[2] + context.shape[2]))
    kernel, waits = run_after(attn_grad_kernel, 4, after)
    return pl.pallas_call(
        kernel,
        in_specs=[FULL] * 4 + waits,
        out_specs=[FULL] * 2,
        out_shape=[jax.ShapeDtypeStruct(shape, bf16)] * 2,
        compiler_params=params(),
        cost_estimate=cost(3.6),
        name="attn_grad",
    )(normed, g_tri, low, context, *after)


def enter_back_kernel(
    core_ref, g_tri_ref, own_ref, other_ref, embed_ref, token_ref, g_resid_ref, embed_w_ref,
    g_skips_ref, skip_own_ref, skip_other_ref, slope_ref, low_ref, g_stem_ref, g_pos_ref, sums_ref, g_normed, g_embed,
):
    width = g_tri_ref.shape[2]
    stride = width + width // 3
    for p in range(g_tri_ref.shape[0]):
        start = (p % 2) * stride
        weight_ref = (own_ref, other_ref)[p // 2]
        term = matmul_t(g_tri_ref[p], weight_ref[:, start : start + width])
        if p == 0:
            g_normed[...] = term
        else:
            g_normed[...] += term
    norm_back_rows(
        embed_ref, token_ref[PATCHES : PATCHES + 1, :], g_normed, g_resid_ref, g_embed, low_ref, sums_ref
    )
    pos = g_embed[:PAD, :]
    for s in range(1, embed_ref.shape[0] // PAD):
        pos = pos + g_embed[s * PAD : (s + 1) * PAD, :]
    g_pos_ref[...] = pos
    half = skip_own_ref.shape[1]
    core = core_ref[0]
    for cols in gelu_blocks(C_STEM):
        grad = matmul_t(low_ref[...], embed_w_ref[cols, :])
        for which, weight_ref in ((core, skip_own_ref), (1 - core, skip_other_ref)):
            part = pl.ds(pl.multiple_of(which * half, LANES), half)
            grad += matmul_t(g_skips_ref[:, part], weight_ref[cols, :])
        g_stem_ref[:, cols] = (grad * slope_ref[:, cols].astype(f32)).astype(bf16)


def enter_back(core, g_tri, attn_all, embed, tokens, g_resid, embed_b, g_skips, skip_all, slope, after=()):
    rows = embed.shape[0]
    kernel, waits = run_after(enter_back_kernel, 12, after)
    return pl.pallas_call(
        kernel,
        in_specs=[SCALAR] + [FULL] * 11 + waits,
        out_specs=[FULL] * 4,
        out_shape=[
            jax.ShapeDtypeStruct((rows, D), bf16),
            jax.ShapeDtypeStruct((rows, C_STEM), bf16),
            jax.ShapeDtypeStruct((PAD, D), f32),
            jax.ShapeDtypeStruct((16, D), f32),
        ],
        scratch_shapes=[pltpu.VMEM((rows, D), f32), pltpu.VMEM((rows, D), f32)],
        compiler_params=params(),
        cost_estimate=cost(10.4),
        name="enter_back",
    )(core, g_tri, *attn_all, embed, tokens, g_resid, embed_b, g_skips, *skip_all, slope, *after)


def split_decoder(flat):
    edge_one = D * CHAN_A
    edge_two = edge_one + CHAN_A * 4 * CHAN_B
    edge_three = edge_two + CHAN_B * 4 * CHAN_C
    edge_four = edge_three + CHAN_C * 4 * CHAN_D
    return (
        flat[:edge_one].reshape(D, CHAN_A),
        flat[edge_one:edge_two].reshape(CHAN_A, 4 * CHAN_B),
        flat[edge_two:edge_three].reshape(CHAN_B, 4 * CHAN_C),
        flat[edge_three:edge_four].reshape(CHAN_C, 4 * CHAN_D),
        flat[edge_four:].reshape(CHAN_D, 4 * CLASSES),
    )


def same_block(rows, columns, inner, outer):
    return (np.arange(rows) // inner)[:, None] == (np.arange(columns) // outer)[None, :]


def block_diag(weight, parents):
    inner, outer = weight.shape
    mask = same_block(parents * inner, parents * outer, inner, outer)
    tiled = jnp.tile(weight, (parents, parents))
    return tiled * mask.astype(bf16)


def head_masks():
    column = np.arange(CLASSES * GROUP * 4)
    source = np.arange(4 * CLASSES)[:, None]
    pick = source == ((column % 4) * CLASSES + column // (GROUP * 4))[None, :]
    row = np.arange(GROUP * CHAN_D)[:, None]
    mask = row // CHAN_D == ((column // 4) % GROUP)[None, :]
    return pick, mask


def big_head_of(head_b):
    pick, mask = head_masks()
    spread = matmul(head_b, pick.astype(bf16)).astype(bf16)
    tiled = jnp.tile(spread, (GROUP, 1))
    return tiled * mask.astype(bf16)


def stack_columns(value, width):
    count = value.shape[-1] // width
    return jnp.concatenate(
        [value[..., i * width : (i + 1) * width] for i in range(count)], axis=-2
    )


def unstack_columns(value, count):
    rows = value.shape[-2] // count
    return jnp.concatenate(
        [value[..., i * rows : (i + 1) * rows, :] for i in range(count)], axis=-1
    )


def pad_to(value, axis, size):
    widths = [(0, 0)] * value.ndim
    widths[axis] = (0, size - value.shape[axis])
    return jnp.pad(value, widths)


class Shared:
    def __init__(self, stem_w, embed_w, token_params, decoder_w):
        self.stem_rows = stem_w.shape[0]
        self.embed_rows = embed_w.shape[0]
        self.token_rows = token_params.shape[1]
        self.flat = decoder_w.shape[0]
        self.flat_rows = -(-self.flat // (2 * LANES * 16)) * 16
        self.stem_count = C_STEM // 2 // LANES
        self.embed_count = D // 2 // LANES
        self.cuts = [0]
        for rows in (
            self.stem_rows * self.stem_count,
            self.embed_rows * self.embed_count,
            self.token_rows,
            self.flat_rows,
        ):
            self.cuts.append(self.cuts[-1] + rows)

    def half_flat(self, flat):
        padded = pad_to(flat, flat.ndim - 1, 2 * self.flat_rows * LANES)
        return padded.reshape(flat.shape[:-1] + (2, self.flat_rows, LANES))

    def pieces(self, value):
        one, two, three, four = (
            value[..., a:b, :] for a, b in zip(self.cuts[:-1], self.cuts[1:], strict=True)
        )
        return (
            unstack_columns(one, self.stem_count),
            unstack_columns(two, self.embed_count),
            three,
            four,
        )


def half_columns(value, core, axis=-1):
    axis = axis % value.ndim
    size = value.shape[axis] // 2
    return lax.dynamic_slice_in_dim(value, core * size, size, axis)


def adamw(weight, grad, first, second, rate):
    first_new = beta_one * first + (1.0 - beta_one) * grad
    second_new = beta_two * second + (1.0 - beta_two) * grad * grad
    first_hat = first_new / (1.0 - beta_one**STEP)
    second_hat = second_new / (1.0 - beta_two**STEP)
    new_weight = weight - rate * (
        first_hat / (jnp.sqrt(second_hat) + adam_eps) + decay_rate * weight
    )
    return (new_weight, first_new, second_new)


def body(
    images,
    labels,
    background,
    patients,
    *state,
):
    masters, firsts, seconds = state[:9], state[9:18], state[18:]
    stem_w, embed_w, token_params, qkv_w, out_w, mlp_in_w, mlp_out_w, skip_w, decoder_w = masters
    n_dp = lax.axis_size("dp")
    n_mp = lax.axis_size("mp")
    mp_id = lax.axis_index("mp")
    core = mp_id & 1
    slices = images.shape[0] // n_mp
    rows = slices * PAD
    shared = Shared(stem_w, embed_w, token_params, decoder_w)
    attn_cut = qkv_w.shape[1]

    core_id = core.reshape(1)
    token_t = pad_to(token_params.T, 1, 2 * LANES)
    aligned = shared.stem_rows % 16 == 0 and shared.token_rows % 16 == 0
    mlp_block = jnp.concatenate([mlp_in_w, mlp_out_w.T], axis=1).astype(bf16)
    mlp_all = lax.all_gather(mlp_block, ("mp", "dp"), axis=0, tiled=True).reshape(n_mp, D, -1)
    if aligned:
        first_block = pack(
            core_id, stem_w, embed_w, token_t, shared.half_flat(decoder_w), shared.cuts[-1]
        )
    else:
        dec_half = lax.dynamic_index_in_dim(shared.half_flat(decoder_w), core, 0, keepdims=False)
        first_block = jnp.concatenate(
            [
                stack_columns(half_columns(stem_w, core), LANES),
                stack_columns(half_columns(embed_w, core), LANES),
                half_columns(token_t, core),
                dec_half,
            ],
            axis=0,
        ).astype(bf16)
    attn_block = jnp.concatenate([qkv_w, out_w.T], axis=1).astype(bf16)
    skip_block = half_columns(skip_w, core).astype(bf16)

    first, split, skip = Gather(first_block), Gather(attn_block), Gather(skip_block)
    order = list(reversed(range(log_two(n_dp))))
    for bit in order[3:]:
        for part in (first, split, skip):
            part.step("dp", bit)
    top, middle_bit, last = order[:3]
    first.start("dp", top)
    split.start("dp", top)
    token = first.finish()
    first.start("dp", last)
    token = split.finish(after=(token,))
    split.start("dp", middle_bit)
    skip.value = run_gate(skip.value, token)
    skip.start("dp", top)
    token = first.finish(after=(token,))
    first.start("dp", middle_bit)
    token = split.finish(after=(token,))
    split.start("dp", last)
    token = skip.finish(after=(token,))
    skip.start("dp", middle_bit)
    token = split.finish(after=(token,))
    split.start("mp", 1)
    token = first.finish(after=(token,))
    first_own = first.value
    first_pair = [
        value.reshape(n_dp, -1, LANES) for value in (first_own, swap(first_own, "mp", 0))
    ]
    by_core = lambda pair: [
        jnp.where(core == 0, pair[0], pair[1]), jnp.where(core == 0, pair[1], pair[0])
    ]
    dec_parts = by_core([value[:, shared.cuts[3] :] for value in first_pair])
    if aligned:
        stem_b, embed_b, table = unpack(core_id, *first_pair)
    else:
        both = [shared.pieces(value) for value in by_core(first_pair)]
        side = lambda k: jnp.concatenate([both[0][k], both[1][k]], axis=-1)
        stem_b = side(0).reshape(PIXELS, C_STEM)
        embed_b = side(1).reshape(C_STEM, D)
        table = side(2).reshape(D, 2 * LANES).T.astype(f32)
    dec_flat = jnp.stack(dec_parts, axis=1).reshape(n_dp, -1)[:, : shared.flat].reshape(-1)
    dec_b, one_b, two_b, three_b, head_b = split_decoder(dec_flat)
    three_four = block_diag(three_b, 4)
    big_head = big_head_of(head_b)
    token = skip.finish(after=(token, dec_b, one_b, two_b, three_four, big_head, table))
    skip.start("dp", last)
    token = split.finish(after=(token,))
    attn_weights = split.value

    attn_all = (attn_weights, swap(attn_weights, "mp", 0))

    take = lambda value: lax.dynamic_slice_in_dim(value, mp_id * slices, slices, 0)
    pixels = pad_to(take(images), 1, PAD).reshape(rows, PIXELS)
    label_own = jnp.pad(take(labels), ((0, 0), (0, PAD - PATCHES), (0, 0)), constant_values=-1)
    label_own = label_own.reshape(rows, PIXELS)
    keep = (1 - take(background)).astype(f32)
    owner = (take(patients)[:, None] == jnp.arange(PATIENTS, dtype=jnp.int32)).astype(f32)

    hidden, slope_stem, embed, normed, triple, context = enter(
        pixels, stem_b, embed_b, table, attn_all, attn_cut
    )
    resid, normed2, slope_mlp, inner, resid2, final_low = middle(
        context, embed, table, attn_all, mlp_all
    )
    skip_weights = skip.finish(after=(final_low,))
    skip_all = (skip_weights, swap(skip_weights, "mp", 0))
    slope0, level0, slope_skips, level1, level2, level3, logits, stats = leave(
        core_id, hidden, final_low, skip_all, dec_b, one_b, two_b, three_four, big_head, label_own
    )

    sums = jnp.sum(stats.reshape(slices, 3 * CLASSES + 1, 8 * LANES), axis=-1)
    class_sums = sums[:, : 3 * CLASSES]
    pat_sums = jnp.sum(owner[:, :, None] * class_sums[:, None, :], axis=0)
    cross_sum = jnp.sum(keep * sums[:, 3 * CLASSES])
    packed = jnp.concatenate(
        [pat_sums.reshape(-1), cross_sum[None], jnp.sum(keep)[None]]
    )
    packed = pad_to(packed, 0, 4 * LANES).reshape(4, LANES)
    packed = butterfly(packed).reshape(-1)
    pat_all = packed[: PATIENTS * 3 * CLASSES].reshape(PATIENTS, CLASSES, 3)
    ce_total = packed[PATIENTS * 3 * CLASSES]
    pixel_count = packed[PATIENTS * 3 * CLASSES + 1] * (PATCHES * PIXELS)
    pat_over, pat_pred, pat_true = pat_all[..., 0], pat_all[..., 1], pat_all[..., 2]
    denominator = pat_pred + pat_true + dice_eps
    dice = (2.0 * pat_over + dice_eps) / denominator
    count_floor = jnp.maximum(pixel_count, 1.0)
    loss = ce_total / count_floor + 1.0 - jnp.mean(dice)
    cells = PATIENTS * CLASSES
    over_coef = -2.0 / (cells * denominator)
    pred_coef = (2.0 * pat_over + dice_eps) / (cells * denominator * denominator)
    pick_own = lambda table: jnp.sum(owner[:, :, None] * table[None], axis=1)
    coef = jnp.concatenate(
        [pick_own(over_coef), pick_own(pred_coef), (keep / count_floor)[:, None]], axis=1
    )

    def x_sum(value):
        value = lax.reduce_precision(value, 8, 7).astype(bf16)
        return value.astype(f32) + swap(value, "mp", 1).astype(f32)

    def core_pair(send, own):
        return Scatter(own, swap(send, "mp", 0))

    grad_logits, grad_skips = leave_back(
        coef, logits, label_own, slope_skips, big_head, three_four, two_b
    )
    skip_send, skip_keep = skip_grad(core_id, hidden, grad_skips)
    grad_pre0, grad_resid2, grad_resid2_low, sums_f = turn(
        grad_skips, one_b, slope0, dec_b, resid2, table, after=(skip_send,)
    )
    low_bits = list(range(log_two(n_dp)))
    bit_y, bit_one, bit_two = low_bits[:3]
    skip_part = core_pair(skip_send, skip_keep)
    token = skip_part.step("dp", bit_y, bf16, after=(grad_pre0,))
    down_send, down_keep = half_grad(core_id, grad_resid2_low, inner, after=(token,))
    grad_pre, grad_resid, grad_resid_low, grad_context, sums_2 = middle_back(
        grad_resid2_low, mlp_all, slope_mlp, resid, table, grad_resid2, attn_all,
        after=(down_send,),
    )
    down = core_pair(down_send, down_keep)
    token = down.step("dp", bit_y, bf16, after=(grad_pre,))
    in_send, in_keep = half_grad(core_id, normed2, grad_pre, after=(token,))
    grad_triple = attn_back(triple, grad_context, after=(in_send,))
    into = core_pair(in_send, in_keep)
    token = into.step("mp", 1, bf16, after=(grad_triple,))
    token = skip_part.step("dp", bit_one, after=(token,))
    attn_send, attn_keep = attn_grad(
        normed, grad_triple, grad_resid_low, context, after=(token,)
    )
    decoder_halves = decoder_grad(
        level3, grad_logits, level2, level1, grad_skips, level0, final_low, grad_pre0,
        n_dp, shared.flat_rows, after=(attn_send,),
    )
    grad_embed_low, grad_pre_stem, grad_pos, sums_1 = enter_back(
        core_id, grad_triple, attn_all, embed, table, grad_resid, embed_b, grad_skips, skip_all,
        slope_stem, after=(decoder_halves,),
    )
    attn = core_pair(attn_send, attn_keep)
    token = attn.step("mp", 1, bf16, after=(grad_embed_low,))
    token = down.step("dp", bit_one, after=(token,))
    token = skip_part.step("dp", bit_two, after=(token,))
    token = into.step("dp", bit_y, after=(token,))
    if aligned:
        first_send, first_keep = first_grad(
            core_id, pixels, grad_pre_stem, hidden, grad_embed_low, grad_pos, sums_1, sums_2,
            sums_f, decoder_halves, shared.cuts[-1], after=(token,),
        )
    else:
        gains = jnp.concatenate([sums_1, sums_2, sums_f], axis=0).reshape(6, 8, D).sum(axis=1)
        grad_token = pad_to(jnp.concatenate([grad_pos[:PATCHES], gains], axis=0).T, 1, 2 * LANES)

        def first_half(which):
            blocks = lambda value: value.reshape(n_dp, -1, value.shape[-1])
            stem_part = t_matmul(pixels, half_columns(grad_pre_stem, which))
            embed_part = t_matmul(hidden, half_columns(grad_embed_low, which))
            return jnp.concatenate(
                [
                    stack_columns(blocks(stem_part), LANES),
                    stack_columns(blocks(embed_part), LANES),
                    blocks(half_columns(grad_token, which)),
                    lax.dynamic_index_in_dim(decoder_halves, which, 0, keepdims=False).astype(f32),
                ],
                axis=1,
            ).astype(bf16)

        first_send, first_keep = first_half(1 - core), first_half(core)
    wide = lambda value: value.reshape(-1, LANES)
    first = core_pair(wide(first_send), wide(first_keep))
    token = first_send
    token = first.step("dp", bit_y, after=(token,))
    token = down.step("dp", bit_two, after=(token,))
    token = into.step("dp", bit_one, after=(token,))
    for bit in low_bits[3:]:
        skip_part.step("dp", bit)
    skip_half = run_gate(skip_part.total(), token)
    skip_half = x_sum(skip_half)
    token = attn.step("dp", bit_y, after=(token,))
    token = into.step("dp", bit_two, after=(token,))
    token = down.step("mp", 1, after=(token,))
    token = first.step("dp", bit_one, after=(token,))
    token = attn.step("dp", bit_one, after=(token,))
    token = first.step("dp", bit_two, after=(token,))
    token = attn.step("dp", bit_two, after=(token,))
    for bit in low_bits[3:]:
        for part in (down, into, first, attn):
            part.step("dp", bit)
    down_own, in_own, attn_own = down.total(), into.total(), attn.total()
    first_half_sum = x_sum(first.total())

    square = lambda value: jnp.sum(value * value)
    n_copies = n_mp // 2
    local = (
        square(down_own)
        + square(in_own)
        + square(attn_own)
        + (square(skip_half) + square(first_half_sum)) / n_copies
    )
    total = butterfly(jnp.broadcast_to(local, (8, LANES)))[0, 0]
    grad_norm = jnp.sqrt(total)
    factor = jnp.minimum(1.0, clip_limit / (grad_norm + 1e-06))

    red_skip = jnp.concatenate(by_core([skip_half, swap(skip_half, "mp", 0)]), axis=1)
    own = [shared.pieces(part) for part in by_core([first_half_sum, swap(first_half_sum, "mp", 0)])]
    red_stem = jnp.concatenate([own[0][0], own[1][0]], axis=-1)
    red_embed = jnp.concatenate([own[0][1], own[1][1]], axis=-1)
    red_token = jnp.concatenate([own[0][2], own[1][2]], axis=-1)[:, : PATCHES + 6].T
    red_decoder = jnp.concatenate([own[0][3], own[1][3]], axis=0).reshape(-1)[: shared.flat]
    red_qkv = attn_own[:, :attn_cut]
    red_out = attn_own[:, attn_cut:].T
    red_in = in_own
    red_down = down_own.T
    reduced = (
        red_stem, red_embed, red_token, red_qkv, red_out, red_in, red_down, red_skip, red_decoder,
    )
    rates = [learn_rate] * 9
    rates[2] = token_rate
    results = [
        adamw(weight, grad * factor, first, second, rate)
        for weight, grad, first, second, rate in zip(
            masters, reduced, firsts, seconds, rates, strict=True
        )
    ]
    news = [item[0] for item in results]
    moms = [item[1] for item in results]
    secs = [item[2] for item in results]
    return (loss, pixel_count, grad_norm, *news, *moms, *secs)


def solution(mesh):
    weights = (
        P("dp", None),
        P("dp", None),
        P(None, "dp"),
        P("dp", "mp"),
        P("mp", "dp"),
        P("dp", "mp"),
        P("mp", "dp"),
        P("dp", None),
        P("dp"),
    )
    placed = (P("dp", None, None), P("dp", None, None), P("dp"), P("dp")) + weights * 3
    outs = (P(), P(), P()) + weights * 3
    return jax.shard_map(body, mesh=mesh, in_specs=placed, out_specs=outs, check_vma=False)
```

```python
import jax
import jax.numpy as jnp
import numpy as np
from jax import lax
from jax.experimental import pallas as pl
from jax.experimental.pallas import tpu as pltpu
from jax.sharding import PartitionSpec as P

D = 768
HEAD_DIM = 64
PATCHES = 196
PAD = 208
PIXELS = 256
C_STEM = 1024
CHAN_A = 256
CHAN_B = 128
CHAN_C = 64
CHAN_D = 16
CLASSES = 9
PATIENTS = 16
STEP = 10
GROUP = 32
LANES = 128

norm_eps = 1e-06
dice_eps = 1e-05
clip_limit = 0.002
learn_rate = 0.05
token_rate = 0.5
beta_one = 0.9
beta_two = 0.999
adam_eps = 1e-08
decay_rate = 0.01
highest = lax.Precision.HIGHEST
bf16 = jnp.bfloat16
f32 = jnp.float32
MIB = 1024 * 1024


def layer_norm(inputs, gain, shift):
    center = inputs - jnp.mean(inputs, axis=-1, keepdims=True)
    spread = jnp.mean(center * center, axis=-1, keepdims=True)
    return center * lax.rsqrt(spread + norm_eps) * gain + shift


def matmul(left, right):
    return jnp.dot(left, right, preferred_element_type=f32)


def matmul_t(left, right):
    return lax.dot_general(left, right, (((1,), (1,)), ((), ())), preferred_element_type=f32)


def t_matmul(left, right):
    return lax.dot_general(left, right, (((0,), (0,)), ((), ())), preferred_element_type=f32)


FULL = pl.BlockSpec(memory_space=pltpu.VMEM)
SCALAR = pl.BlockSpec(memory_space=pltpu.SMEM)
BLOCK = 256
CHUNK = 16
GELU_SCALE = 0.7978845608028654
GELU_CUBE = 0.044715


def cost(micros):
    return pl.CostEstimate(
        flops=int(micros * 2e9), bytes_accessed=int(micros * 6e6), transcendentals=0
    )


def params(size=27):
    return pltpu.CompilerParams(vmem_limit_bytes=size * MIB)


def run_after(kernel, count, after):
    extra = len(after)

    def ordered(*refs):
        kernel(*refs[:count], *refs[count + extra :])

    return ordered, [pl.BlockSpec(memory_space=pl.ANY)] * extra


def swap(value, axis, bit):
    size = lax.axis_size(axis)
    return lax.ppermute(value, axis, [(i, i ^ (1 << bit)) for i in range(size)])


def my_bit(axis, bit):
    return (lax.axis_index(axis) >> bit) & 1


def log_two(size):
    return size.bit_length() - 1


def gather_kernel(lanes, mine_ref, own_ref, other_ref, out_ref):
    mine = mine_ref[0]
    for which, source_ref in ((mine, own_ref), (1 - mine, other_ref)):
        if lanes:
            width = own_ref.shape[1]
            out_ref[:, pl.ds(pl.multiple_of(which * width, LANES), width)] = source_ref[...]
        else:
            for a in range(out_ref.shape[0]):
                out_ref[a, which] = source_ref[a]


def gate_kernel(value_ref, *refs):
    pass


def run_gate(value, *tokens):
    anywhere = pl.BlockSpec(memory_space=pl.ANY)
    return pl.pallas_call(
        gate_kernel,
        in_specs=[anywhere] * (1 + len(tokens)),
        out_specs=anywhere,
        out_shape=jax.ShapeDtypeStruct(value.shape, value.dtype),
        input_output_aliases={0: 0},
        name="gate",
    )(value, *tokens)


class Gather:
    def __init__(self, block):
        self.value = block
        self.bits = []
        self.pending = None

    def start(self, axis, bit):
        self.pending = (axis, bit, swap(self.value, axis, bit))
        return self.value

    def finish(self, after=()):
        axis, bit, other = self.pending
        rows, columns = self.value.shape
        lanes = axis == "mp"
        if lanes:
            shape, out = (rows, columns), (rows, 2 * columns)
        else:
            ahead = 2 ** sum(b > bit for b in self.bits)
            self.bits.append(bit)
            shape = (ahead, rows // ahead, columns)
            out = (ahead, 2, rows // ahead, columns)
        kernel, waits = run_after(lambda *refs: gather_kernel(lanes, *refs), 3, after)
        value = pl.pallas_call(
            kernel,
            in_specs=[SCALAR] + [FULL] * 2 + waits,
            out_specs=FULL,
            out_shape=jax.ShapeDtypeStruct(out, self.value.dtype),
            compiler_params=params(12),
            cost_estimate=cost(0.1),
            name="gather_step",
        )(my_bit(axis, bit).reshape(1), self.value.reshape(shape), other.reshape(shape), *after)
        self.value = value.reshape(-1, value.shape[-1])
        return self.value

    def step(self, axis, bit, after=()):
        self.start(axis, bit)
        return self.finish(after)


def scatter_kernel(lanes, mine_ref, *refs):
    terms, (send_ref, keep_ref) = refs[:-2], refs[-2:]
    mine = mine_ref[0]
    for which, out_ref in ((1 - mine, send_ref), (mine, keep_ref)):
        if lanes:
            width = out_ref.shape[1]
            cols = pl.ds(pl.multiple_of(which * width, LANES), width)
            total = sum(term[:, cols].astype(f32) for term in terms)
            out_ref[...] = total.astype(out_ref.dtype)
        else:
            total = sum(term[0, which].astype(f32) for term in terms)
            out_ref[0] = total.astype(out_ref.dtype)


class Scatter:
    def __init__(self, *terms):
        self.bits = list(reversed(range(log_two(lax.axis_size("dp")))))
        self.terms = list(terms)
        self.send = None

    def step(self, axis, bit, kept_type=f32, after=()):
        rows, columns = self.terms[0].shape
        lanes = axis == "mp"
        if lanes:
            shape, half = (rows, columns), (rows, columns // 2)
            steps = max(rows // (LANES + CHUNK), 1)
            steps = next(k for k in range(steps, 0, -1) if rows % (k * CHUNK) == 0 or k == 1)
            block = lambda size: pl.BlockSpec((rows // steps, size[1]), lambda i: (i, 0))
        else:
            steps = 2 ** self.bits.index(bit)
            self.bits.remove(bit)
            shape = (steps, 2, rows // (2 * steps), columns)
            half = (steps, rows // (2 * steps), columns)
            block = lambda size: pl.BlockSpec(
                (1,) + size[1:], lambda i: (i,) + (0,) * (len(size) - 1)
            )
        count = len(self.terms)
        body_kernel = lambda *refs: scatter_kernel(lanes, *refs)
        kernel, waits = run_after(body_kernel, 1 + count, after)
        send, kept = pl.pallas_call(
            kernel,
            grid=(steps,),
            in_specs=[SCALAR] + [block(shape)] * count + waits,
            out_specs=[block(half)] * 2,
            out_shape=[jax.ShapeDtypeStruct(half, bf16), jax.ShapeDtypeStruct(half, kept_type)],
            compiler_params=params(12),
            cost_estimate=cost(0.1),
            name="scatter_step",
        )(my_bit(axis, bit).reshape(1), *[term.reshape(shape) for term in self.terms], *after)
        flat = lambda value: value.reshape(-1, value.shape[-1])
        self.send = flat(send)
        self.terms = [flat(kept), swap(self.send, axis, bit)]
        return self.send

    def total(self):
        return sum(term.astype(f32) for term in self.terms)


def butterfly(value):
    def hop(value, moves):
        size = lax.axis_size("dp") * lax.axis_size("mp")
        get = lambda move: lax.ppermute(value, ("dp", "mp"), [(i, i ^ move) for i in range(size)])
        if len(moves) == 1:
            return value + get(moves[0])
        one, two = moves
        first, second, third = get(one), get(two), get(one | two)
        return (value + first) + (second + third)

    value = hop(value, (1,))
    bits = log_two(lax.axis_size("dp"))
    moves = [2] + [4 << bit for bit in range(bits)]
    for i in range(0, len(moves), 2):
        value = hop(value, tuple(moves[i : i + 2]))
    return value


def gelu_pair(value):
    square = value * value
    wave = jnp.tanh(value * (GELU_SCALE + (GELU_SCALE * GELU_CUBE) * square))
    half = 0.5 + 0.5 * wave
    inner = GELU_SCALE + (3.0 * GELU_SCALE * GELU_CUBE) * square
    return value * half, half + 0.5 * value * (1.0 - wave * wave) * inner


def norm_rows(x_ref, gain, shift, out_ref):
    @pl.loop(0, x_ref.shape[0] // CHUNK, unroll=13)
    def _(i):
        rows = pl.ds(pl.multiple_of(i * CHUNK, CHUNK), CHUNK)
        out_ref[rows, :] = layer_norm(x_ref[rows, :], gain, shift).astype(out_ref.dtype)


def norm_back_rows(x_ref, gain, grad_ref, extra_ref, out_ref, low_ref, sum_ref):
    sum_ref[...] = jnp.zeros_like(sum_ref)

    @pl.loop(0, x_ref.shape[0] // CHUNK, unroll=13)
    def _(i):
        rows = pl.ds(pl.multiple_of(i * CHUNK, CHUNK), CHUNK)
        value = x_ref[rows, :]
        grad = grad_ref[rows, :]
        center = value - jnp.mean(value, axis=-1, keepdims=True)
        scale = lax.rsqrt(jnp.mean(center * center, axis=-1, keepdims=True) + norm_eps)
        hat = center * scale
        for k, term in enumerate((grad * hat, grad)):
            sum_ref[8 * k : 8 * k + 8, :] += term[:8] + term[8:]
        pull = grad * gain
        mean_one = jnp.mean(pull, axis=-1, keepdims=True)
        mean_two = jnp.mean(pull * hat, axis=-1, keepdims=True)
        result = scale * (pull - mean_one - hat * mean_two)
        if extra_ref is not None:
            result = result + extra_ref[rows, :]
        out_ref[rows, :] = result
        low_ref[rows, :] = result.astype(bf16)


def gelu_blocks(width):
    return [slice(j, j + BLOCK) for j in range(0, width, BLOCK)]


def soft_rows(scores, column):
    scores = jnp.where(column < PATCHES, scores * HEAD_DIM ** (-0.5), -jnp.inf)
    top = jnp.max(scores, axis=-1, keepdims=True)
    weight = jnp.exp(scores - top)
    return weight * (1.0 / jnp.sum(weight, axis=-1, keepdims=True))


def enter_kernel(
    pixels_ref, stem_ref, embed_w_ref, token_ref, own_ref, other_ref,
    hidden_ref, slope_ref, embed_ref, normed_ref, tri_ref, ctx_ref,
):
    for cols in gelu_blocks(C_STEM):
        value, slope = gelu_pair(matmul(pixels_ref[...], stem_ref[:, cols]))
        hidden_ref[:, cols] = value.astype(bf16)
        slope_ref[:, cols] = slope.astype(bf16)
    slices = pixels_ref.shape[0] // PAD
    for cols in gelu_blocks(D):
        value = matmul(hidden_ref[...], embed_w_ref[:, cols])
        for s in range(slices):
            rows = slice(s * PAD, (s + 1) * PAD)
            embed_ref[rows, cols] = value[rows] + token_ref[:PAD, cols]
    gain, shift = token_ref[PATCHES : PATCHES + 1, :], token_ref[PATCHES + 1 : PATCHES + 2, :]
    norm_rows(embed_ref, gain, shift, normed_ref)
    width = tri_ref.shape[2]
    heads = width // (3 * HEAD_DIM)
    stride = width + width // 3
    column = lax.broadcasted_iota(jnp.int32, (PAD, PAD), 1)
    for p in range(tri_ref.shape[0]):
        start = (p % 2) * stride
        weight_ref = (own_ref, other_ref)[p // 2]
        tri_ref[p] = matmul(normed_ref[...], weight_ref[:, start : start + width]).astype(bf16)

    @pl.loop(0, tri_ref.shape[0])
    def _(p):
        for s in range(slices):
            rows = slice(s * PAD, (s + 1) * PAD)
            for h in range(heads):
                base = h * 3 * HEAD_DIM
                queries = tri_ref[p, rows, base : base + HEAD_DIM]
                keys_low = tri_ref[p, rows, base + HEAD_DIM : base + 2 * HEAD_DIM]
                values = tri_ref[p, rows, base + 2 * HEAD_DIM : base + 3 * HEAD_DIM]
                attend = soft_rows(matmul_t(queries, keys_low), column)
                context = matmul(attend.astype(bf16), values)
                ctx_ref[p, rows, h * HEAD_DIM : (h + 1) * HEAD_DIM] = context.astype(bf16)


def enter(pixels, stem_b, embed_b, tokens, attn_all, width):
    rows = pixels.shape[0]
    parts = 4
    return pl.pallas_call(
        enter_kernel,
        in_specs=[FULL] * 6,
        out_specs=[FULL] * 6,
        out_shape=[
            jax.ShapeDtypeStruct((rows, C_STEM), bf16),
            jax.ShapeDtypeStruct((rows, C_STEM), bf16),
            jax.ShapeDtypeStruct((rows, D), f32),
            jax.ShapeDtypeStruct((rows, D), bf16),
            jax.ShapeDtypeStruct((parts, rows, width), bf16),
            jax.ShapeDtypeStruct((parts, rows, width // 3), bf16),
        ],
        compiler_params=params(),
        cost_estimate=cost(13),
        name="enter",
    )(pixels, stem_b, embed_b, tokens, *attn_all)


def middle_kernel(
    ctx_ref, embed_ref, token_ref, own_ref, other_ref, mlp_ref,
    resid_ref, normed2_ref, slope_ref, inner_ref, resid2_ref, final_ref,
):
    p = pl.program_id(0)

    @pl.when(p == 0)
    def _():
        part = ctx_ref.shape[2]
        stride = 4 * part
        for q in range(ctx_ref.shape[0]):
            start = (q % 2) * stride + 3 * part
            weight_ref = (own_ref, other_ref)[q // 2]
            term = matmul_t(ctx_ref[q], weight_ref[:, start : start + part])
            if q == 0:
                resid_ref[...] = embed_ref[...] + term
            else:
                resid_ref[...] += term
        gain, shift = token_ref[PATCHES + 2 : PATCHES + 3, :], token_ref[PATCHES + 3 : PATCHES + 4, :]
        norm_rows(resid_ref, gain, shift, normed2_ref)
        resid2_ref[...] = resid_ref[...]

    each = mlp_ref.shape[2] // 2
    for cols in gelu_blocks(each):
        value, slope = gelu_pair(matmul(normed2_ref[...], mlp_ref[0, :, cols]))
        inner_ref[0, :, cols] = value.astype(bf16)
        slope_ref[0, :, cols] = slope.astype(bf16)
    resid2_ref[...] += matmul_t(inner_ref[0], mlp_ref[0, :, each:])

    @pl.when(p == pl.num_programs(0) - 1)
    def _():
        gain, shift = token_ref[PATCHES + 4 : PATCHES + 5, :], token_ref[PATCHES + 5 : PATCHES + 6, :]
        norm_rows(resid2_ref, gain, shift, final_ref)


def whole_of(value):
    return pl.BlockSpec(value.shape, lambda *_: (0,) * len(value.shape))


def part_of(value):
    rest = len(value.shape) - 1
    return pl.BlockSpec((1,) + tuple(value.shape[1:]), lambda i, *_: (i,) + (0,) * rest)


def middle(context, embed, tokens, attn_all, mlp_all):
    rows = embed.shape[0]
    parts, _, width = mlp_all.shape
    each = width // 2
    outs = [
        jax.ShapeDtypeStruct((rows, D), f32),
        jax.ShapeDtypeStruct((rows, D), bf16),
        jax.ShapeDtypeStruct((parts, rows, each), bf16),
        jax.ShapeDtypeStruct((parts, rows, each), bf16),
        jax.ShapeDtypeStruct((rows, D), f32),
        jax.ShapeDtypeStruct((rows, D), bf16),
    ]
    values = (context, embed, tokens, *attn_all)
    return pl.pallas_call(
        middle_kernel,
        grid=(parts,),
        in_specs=[whole_of(value) for value in values] + [part_of(mlp_all)],
        out_specs=[(part_of if len(out.shape) == 3 else whole_of)(out) for out in outs],
        out_shape=outs,
        compiler_params=params(),
        cost_estimate=cost(2),
        name="middle",
    )(*values, mlp_all)


def class_probs(logits_ref, rows, group):
    width = CLASSES * LANES
    values = [
        logits_ref[rows, group * width + c * LANES : group * width + (c + 1) * LANES]
        for c in range(CLASSES)
    ]
    top = values[0]
    for value in values[1:]:
        top = jnp.maximum(top, value)
    weights = [jnp.exp(value - top) for value in values]
    total = weights[0]
    for weight in weights[1:]:
        total = total + weight
    scale = 1.0 / total
    return values, [weight * scale for weight in weights], top + jnp.log(total)


SPLIT_A = 4 * CHAN_B
SPLIT_B = SPLIT_A + 16 * CHAN_C
SKIPW = SPLIT_B + 64 * CHAN_D


def leave_kernel(
    core_ref, hidden_ref, final_ref, skip_own_ref, skip_other_ref, dec_ref, one_ref, two_ref, three_ref, head_ref, label_ref,
    slope0_ref, level0_ref, slope_ref, level1_ref, level2_ref, level3_ref, logits_ref, stats_ref,
    skips,
):
    value, slope = gelu_pair(matmul(final_ref[...], dec_ref[...]))
    level0_ref[...] = value.astype(bf16)
    slope0_ref[...] = slope

    half = skip_own_ref.shape[1]
    core = core_ref[0]
    for which, weight_ref in ((core, skip_own_ref), (1 - core, skip_other_ref)):
        for j in range(0, half, BLOCK):
            cols = pl.ds(pl.multiple_of(which * half + j, LANES), BLOCK)
            skips[:, cols] = matmul(hidden_ref[...], weight_ref[:, j : j + BLOCK])

    def stage(source, weight, out_ref, cols, skip_cols):
        pre = matmul(source, weight) + skips[:, skip_cols : skip_cols + BLOCK]
        value, slope = gelu_pair(pre)
        out_ref[:, cols : cols + BLOCK] = value.astype(bf16)
        slope_ref[:, skip_cols : skip_cols + BLOCK] = slope.astype(bf16)

    for i in range(2):
        stage(level0_ref[...], one_ref[:, i * BLOCK : (i + 1) * BLOCK], level1_ref, i * BLOCK, i * BLOCK)
    for i in range(4):
        stage(
            level1_ref[:, i * CHAN_B : (i + 1) * CHAN_B], two_ref[...], level2_ref, i * BLOCK,
            SPLIT_A + i * BLOCK,
        )
    for i in range(4):
        stage(
            level2_ref[:, i * BLOCK : (i + 1) * BLOCK], three_ref[...], level3_ref, i * BLOCK,
            SPLIT_B + i * BLOCK,
        )
    inner = head_ref.shape[0]
    width = head_ref.shape[1]
    groups = level3_ref.shape[1] // inner
    for g in range(groups):
        logits_ref[:, g * width : (g + 1) * width] = matmul(
            level3_ref[:, g * inner : (g + 1) * inner], head_ref[...]
        )
    stats_ref[...] = jnp.zeros_like(stats_ref)
    slices = stats_ref.shape[0]
    per_slice = PAD // CHUNK

    @pl.loop(0, slices)
    def _(s):
        @pl.loop(0, per_slice)
        def _(i):
            start = pl.multiple_of(s * PAD + i * CHUNK, CHUNK)
            rows = pl.ds(start, CHUNK)
            row_id = lax.broadcasted_iota(jnp.int32, (CHUNK, LANES), 0) + i * CHUNK
            inside = (row_id < PATCHES).astype(f32)
            for g in range(groups):
                values, probs, log_total = class_probs(logits_ref, rows, g)
                label = label_ref[rows, g * LANES : (g + 1) * LANES]
                cross = jnp.zeros((CHUNK, LANES), f32)
                for c in range(CLASSES):
                    hot = (label == c).astype(f32)
                    cross = cross + hot * (log_total - values[c])
                    for k, term in enumerate((hot * probs[c], inside * probs[c], hot)):
                        spot = 8 * (3 * c + k)
                        stats_ref[s, spot : spot + 8, :] += term[:8] + term[8:]
                spot = 8 * 3 * CLASSES
                stats_ref[s, spot : spot + 8, :] += cross[:8] + cross[8:]


def leave(core, hidden, final_low, skip_all, dec_b, one_b, two_b, three_four, big_head, labels):
    rows = hidden.shape[0]
    slices = rows // PAD
    stat_rows = 8 * (3 * CLASSES + 1)
    return pl.pallas_call(
        leave_kernel,
        in_specs=[SCALAR] + [FULL] * 10,
        out_specs=[FULL] * 8,
        out_shape=[
            jax.ShapeDtypeStruct((rows, CHAN_A), f32),
            jax.ShapeDtypeStruct((rows, CHAN_A), bf16),
            jax.ShapeDtypeStruct((rows, SKIPW), bf16),
            jax.ShapeDtypeStruct((rows, 4 * CHAN_B), bf16),
            jax.ShapeDtypeStruct((rows, 16 * CHAN_C), bf16),
            jax.ShapeDtypeStruct((rows, 64 * CHAN_D), bf16),
            jax.ShapeDtypeStruct((rows, CLASSES * PIXELS), f32),
            jax.ShapeDtypeStruct((slices, stat_rows, LANES), f32),
        ],
        scratch_shapes=[pltpu.VMEM((rows, SKIPW), f32)],
        compiler_params=params(),
        cost_estimate=cost(12),
        name="leave",
    )(core, hidden, final_low, *skip_all, dec_b, one_b, two_b, three_four, big_head, labels)


def leave_back_kernel(
    coef_ref, logits_ref, label_ref, slope_ref, head_ref, three_ref, two_ref,
    g_logits_ref, g_skips_ref,
):
    inner = head_ref.shape[0]
    width = head_ref.shape[1]
    groups = 64 * CHAN_D // inner
    slices = logits_ref.shape[0] // PAD

    @pl.loop(0, slices)
    def _(s):
        cross_scale = coef_ref[s, 2 * CLASSES]

        @pl.loop(0, PAD // CHUNK)
        def _(i):
            start = pl.multiple_of(s * PAD + i * CHUNK, CHUNK)
            rows = pl.ds(start, CHUNK)
            row_id = lax.broadcasted_iota(jnp.int32, (CHUNK, LANES), 0) + i * CHUNK
            inside = (row_id < PATCHES).astype(f32)
            for g in range(groups):
                _, probs, _ = class_probs(logits_ref, rows, g)
                label = label_ref[rows, g * LANES : (g + 1) * LANES]
                mean = jnp.zeros((CHUNK, LANES), f32)
                pulls = []
                for c in range(CLASSES):
                    pull = jnp.where(label == c, coef_ref[s, c], 0.0) + coef_ref[s, CLASSES + c]
                    pulls.append(pull)
                    mean = mean + probs[c] * pull
                mean = mean - cross_scale
                for c in range(CLASSES):
                    grad = probs[c] * (pulls[c] - mean)
                    grad = grad - jnp.where(label == c, cross_scale, 0.0)
                    spot = g * width + c * LANES
                    g_logits_ref[rows, spot : spot + LANES] = (grad * inside).astype(bf16)

    for i in range(4):
        g, part = (i * BLOCK) // inner, (i * BLOCK) % inner
        grad = matmul_t(g_logits_ref[:, g * width : (g + 1) * width], head_ref[part : part + BLOCK, :])
        cols = slice(SPLIT_B + i * BLOCK, SPLIT_B + (i + 1) * BLOCK)
        g_skips_ref[:, cols] = (grad * slope_ref[:, cols].astype(f32)).astype(bf16)
    for i in range(4):
        source = g_skips_ref[:, SPLIT_B + i * BLOCK : SPLIT_B + (i + 1) * BLOCK]
        cols = slice(SPLIT_A + i * BLOCK, SPLIT_A + (i + 1) * BLOCK)
        g_skips_ref[:, cols] = (matmul_t(source, three_ref[...]) * slope_ref[:, cols].astype(f32)).astype(bf16)
    for i in range(4):
        source = g_skips_ref[:, SPLIT_A + i * BLOCK : SPLIT_A + (i + 1) * BLOCK]
        cols = slice(i * CHAN_B, (i + 1) * CHAN_B)
        g_skips_ref[:, cols] = (matmul_t(source, two_ref[...]) * slope_ref[:, cols].astype(f32)).astype(bf16)


def leave_back(coef, logits, labels, slope, big_head, three_four, two_b):
    rows = logits.shape[0]
    return pl.pallas_call(
        leave_back_kernel,
        in_specs=[SCALAR] + [FULL] * 6,
        out_specs=[FULL] * 2,
        out_shape=[
            jax.ShapeDtypeStruct((rows, CLASSES * PIXELS), bf16),
            jax.ShapeDtypeStruct((rows, SKIPW), bf16),
        ],
        compiler_params=params(),
        cost_estimate=cost(6),
        name="leave_back",
    )(coef, logits, labels, slope, big_head, three_four, two_b)


def skip_grad_kernel(core_ref, hidden_ref, g_skips_ref, send_ref, keep_ref):
    half = send_ref.shape[1]
    core = core_ref[0]
    for which, out_ref in ((1 - core, send_ref), (core, keep_ref)):
        for j in range(0, half, half // 2):
            cols = pl.ds(pl.multiple_of(which * half + j, LANES), half // 2)
            out_ref[:, j : j + half // 2] = t_matmul(hidden_ref[...], g_skips_ref[:, cols]).astype(
                bf16
            )


def skip_grad(core, hidden, g_skips):
    shape = (hidden.shape[1], g_skips.shape[1] // 2)
    return pl.pallas_call(
        skip_grad_kernel,
        in_specs=[SCALAR] + [FULL] * 2,
        out_specs=[FULL] * 2,
        out_shape=[jax.ShapeDtypeStruct(shape, bf16)] * 2,
        compiler_params=params(),
        cost_estimate=cost(3.5),
        name="skip_grad",
    )(core, hidden, g_skips)


def turn_kernel(
    g_skips_ref, one_ref, slope0_ref, dec_ref, resid2_ref, token_ref,
    g_pre0_ref, g_resid2_ref, low_ref, sums_ref, g_final,
):
    grad = matmul_t(g_skips_ref[:, :SPLIT_A], one_ref[...])
    g_pre0_ref[...] = (grad * slope0_ref[...]).astype(bf16)
    g_final[...] = matmul_t(g_pre0_ref[...], dec_ref[...])
    norm_back_rows(
        resid2_ref, token_ref[PATCHES + 4 : PATCHES + 5, :], g_final, None, g_resid2_ref, low_ref, sums_ref
    )


def turn(g_skips, one_b, slope0, dec_b, resid2, tokens, after=()):
    rows = resid2.shape[0]
    kernel, waits = run_after(turn_kernel, 6, after)
    return pl.pallas_call(
        kernel,
        in_specs=[FULL] * 6 + waits,
        out_specs=[FULL] * 4,
        out_shape=[
            jax.ShapeDtypeStruct((rows, CHAN_A), bf16),
            jax.ShapeDtypeStruct((rows, D), f32),
            jax.ShapeDtypeStruct((rows, D), bf16),
            jax.ShapeDtypeStruct((16, D), f32),
        ],
        scratch_shapes=[pltpu.VMEM((rows, D), f32)],
        compiler_params=params(),
        cost_estimate=cost(3),
        name="turn",
    )(g_skips, one_b, slope0, dec_b, resid2, tokens, *after)


FLAT_DEC = D * CHAN_A // LANES
FLAT_ONE = FLAT_DEC + CHAN_A * 4 * CHAN_B // LANES
FLAT_TWO = FLAT_ONE + CHAN_B * 4 * CHAN_C // LANES
FLAT_THREE = FLAT_TWO + CHAN_C * 4 * CHAN_D // LANES


def decoder_grad_kernel(
    level3_ref, g_logits_ref, level2_ref, level1_ref, g_skips_ref, level0_ref, final_ref, g_pre0_ref,
    out_ref, flat_ref, square_ref,
):
    size = out_ref.shape[1]
    flat = (FLAT_THREE * LANES + 4 * CLASSES * CHAN_D) // size
    inner, width = GROUP * CHAN_D, CLASSES * LANES
    tail = flat_ref.shape[0] - FLAT_THREE
    flat_ref[FLAT_THREE:, :] = jnp.zeros((tail, LANES), f32)

    def spread(value, base, count):
        for j in range(count):
            flat_ref[pl.ds(base + j, value.shape[0], stride=count), :] = value[
                :, j * LANES : (j + 1) * LANES
            ]

    spread(t_matmul(final_ref[...], g_pre0_ref[...]), 0, CHAN_A // LANES)
    spread(t_matmul(level0_ref[...], g_skips_ref[:, :SPLIT_A]), FLAT_DEC, SPLIT_A // LANES)
    three = jnp.zeros((CHAN_C, 4 * CHAN_D), f32)
    two = jnp.zeros((CHAN_B, 4 * CHAN_C), f32)
    for i in range(4):
        big = t_matmul(
            level2_ref[:, i * BLOCK : (i + 1) * BLOCK],
            g_skips_ref[:, SPLIT_B + i * BLOCK : SPLIT_B + (i + 1) * BLOCK],
        )
        for k in range(4):
            at = slice(k * CHAN_C, (k + 1) * CHAN_C)
            three += big[at, at]
        two += t_matmul(
            level1_ref[:, i * CHAN_B : (i + 1) * CHAN_B],
            g_skips_ref[:, SPLIT_A + i * BLOCK : SPLIT_A + (i + 1) * BLOCK],
        )
    spread(two, FLAT_ONE, 4 * CHAN_C // LANES)
    square_ref[...] = three
    flat_ref[FLAT_TWO:FLAT_THREE, :] = jnp.concatenate(
        [square_ref[pl.ds(j, CHAN_C // 2, stride=2), :] for j in range(2)], axis=1
    )
    head = jnp.zeros((CHAN_D, width), f32)
    row = lax.broadcasted_iota(jnp.int32, (CHAN_D, width), 0)
    across = lax.broadcasted_iota(jnp.int32, (CHAN_D, width), 1)
    parent = (across // 4) % GROUP
    for g in range(level3_ref.shape[1] // inner):
        big = t_matmul(
            level3_ref[:, g * inner : (g + 1) * inner], g_logits_ref[:, g * width : (g + 1) * width]
        )
        for k in range(GROUP):
            head += jnp.where(parent == k, big[k * CHAN_D : (k + 1) * CHAN_D, :], 0.0)
    column = lax.broadcasted_iota(jnp.int32, (width, LANES), 0)
    target = lax.broadcasted_iota(jnp.int32, (width, LANES), 1)
    pick = target == (column % 4) * CLASSES + column // (GROUP * 4)
    small = jnp.dot(head, pick.astype(f32), precision=highest, preferred_element_type=f32)
    lane = lax.broadcasted_iota(jnp.int32, (1, LANES), 1)
    lines = [jnp.zeros((1, LANES), f32) for _ in range(8)]
    for k in range(CHAN_D):
        line, start = divmod(k * 4 * CLASSES, LANES)
        value = small[k : k + 1, :]
        if start:
            value = pltpu.roll(value, start, 1)
        lines[line] = lines[line] + jnp.where(lane >= start, value, 0.0)
        if start + 4 * CLASSES > LANES:
            lines[line + 1] = lines[line + 1] + jnp.where(
                lane < start + 4 * CLASSES - LANES, value, 0.0
            )
    flat_ref[FLAT_THREE : FLAT_THREE + 8, :] = jnp.concatenate(lines, axis=0)

    rows = out_ref.shape[2]
    line_id = lax.broadcasted_iota(jnp.int32, (rows, LANES), 0)
    lane_id = lax.broadcasted_iota(jnp.int32, (rows, LANES), 1)
    for d in range(size):
        for c in range(2):
            first, start = divmod(d * flat + c * rows * LANES, LANES)
            value = flat_ref[first : first + rows, :]
            if start:
                after = flat_ref[first + 1 : first + 1 + rows, :]
                value = jnp.where(
                    lane_id < LANES - start,
                    pltpu.roll(value, LANES - start, 1),
                    pltpu.roll(after, LANES - start, 1),
                )
            inside = (line_id + c * rows) * LANES + lane_id < flat
            out_ref[c, d] = jnp.where(inside, value, 0.0).astype(bf16)


def decoder_grad(
    level3, g_logits, level2, level1, g_skips, level0, final_low, g_pre0, size, rows, after=()
):
    kernel, waits = run_after(decoder_grad_kernel, 8, after)
    flat = (FLAT_THREE * LANES + 4 * CLASSES * CHAN_D) // size
    lines = (size - 1) * flat // LANES + 2 * rows + 8
    lines = -(-max(lines, FLAT_THREE + 8) // 8) * 8
    return pl.pallas_call(
        kernel,
        in_specs=[FULL] * 8 + waits,
        out_specs=FULL,
        out_shape=jax.ShapeDtypeStruct((2, size, rows, LANES), bf16),
        scratch_shapes=[pltpu.VMEM((lines, LANES), f32), pltpu.VMEM((CHAN_C, 4 * CHAN_D), f32)],
        compiler_params=params(),
        cost_estimate=cost(3),
        name="decoder_grad",
    )(level3, g_logits, level2, level1, g_skips, level0, final_low, g_pre0, *after)


def first_grad_kernel(
    core_ref, pixels_ref, g_stem_ref, hidden_ref, low_ref, pos_ref, sums1_ref, sums2_ref, sumsf_ref,
    dec_ref, send_ref, keep_ref, token_ref,
):
    core = core_ref[0]
    size = send_ref.shape[0]
    stem_rows, embed_rows, token_rows = PIXELS // size, C_STEM // size, D // size
    token_ref[...] = jnp.zeros_like(token_ref)
    token_ref[:PATCHES, :] = pos_ref[:PATCHES, :]
    for i, sums_ref in enumerate((sums1_ref, sums2_ref, sumsf_ref)):
        for k in range(2):
            at = PATCHES + 2 * i + k
            token_ref[at : at + 1, :] = jnp.sum(
                sums_ref[8 * k : 8 * k + 8, :], axis=0, keepdims=True
            )
    for which, out_ref in ((1 - core, send_ref), (core, keep_ref)):
        spot = 0
        half = C_STEM // 2
        for j in range(0, half, BLOCK):
            cols = pl.ds(pl.multiple_of(which * half + j, LANES), BLOCK)
            part = t_matmul(pixels_ref[...], g_stem_ref[:, cols]).astype(bf16)
            for k in range(0, BLOCK, LANES):
                for d in range(size):
                    out_ref[d, spot : spot + stem_rows, :] = part[
                        d * stem_rows : (d + 1) * stem_rows, k : k + LANES
                    ]
                spot += stem_rows
        half = D // 2
        cols = pl.ds(pl.multiple_of(which * half, LANES), half)
        part = t_matmul(hidden_ref[...], low_ref[:, cols]).astype(bf16)
        for k in range(0, half, LANES):
            for d in range(size):
                out_ref[d, spot : spot + embed_rows, :] = part[
                    d * embed_rows : (d + 1) * embed_rows, k : k + LANES
                ]
            spot += embed_rows
        turned = token_ref[pl.ds(pl.multiple_of(which * LANES, LANES), LANES), :].T.astype(bf16)
        for d in range(size):
            out_ref[d, spot : spot + token_rows, :] = turned[d * token_rows : (d + 1) * token_rows]
            out_ref[d, spot + token_rows :, :] = dec_ref[which, d]


def first_grad(core, pixels, g_stem, hidden, low, pos, sums1, sums2, sumsf, dec, rows, after=()):
    kernel, waits = run_after(first_grad_kernel, 10, after)
    shape = (dec.shape[1], rows, LANES)
    return pl.pallas_call(
        kernel,
        in_specs=[SCALAR] + [FULL] * 9 + waits,
        out_specs=[FULL] * 2,
        out_shape=[jax.ShapeDtypeStruct(shape, bf16)] * 2,
        scratch_shapes=[pltpu.VMEM((2 * LANES, D), f32)],
        compiler_params=params(),
        cost_estimate=cost(2),
        name="first_grad",
    )(core, pixels, g_stem, hidden, low, pos, sums1, sums2, sumsf, dec, *after)


def unpack_kernel(core_ref, own_ref, other_ref, stem_ref, embed_ref, token_ref, turned_ref):
    core = core_ref[0]
    size = own_ref.shape[0]
    stem_rows, embed_rows, token_rows = PIXELS // size, C_STEM // size, D // size
    for which, block_ref in ((core, own_ref), (1 - core, other_ref)):
        spot = 0
        for target_ref, rows, half in (
            (stem_ref, stem_rows, C_STEM // 2),
            (embed_ref, embed_rows, D // 2),
            (turned_ref, token_rows, LANES),
        ):
            for k in range(0, half, LANES):
                cols = pl.ds(pl.multiple_of(which * half + k, LANES), LANES)
                for d in range(size):
                    target_ref[d * rows : (d + 1) * rows, cols] = block_ref[
                        d, spot : spot + rows, :
                    ].astype(target_ref.dtype)
                spot += rows
    token_ref[...] = turned_ref[...].T


def unpack(core, own, other):
    return pl.pallas_call(
        unpack_kernel,
        in_specs=[SCALAR] + [FULL] * 2,
        out_specs=[FULL] * 3,
        out_shape=[
            jax.ShapeDtypeStruct((PIXELS, C_STEM), bf16),
            jax.ShapeDtypeStruct((C_STEM, D), bf16),
            jax.ShapeDtypeStruct((2 * LANES, D), f32),
        ],
        scratch_shapes=[pltpu.VMEM((D, 2 * LANES), f32)],
        compiler_params=params(),
        cost_estimate=cost(3),
        name="unpack",
    )(core, own, other)


def pack_kernel(core_ref, stem_ref, embed_ref, token_ref, dec_ref, out_ref):
    core = core_ref[0]
    spot = 0
    for source_ref in (stem_ref, embed_ref, token_ref):
        rows, half = source_ref.shape[0], source_ref.shape[1] // 2
        for k in range(0, half, LANES):
            cols = pl.ds(pl.multiple_of(core * half + k, LANES), LANES)
            out_ref[spot : spot + rows, :] = source_ref[:, cols].astype(bf16)
            spot += rows
    out_ref[spot:, :] = dec_ref[core].astype(bf16)


def pack(core, stem_w, embed_w, token_t, dec, rows):
    return pl.pallas_call(
        pack_kernel,
        in_specs=[SCALAR] + [FULL] * 4,
        out_specs=FULL,
        out_shape=jax.ShapeDtypeStruct((rows, LANES), bf16),
        compiler_params=params(),
        cost_estimate=cost(2),
        name="pack",
    )(core, stem_w, embed_w, token_t, dec)


def middle_back_kernel(
    low2_ref, mlp_ref, slope_ref, resid_ref, token_ref, g_resid2_ref, own_ref, other_ref,
    g_pre_ref, g_resid_ref, low_ref, g_ctx_ref, sums_ref, g_normed,
):
    p = pl.program_id(0)
    each = mlp_ref.shape[2] // 2
    for cols in gelu_blocks(each):
        down = mlp_ref[0, :, each + cols.start : each + cols.stop]
        grad = matmul(low2_ref[...], down) * slope_ref[0, :, cols].astype(f32)
        g_pre_ref[0, :, cols] = grad.astype(bf16)
    term = matmul_t(g_pre_ref[0], mlp_ref[0, :, :each])

    @pl.when(p == 0)
    def _():
        g_normed[...] = term

    @pl.when(p > 0)
    def _():
        g_normed[...] += term

    @pl.when(p == pl.num_programs(0) - 1)
    def _():
        norm_back_rows(
            resid_ref, token_ref[PATCHES + 2 : PATCHES + 3, :], g_normed, g_resid2_ref,
            g_resid_ref, low_ref, sums_ref,
        )
        part = g_ctx_ref.shape[2]
        for q in range(g_ctx_ref.shape[0]):
            start = (q % 2) * 4 * part + 3 * part
            weight_ref = (own_ref, other_ref)[q // 2]
            g_ctx_ref[q] = matmul(low_ref[...], weight_ref[:, start : start + part]).astype(bf16)


def middle_back(low2, mlp_all, slope, resid, tokens, g_resid2, attn_all, after=()):
    kernel, waits = run_after(middle_back_kernel, 8, after)
    rows = resid.shape[0]
    parts, _, each = slope.shape
    part = attn_all[0].shape[1] // 8
    outs = [
        jax.ShapeDtypeStruct((parts, rows, each), bf16),
        jax.ShapeDtypeStruct((rows, D), f32),
        jax.ShapeDtypeStruct((rows, D), bf16),
        jax.ShapeDtypeStruct((parts, rows, part), bf16),
        jax.ShapeDtypeStruct((16, D), f32),
    ]
    values = (resid, tokens, g_resid2, *attn_all)
    return pl.pallas_call(
        kernel,
        grid=(parts,),
        in_specs=[whole_of(low2), part_of(mlp_all), part_of(slope)]
        + [whole_of(value) for value in values]
        + waits,
        out_specs=[part_of(outs[0])] + [whole_of(out) for out in outs[1:]],
        out_shape=outs,
        scratch_shapes=[pltpu.VMEM((rows, D), f32)],
        compiler_params=params(),
        cost_estimate=cost(11),
        name="middle_back",
    )(low2, mlp_all, slope, *values, *after)


def half_grad_kernel(core_ref, left_ref, right_ref, send_ref, keep_ref):
    core = core_ref[0]
    each = right_ref.shape[2]
    for which, out_ref in ((1 - core, send_ref), (core, keep_ref)):
        for x in range(2):
            out_ref[:, x * each : (x + 1) * each] = t_matmul(
                left_ref[...], right_ref[2 * x + which]
            ).astype(bf16)


def half_grad(core, left, right, after=()):
    kernel, waits = run_after(half_grad_kernel, 3, after)
    shape = (left.shape[1], 2 * right.shape[2])
    return pl.pallas_call(
        kernel,
        in_specs=[SCALAR] + [FULL] * 2 + waits,
        out_specs=[FULL] * 2,
        out_shape=[jax.ShapeDtypeStruct(shape, bf16)] * 2,
        compiler_params=params(),
        cost_estimate=cost(2.7),
        name="half_grad",
    )(core, left, right, *after)


def attn_back_kernel(tri_ref, g_ctx_ref, g_tri_ref):
    slices = tri_ref.shape[1] // PAD
    heads = tri_ref.shape[2] // (3 * HEAD_DIM)
    column = lax.broadcasted_iota(jnp.int32, (PAD, PAD), 1)
    for s in range(slices):
        rows = slice(s * PAD, (s + 1) * PAD)
        for h in range(heads):
            base = h * 3 * HEAD_DIM
            queries = tri_ref[0, rows, base : base + HEAD_DIM]
            keys_low = tri_ref[0, rows, base + HEAD_DIM : base + 2 * HEAD_DIM]
            values = tri_ref[0, rows, base + 2 * HEAD_DIM : base + 3 * HEAD_DIM]
            gctx = g_ctx_ref[0, rows, h * HEAD_DIM : (h + 1) * HEAD_DIM]
            attend = soft_rows(matmul_t(queries, keys_low), column)
            g_attend = matmul_t(gctx, values)
            g_values = t_matmul(attend.astype(bf16), gctx)
            inner = jnp.sum(attend * g_attend, axis=-1, keepdims=True)
            g_scores = attend * (g_attend - inner) * HEAD_DIM ** (-0.5)
            g_low = g_scores.astype(bf16)
            g_tri_ref[0, rows, base : base + HEAD_DIM] = matmul(g_low, keys_low).astype(bf16)
            g_tri_ref[0, rows, base + HEAD_DIM : base + 2 * HEAD_DIM] = t_matmul(
                g_low, queries
            ).astype(bf16)
            g_tri_ref[0, rows, base + 2 * HEAD_DIM : base + 3 * HEAD_DIM] = g_values.astype(bf16)


def attn_back(triple, g_ctx, after=()):
    parts, rows, width = triple.shape
    whole = lambda size: pl.BlockSpec((1, rows, size), lambda i: (i, 0, 0))
    kernel, waits = run_after(attn_back_kernel, 2, after)
    return pl.pallas_call(
        kernel,
        grid=(parts,),
        in_specs=[whole(width), whole(width // 3)] + waits,
        out_specs=whole(width),
        out_shape=jax.ShapeDtypeStruct(triple.shape, bf16),
        compiler_params=params(),
        cost_estimate=cost(13.5),
        name="attn_back",
    )(triple, g_ctx, *after)


def attn_grad_kernel(normed_ref, g_tri_ref, low_ref, ctx_ref, send_ref, keep_ref):
    width = g_tri_ref.shape[2]
    stride = width + width // 3
    for which, out_ref in ((1, send_ref), (0, keep_ref)):
        for x in range(2):
            part = 2 * which + x
            at = x * stride
            out_ref[:, at : at + width] = t_matmul(normed_ref[...], g_tri_ref[part]).astype(
                out_ref.dtype
            )
            out_ref[:, at + width : at + stride] = t_matmul(low_ref[...], ctx_ref[part]).astype(
                out_ref.dtype
            )


def attn_grad(normed, g_tri, low, context, after=()):
    shape = (D, 2 * (g_tri.shape[2] + context.shape[2]))
    kernel, waits = run_after(attn_grad_kernel, 4, after)
    return pl.pallas_call(
        kernel,
        in_specs=[FULL] * 4 + waits,
        out_specs=[FULL] * 2,
        out_shape=[jax.ShapeDtypeStruct(shape, bf16)] * 2,
        compiler_params=params(),
        cost_estimate=cost(3.6),
        name="attn_grad",
    )(normed, g_tri, low, context, *after)


def enter_back_kernel(
    core_ref, g_tri_ref, own_ref, other_ref, embed_ref, token_ref, g_resid_ref, embed_w_ref,
    g_skips_ref, skip_own_ref, skip_other_ref, slope_ref, low_ref, g_stem_ref, g_pos_ref, sums_ref, g_normed, g_embed,
):
    width = g_tri_ref.shape[2]
    stride = width + width // 3
    for p in range(g_tri_ref.shape[0]):
        start = (p % 2) * stride
        weight_ref = (own_ref, other_ref)[p // 2]
        term = matmul_t(g_tri_ref[p], weight_ref[:, start : start + width])
        if p == 0:
            g_normed[...] = term
        else:
            g_normed[...] += term
    norm_back_rows(
        embed_ref, token_ref[PATCHES : PATCHES + 1, :], g_normed, g_resid_ref, g_embed, low_ref, sums_ref
    )
    pos = g_embed[:PAD, :]
    for s in range(1, embed_ref.shape[0] // PAD):
        pos = pos + g_embed[s * PAD : (s + 1) * PAD, :]
    g_pos_ref[...] = pos
    half = skip_own_ref.shape[1]
    core = core_ref[0]
    for cols in gelu_blocks(C_STEM):
        grad = matmul_t(low_ref[...], embed_w_ref[cols, :])
        for which, weight_ref in ((core, skip_own_ref), (1 - core, skip_other_ref)):
            part = pl.ds(pl.multiple_of(which * half, LANES), half)
            grad += matmul_t(g_skips_ref[:, part], weight_ref[cols, :])
        g_stem_ref[:, cols] = (grad * slope_ref[:, cols].astype(f32)).astype(bf16)


def enter_back(core, g_tri, attn_all, embed, tokens, g_resid, embed_b, g_skips, skip_all, slope, after=()):
    rows = embed.shape[0]
    kernel, waits = run_after(enter_back_kernel, 12, after)
    return pl.pallas_call(
        kernel,
        in_specs=[SCALAR] + [FULL] * 11 + waits,
        out_specs=[FULL] * 4,
        out_shape=[
            jax.ShapeDtypeStruct((rows, D), bf16),
            jax.ShapeDtypeStruct((rows, C_STEM), bf16),
            jax.ShapeDtypeStruct((PAD, D), f32),
            jax.ShapeDtypeStruct((16, D), f32),
        ],
        scratch_shapes=[pltpu.VMEM((rows, D), f32), pltpu.VMEM((rows, D), f32)],
        compiler_params=params(),
        cost_estimate=cost(10.4),
        name="enter_back",
    )(core, g_tri, *attn_all, embed, tokens, g_resid, embed_b, g_skips, *skip_all, slope, *after)


def split_decoder(flat):
    edge_one = D * CHAN_A
    edge_two = edge_one + CHAN_A * 4 * CHAN_B
    edge_three = edge_two + CHAN_B * 4 * CHAN_C
    edge_four = edge_three + CHAN_C * 4 * CHAN_D
    return (
        flat[:edge_one].reshape(D, CHAN_A),
        flat[edge_one:edge_two].reshape(CHAN_A, 4 * CHAN_B),
        flat[edge_two:edge_three].reshape(CHAN_B, 4 * CHAN_C),
        flat[edge_three:edge_four].reshape(CHAN_C, 4 * CHAN_D),
        flat[edge_four:].reshape(CHAN_D, 4 * CLASSES),
    )


def same_block(rows, columns, inner, outer):
    return (np.arange(rows) // inner)[:, None] == (np.arange(columns) // outer)[None, :]


def block_diag(weight, parents):
    inner, outer = weight.shape
    mask = same_block(parents * inner, parents * outer, inner, outer)
    tiled = jnp.tile(weight, (parents, parents))
    return tiled * mask.astype(bf16)


def head_masks():
    column = np.arange(CLASSES * GROUP * 4)
    source = np.arange(4 * CLASSES)[:, None]
    pick = source == ((column % 4) * CLASSES + column // (GROUP * 4))[None, :]
    row = np.arange(GROUP * CHAN_D)[:, None]
    mask = row // CHAN_D == ((column // 4) % GROUP)[None, :]
    return pick, mask


def big_head_of(head_b):
    pick, mask = head_masks()
    spread = matmul(head_b, pick.astype(bf16)).astype(bf16)
    tiled = jnp.tile(spread, (GROUP, 1))
    return tiled * mask.astype(bf16)


def stack_columns(value, width):
    count = value.shape[-1] // width
    return jnp.concatenate(
        [value[..., i * width : (i + 1) * width] for i in range(count)], axis=-2
    )


def unstack_columns(value, count):
    rows = value.shape[-2] // count
    return jnp.concatenate(
        [value[..., i * rows : (i + 1) * rows, :] for i in range(count)], axis=-1
    )


def pad_to(value, axis, size):
    widths = [(0, 0)] * value.ndim
    widths[axis] = (0, size - value.shape[axis])
    return jnp.pad(value, widths)


class Shared:
    def __init__(self, stem_w, embed_w, token_params, decoder_w):
        self.stem_rows = stem_w.shape[0]
        self.embed_rows = embed_w.shape[0]
        self.token_rows = token_params.shape[1]
        self.flat = decoder_w.shape[0]
        self.flat_rows = -(-self.flat // (2 * LANES * 16)) * 16
        self.stem_count = C_STEM // 2 // LANES
        self.embed_count = D // 2 // LANES
        self.cuts = [0]
        for rows in (
            self.stem_rows * self.stem_count,
            self.embed_rows * self.embed_count,
            self.token_rows,
            self.flat_rows,
        ):
            self.cuts.append(self.cuts[-1] + rows)

    def half_flat(self, flat):
        padded = pad_to(flat, flat.ndim - 1, 2 * self.flat_rows * LANES)
        return padded.reshape(flat.shape[:-1] + (2, self.flat_rows, LANES))

    def pieces(self, value):
        one, two, three, four = (
            value[..., a:b, :] for a, b in zip(self.cuts[:-1], self.cuts[1:], strict=True)
        )
        return (
            unstack_columns(one, self.stem_count),
            unstack_columns(two, self.embed_count),
            three,
            four,
        )


def half_columns(value, core, axis=-1):
    axis = axis % value.ndim
    size = value.shape[axis] // 2
    return lax.dynamic_slice_in_dim(value, core * size, size, axis)


def adamw(weight, grad, first, second, rate):
    first_new = beta_one * first + (1.0 - beta_one) * grad
    second_new = beta_two * second + (1.0 - beta_two) * grad * grad
    first_hat = first_new / (1.0 - beta_one**STEP)
    second_hat = second_new / (1.0 - beta_two**STEP)
    new_weight = weight - rate * (
        first_hat / (jnp.sqrt(second_hat) + adam_eps) + decay_rate * weight
    )
    return (new_weight, first_new, second_new)


def body(
    images,
    labels,
    background,
    patients,
    *state,
):
    masters, firsts, seconds = state[:9], state[9:18], state[18:]
    stem_w, embed_w, token_params, qkv_w, out_w, mlp_in_w, mlp_out_w, skip_w, decoder_w = masters
    n_dp = lax.axis_size("dp")
    n_mp = lax.axis_size("mp")
    mp_id = lax.axis_index("mp")
    core = mp_id & 1
    slices = images.shape[0] // n_mp
    rows = slices * PAD
    shared = Shared(stem_w, embed_w, token_params, decoder_w)
    attn_cut = qkv_w.shape[1]

    core_id = core.reshape(1)
    token_t = pad_to(token_params.T, 1, 2 * LANES)
    aligned = shared.stem_rows % 16 == 0 and shared.token_rows % 16 == 0
    mlp_block = jnp.concatenate([mlp_in_w, mlp_out_w.T], axis=1).astype(bf16)
    mlp_all = lax.all_gather(mlp_block, ("mp", "dp"), axis=0, tiled=True).reshape(n_mp, D, -1)
    if aligned:
        first_block = pack(
            core_id, stem_w, embed_w, token_t, shared.half_flat(decoder_w), shared.cuts[-1]
        )
    else:
        dec_half = lax.dynamic_index_in_dim(shared.half_flat(decoder_w), core, 0, keepdims=False)
        first_block = jnp.concatenate(
            [
                stack_columns(half_columns(stem_w, core), LANES),
                stack_columns(half_columns(embed_w, core), LANES),
                half_columns(token_t, core),
                dec_half,
            ],
            axis=0,
        ).astype(bf16)
    attn_block = jnp.concatenate([qkv_w, out_w.T], axis=1).astype(bf16)
    skip_block = half_columns(skip_w, core).astype(bf16)

    first, split, skip = Gather(first_block), Gather(attn_block), Gather(skip_block)
    order = list(reversed(range(log_two(n_dp))))
    for bit in order[3:]:
        for part in (first, split, skip):
            part.step("dp", bit)
    top, middle_bit, last = order[:3]
    first.start("dp", top)
    split.start("dp", top)
    token = first.finish()
    first.start("dp", last)
    token = split.finish(after=(token,))
    split.start("dp", middle_bit)
    skip.value = run_gate(skip.value, token)
    skip.start("dp", top)
    token = first.finish(after=(token,))
    first.start("dp", middle_bit)
    token = split.finish(after=(token,))
    split.start("dp", last)
    token = skip.finish(after=(token,))
    skip.start("dp", middle_bit)
    token = split.finish(after=(token,))
    split.start("mp", 1)
    token = first.finish(after=(token,))
    first_own = first.value
    first_pair = [
        value.reshape(n_dp, -1, LANES) for value in (first_own, swap(first_own, "mp", 0))
    ]
    by_core = lambda pair: [
        jnp.where(core == 0, pair[0], pair[1]), jnp.where(core == 0, pair[1], pair[0])
    ]
    dec_parts = by_core([value[:, shared.cuts[3] :] for value in first_pair])
    if aligned:
        stem_b, embed_b, table = unpack(core_id, *first_pair)
    else:
        both = [shared.pieces(value) for value in by_core(first_pair)]
        side = lambda k: jnp.concatenate([both[0][k], both[1][k]], axis=-1)
        stem_b = side(0).reshape(PIXELS, C_STEM)
        embed_b = side(1).reshape(C_STEM, D)
        table = side(2).reshape(D, 2 * LANES).T.astype(f32)
    dec_flat = jnp.stack(dec_parts, axis=1).reshape(n_dp, -1)[:, : shared.flat].reshape(-1)
    dec_b, one_b, two_b, three_b, head_b = split_decoder(dec_flat)
    three_four = block_diag(three_b, 4)
    big_head = big_head_of(head_b)
    token = skip.finish(after=(token, dec_b, one_b, two_b, three_four, big_head, table))
    skip.start("dp", last)
    token = split.finish(after=(token,))
    attn_weights = split.value

    attn_all = (attn_weights, swap(attn_weights, "mp", 0))

    take = lambda value: lax.dynamic_slice_in_dim(value, mp_id * slices, slices, 0)
    pixels = pad_to(take(images), 1, PAD).reshape(rows, PIXELS)
    label_own = jnp.pad(take(labels), ((0, 0), (0, PAD - PATCHES), (0, 0)), constant_values=-1)
    label_own = label_own.reshape(rows, PIXELS)
    keep = (1 - take(background)).astype(f32)
    owner = (take(patients)[:, None] == jnp.arange(PATIENTS, dtype=jnp.int32)).astype(f32)

    hidden, slope_stem, embed, normed, triple, context = enter(
        pixels, stem_b, embed_b, table, attn_all, attn_cut
    )
    resid, normed2, slope_mlp, inner, resid2, final_low = middle(
        context, embed, table, attn_all, mlp_all
    )
    skip_weights = skip.finish(after=(final_low,))
    skip_all = (skip_weights, swap(skip_weights, "mp", 0))
    slope0, level0, slope_skips, level1, level2, level3, logits, stats = leave(
        core_id, hidden, final_low, skip_all, dec_b, one_b, two_b, three_four, big_head, label_own
    )

    sums = jnp.sum(stats.reshape(slices, 3 * CLASSES + 1, 8 * LANES), axis=-1)
    class_sums = sums[:, : 3 * CLASSES]
    pat_sums = jnp.sum(owner[:, :, None] * class_sums[:, None, :], axis=0)
    cross_sum = jnp.sum(keep * sums[:, 3 * CLASSES])
    packed = jnp.concatenate(
        [pat_sums.reshape(-1), cross_sum[None], jnp.sum(keep)[None]]
    )
    packed = pad_to(packed, 0, 8 * LANES).reshape(8, LANES)
    packed = butterfly(packed).reshape(-1)
    pat_all = packed[: PATIENTS * 3 * CLASSES].reshape(PATIENTS, CLASSES, 3)
    ce_total = packed[PATIENTS * 3 * CLASSES]
    pixel_count = packed[PATIENTS * 3 * CLASSES + 1] * (PATCHES * PIXELS)
    pat_over, pat_pred, pat_true = pat_all[..., 0], pat_all[..., 1], pat_all[..., 2]
    denominator = pat_pred + pat_true + dice_eps
    dice = (2.0 * pat_over + dice_eps) / denominator
    count_floor = jnp.maximum(pixel_count, 1.0)
    loss = ce_total / count_floor + 1.0 - jnp.mean(dice)
    cells = PATIENTS * CLASSES
    over_coef = -2.0 / (cells * denominator)
    pred_coef = (2.0 * pat_over + dice_eps) / (cells * denominator * denominator)
    pick_own = lambda table: jnp.sum(owner[:, :, None] * table[None], axis=1)
    coef = jnp.concatenate(
        [pick_own(over_coef), pick_own(pred_coef), (keep / count_floor)[:, None]], axis=1
    )

    def x_sum(value):
        value = lax.reduce_precision(value, 8, 7).astype(bf16)
        return value.astype(f32) + swap(value, "mp", 1).astype(f32)

    def core_pair(send, own):
        return Scatter(own, swap(send, "mp", 0))

    grad_logits, grad_skips = leave_back(
        coef, logits, label_own, slope_skips, big_head, three_four, two_b
    )
    skip_send, skip_keep = skip_grad(core_id, hidden, grad_skips)
    grad_pre0, grad_resid2, grad_resid2_low, sums_f = turn(
        grad_skips, one_b, slope0, dec_b, resid2, table, after=(skip_send,)
    )
    low_bits = list(range(log_two(n_dp)))
    bit_y, bit_one, bit_two = low_bits[:3]
    skip_part = core_pair(skip_send, skip_keep)
    token = skip_part.step("dp", bit_y, bf16, after=(grad_pre0,))
    down_send, down_keep = half_grad(core_id, grad_resid2_low, inner, after=(token,))
    grad_pre, grad_resid, grad_resid_low, grad_context, sums_2 = middle_back(
        grad_resid2_low, mlp_all, slope_mlp, resid, table, grad_resid2, attn_all,
        after=(down_send,),
    )
    down = core_pair(down_send, down_keep)
    token = down.step("dp", bit_y, bf16, after=(grad_pre,))
    in_send, in_keep = half_grad(core_id, normed2, grad_pre, after=(token,))
    grad_triple = attn_back(triple, grad_context, after=(in_send,))
    into = core_pair(in_send, in_keep)
    token = into.step("mp", 1, bf16, after=(grad_triple,))
    token = skip_part.step("dp", bit_one, after=(token,))
    attn_send, attn_keep = attn_grad(
        normed, grad_triple, grad_resid_low, context, after=(token,)
    )
    decoder_halves = decoder_grad(
        level3, grad_logits, level2, level1, grad_skips, level0, final_low, grad_pre0,
        n_dp, shared.flat_rows, after=(attn_send,),
    )
    grad_embed_low, grad_pre_stem, grad_pos, sums_1 = enter_back(
        core_id, grad_triple, attn_all, embed, table, grad_resid, embed_b, grad_skips, skip_all,
        slope_stem, after=(decoder_halves,),
    )
    attn = core_pair(attn_send, attn_keep)
    token = attn.step("mp", 1, bf16, after=(grad_embed_low,))
    token = down.step("dp", bit_one, after=(token,))
    token = skip_part.step("dp", bit_two, after=(token,))
    token = into.step("dp", bit_y, after=(token,))
    if aligned:
        first_send, first_keep = first_grad(
            core_id, pixels, grad_pre_stem, hidden, grad_embed_low, grad_pos, sums_1, sums_2,
            sums_f, decoder_halves, shared.cuts[-1], after=(token,),
        )
    else:
        gains = jnp.concatenate([sums_1, sums_2, sums_f], axis=0).reshape(6, 8, D).sum(axis=1)
        grad_token = pad_to(jnp.concatenate([grad_pos[:PATCHES], gains], axis=0).T, 1, 2 * LANES)

        def first_half(which):
            blocks = lambda value: value.reshape(n_dp, -1, value.shape[-1])
            stem_part = t_matmul(pixels, half_columns(grad_pre_stem, which))
            embed_part = t_matmul(hidden, half_columns(grad_embed_low, which))
            return jnp.concatenate(
                [
                    stack_columns(blocks(stem_part), LANES),
                    stack_columns(blocks(embed_part), LANES),
                    blocks(half_columns(grad_token, which)),
                    lax.dynamic_index_in_dim(decoder_halves, which, 0, keepdims=False).astype(f32),
                ],
                axis=1,
            ).astype(bf16)

        first_send, first_keep = first_half(1 - core), first_half(core)
    wide = lambda value: value.reshape(-1, LANES)
    first = core_pair(wide(first_send), wide(first_keep))
    token = first_send
    token = first.step("dp", bit_y, after=(token,))
    token = down.step("dp", bit_two, after=(token,))
    token = into.step("dp", bit_one, after=(token,))
    for bit in low_bits[3:]:
        skip_part.step("dp", bit)
    skip_half = run_gate(skip_part.total(), token)
    skip_half = x_sum(skip_half)
    token = attn.step("dp", bit_y, after=(token,))
    token = into.step("dp", bit_two, after=(token,))
    token = down.step("mp", 1, after=(token,))
    token = first.step("dp", bit_one, after=(token,))
    token = attn.step("dp", bit_one, after=(token,))
    token = first.step("dp", bit_two, after=(token,))
    token = attn.step("dp", bit_two, after=(token,))
    for bit in low_bits[3:]:
        for part in (down, into, first, attn):
            part.step("dp", bit)
    down_own, in_own, attn_own = down.total(), into.total(), attn.total()
    first_half_sum = x_sum(first.total())

    square = lambda value: jnp.sum(value * value)
    n_copies = n_mp // 2
    local = (
        square(down_own)
        + square(in_own)
        + square(attn_own)
        + (square(skip_half) + square(first_half_sum)) / n_copies
    )
    total = butterfly(jnp.broadcast_to(local, (8, LANES)))[0, 0]
    grad_norm = jnp.sqrt(total)
    factor = jnp.minimum(1.0, clip_limit / (grad_norm + 1e-06))

    red_skip = jnp.concatenate(by_core([skip_half, swap(skip_half, "mp", 0)]), axis=1)
    own = [shared.pieces(part) for part in by_core([first_half_sum, swap(first_half_sum, "mp", 0)])]
    red_stem = jnp.concatenate([own[0][0], own[1][0]], axis=-1)
    red_embed = jnp.concatenate([own[0][1], own[1][1]], axis=-1)
    red_token = jnp.concatenate([own[0][2], own[1][2]], axis=-1)[:, : PATCHES + 6].T
    red_decoder = jnp.concatenate([own[0][3], own[1][3]], axis=0).reshape(-1)[: shared.flat]
    red_qkv = attn_own[:, :attn_cut]
    red_out = attn_own[:, attn_cut:].T
    red_in = in_own
    red_down = down_own.T
    reduced = (
        red_stem, red_embed, red_token, red_qkv, red_out, red_in, red_down, red_skip, red_decoder,
    )
    rates = [learn_rate] * 9
    rates[2] = token_rate
    results = [
        adamw(weight, grad * factor, first, second, rate)
        for weight, grad, first, second, rate in zip(
            masters, reduced, firsts, seconds, rates, strict=True
        )
    ]
    news = [item[0] for item in results]
    moms = [item[1] for item in results]
    secs = [item[2] for item in results]
    return (loss, pixel_count, grad_norm, *news, *moms, *secs)


def solution(mesh):
    weights = (
        P("dp", None),
        P("dp", None),
        P(None, "dp"),
        P("dp", "mp"),
        P("mp", "dp"),
        P("dp", "mp"),
        P("mp", "dp"),
        P("dp", None),
        P("dp"),
    )
    placed = (P("dp", None, None), P("dp", None, None), P("dp"), P("dp")) + weights * 3
    outs = (P(), P(), P()) + weights * 3
    return jax.shard_map(body, mesh=mesh, in_specs=placed, out_specs=outs, check_vma=False)
```
